32 devices in a mesh: groups: 2 (over x), clus: 16 (over z, y, core).
Axes of the slice: x: 2, y: 2, z: 4, core: 2. Of those that a mesh axis runs over, the one named last changes fastest.
Arguments:
- pool_emb: float32 [16384, 768], P(('groups', 'clus')), parts along dimension 0, may hold values from -6 to 6
- target_emb: float32 [4096, 768], P(('groups', 'clus')), parts along dimension 0, may hold values from -6 to 6
- pool_mass: float32 [16384], P(('groups', 'clus')), parts along dimension 0, may hold values from 0.25 to 4
- target_mass: float32 [4096], P(('groups', 'clus')), parts along dimension 0, may hold values from 0.25 to 4
- fetch_table: int32 [32, 16], P(('groups', 'clus')), parts along dimension 0, may hold values from -1 to 7, as said below
- pair_pool: int32 [32, 128], P(('groups', 'clus')), parts along dimension 0, may hold values from 0 to 7, as said below
- listed_pair_slot: int32 [32, 128], P(('groups', 'clus')), parts along dimension 0, may hold values from 0 to 15, as said below
- pair_count: int32 [32], P(('groups', 'clus')), parts along dimension 0, may hold values from 1 to 128, as said below
Outputs:
- log_pool_scaling: float32 [16384], P(('groups', 'clus')), parts along dimension 0
- log_target_scaling: float32 [4096], P(('groups', 'clus')), parts along dimension 0
The draws below stay inside these ranges and needn't reach their ends.
There are 2 independent parts, one for each index of `groups`. The reference program is written for one: setup_inputs(seed, part) draws one part's arguments, and reference() takes and returns one part's arrays. A program takes and returns all parts, laid end to end along the dimension named above; each array names one. Nothing has to cross between parts.
Inputs may be any that keep to these rules, and one draw needn't show every extreme that they name: `fetch_table`: every target block is named by some slot. Some clus index in every draw names a block in all 16 of its slots. `pair_pool`: the first pair_count[d] entries of index d are distinct pairs; every pool block of d and every slot of d that names a block appears in one of them; they name only such slots. `listed_pair_slot`: see pair_pool. `pair_count`: some clus index lists 128 pairs in every draw.
All inputs are finite; a program needn't handle non-finite values.
Results may differ from the reference program's by a relative error of at most 0.0003.
Values sent between devices are 32-bit elements; how exact they have to be, the bound alone decides.
No kernel may reach another device: no remote copies, remote signals or barrier semaphores. Data moves between devices by JAX's collectives and lax.ppermute only.
A program may use at most 128 MiB of HBM per device.

```python
import math
import jax
import jax.numpy as jnp
from jax import lax

D = 768
RB = 64
CB = 16
ITERS = 3
BP = 8
BQ = 8
MAXP = 128
POOL = 8192
TGT = 2048
N_CLUS = 16


def layout(key):
    count_dev = N_CLUS
    keys = jax.random.split(key, 6)
    stride = count_dev // BQ
    offset = jax.random.randint(keys[0], (), 0, count_dev)
    rows = jnp.arange(count_dev)[:, None]
    cols = jnp.arange(count_dev)[None, :]
    delta = (rows - cols - offset) % count_dev
    forced = (delta % stride == 0) & (delta // stride < BQ)
    rolled = jax.random.randint(keys[1], (count_dev, count_dev), 0, 2 * BQ)
    busiest = jax.random.randint(keys[2], (), 0, count_dev)
    table = jnp.where(forced, delta // stride, jnp.where(rolled < BQ, rolled, -1))
    table = jnp.where((rows == busiest) & (table < 0), rolled % BQ, table)
    density = jax.random.randint(keys[3], (count_dev,), 1, 5)
    drawn = jax.random.randint(keys[4], (count_dev, count_dev, BP), 0, 4) < density[:, None, None]
    anchor = jax.random.randint(keys[5], (count_dev, count_dev), 0, BP)
    picked = drawn | forced[:, :, None] | (jnp.arange(BP)[None, None, :] == anchor[:, :, None]) | (rows == busiest)[:, :, None]
    chosen = ((table >= 0)[:, :, None] & picked).reshape(count_dev, count_dev * BP).astype(jnp.int32)
    order = jnp.argsort(1 - chosen, axis=1, stable=True).astype(jnp.int32)
    total = jnp.sum(chosen, axis=1).astype(jnp.int32)
    live = jnp.arange(count_dev * BP)[None, :] < total[:, None]
    order = jnp.where(live, order, order[:, :1])
    return (table.astype(jnp.int32), (order % BP).astype(jnp.int32), (order // BP).astype(jnp.int32), total)


def draw_fetch_table(key, part):
    return layout(key)[0]


def draw_pair_pool(key, part):
    return layout(key)[1]


def draw_listed_pair_slot(key, part):
    return layout(key)[2]


def draw_pair_count(key, part):
    return layout(key)[3]


def block_levels(stream_key, dims, shards, least, largest):
    def one(position, blocks):
        heights = jax.random.uniform(jax.random.fold_in(jax.random.fold_in(stream_key, 6), position), (blocks,), jnp.float32, least / len(shards), largest / len(shards))
        return jnp.repeat(jnp.exp(heights), dims[position] // blocks).reshape((-1,) + (1,) * (len(dims) - position - 1))

    gain = one(*shards[0])
    for cut in shards[1:]:
        gain = gain * one(*cut)
    return gain


def scatter_about(rng, extent, spread, reach, pieces=(), kind=jnp.bfloat16):
    values = spread * jax.random.normal(rng, extent, jnp.float32)
    if pieces:
        values = values * block_levels(rng, extent, pieces, -0.22, 0.18)
    return jnp.clip(values, -reach, reach).astype(kind)


def setup_inputs(seed: int = 0, part: int = 0) -> dict:
    key_of = jax.random.split(jax.random.key(seed), 9)
    part_keys = jax.random.split(jax.random.fold_in(key_of[8], part), 9)
    pool_emb = scatter_about(part_keys[0], (POOL, D), 1.0, 6.0, ((0, 16),), jnp.float32)
    target_emb = scatter_about(part_keys[1], (TGT, D), 1.0, 6.0, ((0, 16),), jnp.float32)
    pool_mass = jnp.clip(jnp.exp(math.log(4.0) - 2.7725887 * jax.random.uniform(part_keys[2], (POOL,), jnp.float32) ** block_levels(part_keys[2], (POOL,), ((0, 16),), -0.2, 0.2)), 0.25, 4.0)
    target_mass = jnp.clip(jnp.exp(math.log(4.0) - 2.7725887 * jax.random.uniform(part_keys[3], (TGT,), jnp.float32) ** block_levels(part_keys[3], (TGT,), ((0, 16),), -0.2, 0.2)), 0.25, 4.0)
    fetch_table = draw_fetch_table(jax.random.fold_in(jax.random.fold_in(key_of[8], part), 71), part)
    pair_pool = draw_pair_pool(jax.random.fold_in(jax.random.fold_in(key_of[8], part), 71), part)
    listed_pair_slot = draw_listed_pair_slot(jax.random.fold_in(jax.random.fold_in(key_of[8], part), 71), part)
    pair_count = draw_pair_count(jax.random.fold_in(jax.random.fold_in(key_of[8], part), 71), part)
    return dict(pool_emb=pool_emb, target_emb=target_emb, pool_mass=pool_mass, target_mass=target_mass, fetch_table=fetch_table, pair_pool=pair_pool, listed_pair_slot=listed_pair_slot, pair_count=pair_count)


def reference(pool_emb, target_emb, pool_mass, target_mass, fetch_table, pair_pool, listed_pair_slot, pair_count):
    width = pool_emb.shape[1]
    scale = 1.5 / math.sqrt(width)
    pool_blocks = pool_emb.reshape(N_CLUS, BP, RB, width)
    target_blocks = target_emb.reshape(N_CLUS * BQ, CB, width)
    owners = jnp.arange(N_CLUS).astype(jnp.int32)

    def one_device(index):
        named = (owners * BQ + jnp.maximum(fetch_table[index], 0)).astype(jnp.int32)
        tblock = named[listed_pair_slot[index]].astype(jnp.int32)
        prow = pool_blocks[index][pair_pool[index]]
        trow = target_blocks[tblock]
        scores = jnp.einsum('prd,pcd->prc', prow, trow, precision=lax.Precision.HIGHEST)
        valid = (jnp.arange(MAXP) < pair_count[index]).astype(jnp.float32)
        return (jnp.exp(scores * scale) * valid[:, None, None], tblock)
    kernel, tblock = lax.map(one_device, owners)
    global_pool = (owners[:, None] * BP + pair_pool).astype(jnp.int32)
    target_scaling = jnp.ones((N_CLUS * BQ, CB), jnp.float32)
    pool_scaling = jnp.ones((N_CLUS * BP, RB), jnp.float32)
    for step in range(ITERS):
        terms = jnp.einsum('dprc,dpc->dpr', kernel, target_scaling[tblock], precision=lax.Precision.HIGHEST)
        row_sums = jnp.zeros((N_CLUS * BP, RB), jnp.float32).at[global_pool.reshape(-1)].add(terms.reshape(-1, RB))
        pool_scaling = pool_mass.reshape(N_CLUS * BP, RB) / row_sums
        cols = jnp.einsum('dprc,dpr->dpc', kernel, pool_scaling[global_pool], precision=lax.Precision.HIGHEST)
        col_sums = jnp.zeros((N_CLUS * BQ, CB), jnp.float32).at[tblock.reshape(-1)].add(cols.reshape(-1, CB))
        target_scaling = target_mass.reshape(N_CLUS * BQ, CB) / col_sums
    return (jnp.log(pool_scaling).reshape(-1), jnp.log(target_scaling).reshape(-1))
```

```python
import functools
import math

import jax
import jax.numpy as jnp
from jax import lax
from jax.experimental import pallas as pl
from jax.experimental.pallas import tpu as pltpu
from jax.sharding import PartitionSpec as P

RB = 64
CB = 16
ITERS = 3
LANES = 128
VMEM_LIMIT = 48 * 1024 * 1024

F32 = jnp.float32
BF16 = jnp.bfloat16


def whole(space=pltpu.VMEM):
    return pl.BlockSpec(memory_space=space)


def exchange(row):
    peers = lax.axis_size("clus")
    return lax.all_to_all(
        jnp.broadcast_to(row[None], (peers,) + row.shape),
        "clus",
        split_axis=0,
        concat_axis=0,
        tiled=True,
    )


def exchange_copies(rows):
    return lax.all_to_all(rows, "clus", split_axis=0, concat_axis=0, tiled=True)


def pick_kernel(column, me_ref, notes_ref, emb_ref, out_ref, sems):
    peers = out_ref.shape[0]

    def copy(d):
        block = jnp.maximum(notes_ref[d, 0, column + me_ref[0]].astype(jnp.int32), 0)
        return pltpu.make_async_copy(emb_ref.at[block], out_ref.at[d], sems.at[d])

    @pl.loop(0, peers)
    def _(d):
        copy(d).start()

    @pl.loop(0, peers)
    def _(d):
        copy(d).wait()


def pick_blocks(me, notes, column, blocks):
    peers = notes.shape[0]
    return pl.pallas_call(
        functools.partial(pick_kernel, column),
        out_shape=jax.ShapeDtypeStruct((peers,) + blocks.shape[1:], F32),
        in_specs=[whole(pltpu.SMEM), whole(pltpu.SMEM), whole(pl.ANY)],
        out_specs=whole(pl.ANY),
        scratch_shapes=[pltpu.SemaphoreType.DMA((peers,))],
        name="pick_blocks",
    )(me, notes, blocks)


def split_kernel(x_ref, high_ref, low_ref):
    x = x_ref[...]
    high = x.astype(BF16)
    high_ref[...] = high
    low_ref[...] = (x - high.astype(F32)).astype(BF16)


def split(x):
    return pl.pallas_call(
        split_kernel,
        out_shape=(jax.ShapeDtypeStruct(x.shape, BF16),) * 2,
        in_specs=[whole()],
        out_specs=(whole(), whole()),
        name="split_pool",
        cost_estimate=pl.CostEstimate(
            flops=3 * x.size, bytes_accessed=8 * x.size, transcendentals=0
        ),
        compiler_params=pltpu.CompilerParams(vmem_limit_bytes=VMEM_LIMIT),
    )(x)


def send_out(row, out_ref):
    out_ref[...] = jnp.broadcast_to(row[None], out_ref.shape)


def assemble_kernel(
    scale, high_ref, low_ref, arrived_ref, listed_ref, mass_ref, kernel_ref, out_ref
):
    q = arrived_ref[...]
    q_high = q.astype(BF16)
    q_low = (q - q_high.astype(F32)).astype(BF16)

    def product(a, b):
        return lax.dot_general(a, b, (((1,), (1,)), ((), ())), preferred_element_type=F32)

    sums = jnp.zeros((1, kernel_ref.shape[1]), F32)
    rows = 256 if kernel_ref.shape[0] % 256 == 0 else RB
    for start in range(0, kernel_ref.shape[0], rows):
        part = pl.ds(start, rows)
        high = high_ref[part, :]
        scores = product(high, q_high) + (product(high, q_low) + product(low_ref[part, :], q_high))
        for block in range(rows // RB):
            inner = pl.ds(start + block * RB, RB)
            at = start // RB + block
            listed = listed_ref[at : at + 1, :] > 0
            values = jnp.where(
                listed, jnp.exp(scores[block * RB : (block + 1) * RB] * scale), 0.0
            )
            kernel_ref[inner, :] = values
            scaling = mass_ref[inner, :] / jnp.sum(values, axis=1, keepdims=True)
            sums += jnp.sum(values * scaling, axis=0, keepdims=True)
    send_out(sums, out_ref)


def assemble(high, low, arrived, listed, mass, peers):
    rows, width = high.shape
    columns = arrived.shape[0]
    return pl.pallas_call(
        functools.partial(assemble_kernel, 1.5 / math.sqrt(width)),
        out_shape=(
            jax.ShapeDtypeStruct((rows, columns), F32),
            jax.ShapeDtypeStruct((peers, 1, columns), F32),
        ),
        in_specs=[whole()] * 5,
        out_specs=(whole(), whole()),
        name="assemble",
        cost_estimate=pl.CostEstimate(
            flops=6 * rows * columns * width,
            bytes_accessed=4 * rows * width + 4 * columns * width + 4 * rows * columns,
            transcendentals=rows * columns,
        ),
        compiler_params=pltpu.CompilerParams(vmem_limit_bytes=VMEM_LIMIT),
    )(high, low, arrived, listed, mass)


def iterate_kernel(
    kernel_ref, notes_ref, same_ref, slot_mass_ref, spare_ref, mass_ref, out_ref, log_ref=None
):
    col_sums = jnp.sum(notes_ref[...] * same_ref[...], axis=0)
    target_scaling = slot_mass_ref[...] / (col_sums + spare_ref[...])
    sums = jnp.zeros_like(target_scaling)
    for start in range(0, kernel_ref.shape[0], RB):
        inner = pl.ds(start, RB)
        values = kernel_ref[inner, :]
        scaling = mass_ref[inner, :] / jnp.sum(values * target_scaling, axis=1, keepdims=True)
        sums += jnp.sum(values * scaling, axis=0, keepdims=True)
        if log_ref is not None:
            log_ref[inner, :] = jnp.log(scaling)
    send_out(sums, out_ref)


def iterate(kernel, notes, same, slot_mass, spare, mass, last):
    rows, columns = kernel.shape
    out_shape = [jax.ShapeDtypeStruct(notes.shape, F32)]
    if last:
        out_shape.append(jax.ShapeDtypeStruct((rows, 1), F32))
    return pl.pallas_call(
        iterate_kernel,
        out_shape=out_shape,
        in_specs=[whole()] * 6,
        out_specs=[whole()] * len(out_shape),
        name="iterate",
        cost_estimate=pl.CostEstimate(
            flops=4 * rows * columns, bytes_accessed=4 * rows * columns, transcendentals=0
        ),
        compiler_params=pltpu.CompilerParams(vmem_limit_bytes=VMEM_LIMIT),
    )(kernel, notes, same, slot_mass, spare, mass)


def finish_kernel(notes_ref, own_ref, mass_ref, out_ref):
    total = jnp.sum(notes_ref[...] * own_ref[...], axis=0)
    folded = total[:, :LANES]
    for start in range(LANES, total.shape[1], LANES):
        folded += total[:, start : start + LANES]
    step = LANES // 2
    while step >= CB:
        folded += pltpu.roll(folded, step, 1)
        step //= 2
    blocks = folded.shape[0]
    lane = lax.broadcasted_iota(jnp.int32, (blocks, LANES), 1)
    block = lax.broadcasted_iota(jnp.int32, (blocks, LANES), 0)
    col_sums = jnp.sum(jnp.where(lane // CB == block, folded, 0.0), axis=0, keepdims=True)
    out_ref[...] = jnp.log(mass_ref[...] / col_sums)


def finish(notes, own, mass):
    return pl.pallas_call(
        finish_kernel,
        out_shape=jax.ShapeDtypeStruct(mass.shape, F32),
        in_specs=[whole()] * 3,
        out_specs=whole(),
        name="finish",
        compiler_params=pltpu.CompilerParams(vmem_limit_bytes=VMEM_LIMIT),
    )(notes, own, mass)


def local(
    pool_emb,
    target_emb,
    pool_mass,
    target_mass,
    fetch_table,
    pair_pool,
    listed_pair_slot,
    pair_count,
):
    peers = lax.axis_size("clus")
    me = lax.axis_index("clus")
    width = pool_emb.shape[1]
    pool_count = pool_emb.shape[0] // RB
    targets = target_emb.shape[0]
    target_count = targets // CB
    columns = peers * CB

    table_width = -(-peers // LANES) * LANES
    note = jnp.concatenate(
        [
            target_mass[None],
            jnp.pad(fetch_table.astype(F32), ((0, 0), (0, table_width - peers))),
        ],
        axis=1,
    )
    notes = exchange(note)
    outgoing = pick_blocks(
        me.astype(jnp.int32)[None], notes, targets, target_emb.reshape(target_count, CB, width)
    )
    arrived = exchange_copies(outgoing).reshape(columns, width)

    table = fetch_table[0]
    tables = notes[:, 0, targets : targets + peers].astype(jnp.int32)
    masses = notes[:, 0, :targets].reshape(peers, target_count, CB)
    valid = table >= 0
    chosen = table[:, None] == jnp.arange(target_count)[None, :]
    slot_mass = jnp.sum(jnp.where(chosen[:, :, None], masses, 0.0), axis=1).reshape(1, columns)
    spare = jnp.repeat(jnp.where(valid, 0.0, 1.0), CB).reshape(1, columns)
    same = jnp.repeat((tables == table[None, :]).astype(F32), CB, axis=1)[:, None, :]
    asked = lax.dynamic_index_in_dim(tables, me, 1, keepdims=False)
    own = (
        (asked[:, None, None] == jnp.arange(target_count)[None, :, None])
        & ((jnp.arange(columns) // CB == me)[None, None, :])
    ).astype(F32)
    live = jnp.arange(pair_pool.shape[1]) < pair_count[0]
    pool_hot = (pair_pool[0][None, :] == jnp.arange(pool_count)[:, None]).astype(BF16)
    slot_hot = (
        (listed_pair_slot[0][:, None] == (jnp.arange(columns) // CB)[None, :]) & live[:, None]
    ).astype(BF16)
    listed = jnp.dot(pool_hot, slot_hot, preferred_element_type=F32)
    mass = pool_mass[:, None]

    high, low = split(pool_emb)
    kernel, sums = assemble(high, low, arrived, listed, mass, peers)
    for step in range(1, ITERS):
        sums = exchange_copies(sums)
        sums, *logs = iterate(kernel, sums, same, slot_mass, spare, mass, step == ITERS - 1)
    log_target = finish(exchange_copies(sums), own, target_mass[None])
    return (logs[0].reshape(-1), log_target.reshape(-1))


def solution(mesh):
    return jax.shard_map(
        local,
        mesh=mesh,
        in_specs=(
            P(("groups", "clus"), None),
            P(("groups", "clus"), None),
            P(("groups", "clus")),
            P(("groups", "clus")),
            P(("groups", "clus"), None),
            P(("groups", "clus"), None),
            P(("groups", "clus"), None),
            P(("groups", "clus")),
        ),
        out_specs=(P(("groups", "clus")), P(("groups", "clus"))),
        check_vma=False,
    )
```

```python
import functools
import math

import jax
import jax.numpy as jnp
from jax import lax
from jax.experimental import pallas as pl
from jax.experimental.pallas import tpu as pltpu
from jax.sharding import PartitionSpec as P

RB = 64
CB = 16
ITERS = 3
LANES = 128
VMEM_LIMIT = 48 * 1024 * 1024

F32 = jnp.float32
BF16 = jnp.bfloat16


def whole(space=pltpu.VMEM):
    return pl.BlockSpec(memory_space=space)


def exchange(row):
    peers = lax.axis_size("clus")
    return lax.all_to_all(
        jnp.broadcast_to(row[None], (peers,) + row.shape),
        "clus",
        split_axis=0,
        concat_axis=0,
        tiled=True,
    )


def exchange_copies(rows):
    return lax.all_to_all(rows, "clus", split_axis=0, concat_axis=0, tiled=True)


def pick_kernel(column, me_ref, notes_ref, emb_ref, out_ref, sems):
    peers = out_ref.shape[0]

    def copy(d):
        block = jnp.maximum(notes_ref[d, 0, column + me_ref[0]].astype(jnp.int32), 0)
        return pltpu.make_async_copy(emb_ref.at[block], out_ref.at[d], sems.at[d])

    @pl.loop(0, peers)
    def _(d):
        copy(d).start()

    @pl.loop(0, peers)
    def _(d):
        copy(d).wait()


def pick_blocks(me, notes, column, blocks):
    peers = notes.shape[0]
    return pl.pallas_call(
        functools.partial(pick_kernel, column),
        out_shape=jax.ShapeDtypeStruct((peers,) + blocks.shape[1:], F32),
        in_specs=[whole(pltpu.SMEM), whole(pltpu.SMEM), whole()],
        out_specs=whole(pl.ANY),
        scratch_shapes=[pltpu.SemaphoreType.DMA((peers,))],
        name="pick_blocks",
    )(me, notes, blocks)


def split_kernel(x_ref, high_ref, low_ref):
    x = x_ref[...]
    high = x.astype(BF16)
    high_ref[...] = high
    low_ref[...] = (x - high.astype(F32)).astype(BF16)


def split(x):
    return pl.pallas_call(
        split_kernel,
        out_shape=(jax.ShapeDtypeStruct(x.shape, BF16),) * 2,
        in_specs=[whole()],
        out_specs=(whole(), whole()),
        name="split_pool",
        cost_estimate=pl.CostEstimate(
            flops=3 * x.size, bytes_accessed=8 * x.size, transcendentals=0
        ),
        compiler_params=pltpu.CompilerParams(vmem_limit_bytes=VMEM_LIMIT),
    )(x)


def send_out(row, out_ref):
    out_ref[...] = jnp.broadcast_to(row[None], out_ref.shape)


def assemble_kernel(
    scale, high_ref, low_ref, arrived_ref, listed_ref, mass_ref, kernel_ref, out_ref
):
    q = arrived_ref[...]
    q_high = q.astype(BF16)
    q_low = (q - q_high.astype(F32)).astype(BF16)

    def product(a, b):
        return lax.dot_general(a, b, (((1,), (1,)), ((), ())), preferred_element_type=F32)

    sums = jnp.zeros((1, kernel_ref.shape[1]), F32)
    rows = 256 if kernel_ref.shape[0] % 256 == 0 else RB
    for start in range(0, kernel_ref.shape[0], rows):
        part = pl.ds(start, rows)
        high = high_ref[part, :]
        scores = product(high, q_high) + (product(high, q_low) + product(low_ref[part, :], q_high))
        for block in range(rows // RB):
            inner = pl.ds(start + block * RB, RB)
            at = start // RB + block
            listed = listed_ref[at : at + 1, :] > 0
            values = jnp.where(
                listed, jnp.exp(scores[block * RB : (block + 1) * RB] * scale), 0.0
            )
            kernel_ref[inner, :] = values
            scaling = mass_ref[inner, :] / jnp.sum(values, axis=1, keepdims=True)
            sums += jnp.sum(values * scaling, axis=0, keepdims=True)
    send_out(sums, out_ref)


def assemble(high, low, arrived, listed, mass, peers):
    rows, width = high.shape
    columns = arrived.shape[0]
    return pl.pallas_call(
        functools.partial(assemble_kernel, 1.5 / math.sqrt(width)),
        out_shape=(
            jax.ShapeDtypeStruct((rows, columns), F32),
            jax.ShapeDtypeStruct((peers, 1, columns), F32),
        ),
        in_specs=[whole()] * 5,
        out_specs=(whole(), whole()),
        name="assemble",
        cost_estimate=pl.CostEstimate(
            flops=6 * rows * columns * width,
            bytes_accessed=4 * rows * width + 4 * columns * width + 4 * rows * columns,
            transcendentals=rows * columns,
        ),
        compiler_params=pltpu.CompilerParams(vmem_limit_bytes=VMEM_LIMIT),
    )(high, low, arrived, listed, mass)


def iterate_kernel(
    kernel_ref, notes_ref, same_ref, slot_mass_ref, spare_ref, mass_ref, out_ref, log_ref=None
):
    col_sums = jnp.sum(notes_ref[...] * same_ref[...], axis=0)
    target_scaling = slot_mass_ref[...] / (col_sums + spare_ref[...])
    sums = jnp.zeros_like(target_scaling)
    for start in range(0, kernel_ref.shape[0], RB):
        inner = pl.ds(start, RB)
        values = kernel_ref[inner, :]
        scaling = mass_ref[inner, :] / jnp.sum(values * target_scaling, axis=1, keepdims=True)
        sums += jnp.sum(values * scaling, axis=0, keepdims=True)
        if log_ref is not None:
            log_ref[inner, :] = jnp.log(scaling)
    send_out(sums, out_ref)


def iterate(kernel, notes, same, slot_mass, spare, mass, last):
    rows, columns = kernel.shape
    out_shape = [jax.ShapeDtypeStruct(notes.shape, F32)]
    if last:
        out_shape.append(jax.ShapeDtypeStruct((rows, 1), F32))
    return pl.pallas_call(
        iterate_kernel,
        out_shape=out_shape,
        in_specs=[whole()] * 6,
        out_specs=[whole()] * len(out_shape),
        name="iterate",
        cost_estimate=pl.CostEstimate(
            flops=4 * rows * columns, bytes_accessed=4 * rows * columns, transcendentals=0
        ),
        compiler_params=pltpu.CompilerParams(vmem_limit_bytes=VMEM_LIMIT),
    )(kernel, notes, same, slot_mass, spare, mass)


def finish_kernel(notes_ref, own_ref, mass_ref, out_ref):
    total = jnp.sum(notes_ref[...] * own_ref[...], axis=0)
    folded = total[:, :LANES]
    for start in range(LANES, total.shape[1], LANES):
        folded += total[:, start : start + LANES]
    step = LANES // 2
    while step >= CB:
        folded += pltpu.roll(folded, step, 1)
        step //= 2
    blocks = folded.shape[0]
    lane = lax.broadcasted_iota(jnp.int32, (blocks, LANES), 1)
    block = lax.broadcasted_iota(jnp.int32, (blocks, LANES), 0)
    col_sums = jnp.sum(jnp.where(lane // CB == block, folded, 0.0), axis=0, keepdims=True)
    out_ref[...] = jnp.log(mass_ref[...] / col_sums)


def finish(notes, own, mass):
    return pl.pallas_call(
        finish_kernel,
        out_shape=jax.ShapeDtypeStruct(mass.shape, F32),
        in_specs=[whole()] * 3,
        out_specs=whole(),
        name="finish",
        compiler_params=pltpu.CompilerParams(vmem_limit_bytes=VMEM_LIMIT),
    )(notes, own, mass)


def local(
    pool_emb,
    target_emb,
    pool_mass,
    target_mass,
    fetch_table,
    pair_pool,
    listed_pair_slot,
    pair_count,
):
    peers = lax.axis_size("clus")
    me = lax.axis_index("clus")
    width = pool_emb.shape[1]
    pool_count = pool_emb.shape[0] // RB
    targets = target_emb.shape[0]
    target_count = targets // CB
    columns = peers * CB

    table_width = -(-peers // LANES) * LANES
    note = jnp.concatenate(
        [
            target_mass[None],
            jnp.pad(fetch_table.astype(F32), ((0, 0), (0, table_width - peers))),
        ],
        axis=1,
    )
    notes = exchange(note)
    outgoing = pick_blocks(
        me.astype(jnp.int32)[None], notes, targets, target_emb.reshape(target_count, CB, width)
    )
    arrived = exchange_copies(outgoing).reshape(columns, width)

    table = fetch_table[0]
    tables = notes[:, 0, targets : targets + peers].astype(jnp.int32)
    masses = notes[:, 0, :targets].reshape(peers, target_count, CB)
    valid = table >= 0
    chosen = table[:, None] == jnp.arange(target_count)[None, :]
    slot_mass = jnp.sum(jnp.where(chosen[:, :, None], masses, 0.0), axis=1).reshape(1, columns)
    spare = jnp.repeat(jnp.where(valid, 0.0, 1.0), CB).reshape(1, columns)
    same = jnp.repeat((tables == table[None, :]).astype(F32), CB, axis=1)[:, None, :]
    asked = lax.dynamic_index_in_dim(tables, me, 1, keepdims=False)
    own = (
        (asked[:, None, None] == jnp.arange(target_count)[None, :, None])
        & ((jnp.arange(columns) // CB == me)[None, None, :])
    ).astype(F32)
    live = jnp.arange(pair_pool.shape[1]) < pair_count[0]
    pool_hot = (pair_pool[0][None, :] == jnp.arange(pool_count)[:, None]).astype(BF16)
    slot_hot = (
        (listed_pair_slot[0][:, None] == (jnp.arange(columns) // CB)[None, :]) & live[:, None]
    ).astype(BF16)
    listed = jnp.dot(pool_hot, slot_hot, preferred_element_type=F32)
    mass = pool_mass[:, None]

    high, low = split(pool_emb)
    kernel, sums = assemble(high, low, arrived, listed, mass, peers)
    for step in range(1, ITERS):
        sums = exchange_copies(sums)
        sums, *logs = iterate(kernel, sums, same, slot_mass, spare, mass, step == ITERS - 1)
    log_target = finish(exchange_copies(sums), own, target_mass[None])
    return (logs[0].reshape(-1), log_target.reshape(-1))


def solution(mesh):
    return jax.shard_map(
        local,
        mesh=mesh,
        in_specs=(
            P(("groups", "clus"), None),
            P(("groups", "clus"), None),
            P(("groups", "clus")),
            P(("groups", "clus")),
            P(("groups", "clus"), None),
            P(("groups", "clus"), None),
            P(("groups", "clus"), None),
            P(("groups", "clus")),
        ),
        out_specs=(P(("groups", "clus")), P(("groups", "clus"))),
        check_vma=False,
    )
```

```python
import functools
import math

import jax
import jax.numpy as jnp
from jax import lax
from jax.experimental import pallas as pl
from jax.experimental.pallas import tpu as pltpu
from jax.sharding import PartitionSpec as P

RB = 64
CB = 16
ITERS = 3
LANES = 128
VMEM_LIMIT = 48 * 1024 * 1024

F32 = jnp.float32
BF16 = jnp.bfloat16


def whole(space=pltpu.VMEM):
    return pl.BlockSpec(memory_space=space)


def exchange(row):
    peers = lax.axis_size("clus")
    return lax.all_to_all(
        jnp.broadcast_to(row[None], (peers,) + row.shape),
        "clus",
        split_axis=0,
        concat_axis=0,
        tiled=True,
    )


def partner(me, turn, peers):
    if peers & (peers - 1) == 0:
        return me ^ turn
    return (turn - me) % peers


def swap_rows(row):
    peers = lax.axis_size("clus")
    rows = []
    for turn in range(peers):
        pairs = [(partner(i, turn, peers), i) for i in range(peers)]
        same = all(a == b for a, b in pairs)
        rows.append(row if same else lax.ppermute(row, "clus", pairs))
    return rows


def pick_kernel(column, me_ref, notes_ref, emb_ref, out_ref, sems):
    peers = out_ref.shape[0]

    def copy(d):
        block = jnp.maximum(notes_ref[d, 0, column + me_ref[0]].astype(jnp.int32), 0)
        return pltpu.make_async_copy(emb_ref.at[block], out_ref.at[d], sems.at[d])

    @pl.loop(0, peers)
    def _(d):
        copy(d).start()

    @pl.loop(0, peers)
    def _(d):
        copy(d).wait()


def pick_blocks(me, notes, column, blocks):
    peers = notes.shape[0]
    return pl.pallas_call(
        functools.partial(pick_kernel, column),
        out_shape=jax.ShapeDtypeStruct((peers,) + blocks.shape[1:], F32),
        in_specs=[whole(pltpu.SMEM), whole(pltpu.SMEM), whole()],
        out_specs=whole(pl.ANY),
        scratch_shapes=[pltpu.SemaphoreType.DMA((peers,))],
        name="pick_blocks",
    )(me, notes, blocks)


def split_kernel(x_ref, high_ref, low_ref):
    x = x_ref[...]
    high = x.astype(BF16)
    high_ref[...] = high
    low_ref[...] = (x - high.astype(F32)).astype(BF16)


def split(x):
    return pl.pallas_call(
        split_kernel,
        out_shape=(jax.ShapeDtypeStruct(x.shape, BF16),) * 2,
        in_specs=[whole()],
        out_specs=(whole(), whole()),
        name="split_pool",
        cost_estimate=pl.CostEstimate(
            flops=3 * x.size, bytes_accessed=8 * x.size, transcendentals=0
        ),
        compiler_params=pltpu.CompilerParams(vmem_limit_bytes=VMEM_LIMIT),
    )(x)


def assemble_kernel(
    scale, high_ref, low_ref, arrived_ref, listed_ref, mass_ref, kernel_ref, out_ref
):
    q = arrived_ref[...]
    q_high = q.astype(BF16)
    q_low = (q - q_high.astype(F32)).astype(BF16)

    def product(a, b):
        return lax.dot_general(a, b, (((1,), (1,)), ((), ())), preferred_element_type=F32)

    sums = jnp.zeros((1, kernel_ref.shape[1]), F32)
    rows = 256 if kernel_ref.shape[0] % 256 == 0 else RB
    for start in range(0, kernel_ref.shape[0], rows):
        part = pl.ds(start, rows)
        high = high_ref[part, :]
        scores = product(high, q_high) + (product(high, q_low) + product(low_ref[part, :], q_high))
        for block in range(rows // RB):
            inner = pl.ds(start + block * RB, RB)
            at = start // RB + block
            listed = listed_ref[at : at + 1, :] > 0
            values = jnp.where(
                listed, jnp.exp(scores[block * RB : (block + 1) * RB] * scale), 0.0
            )
            kernel_ref[inner, :] = values
            scaling = mass_ref[inner, :] / jnp.sum(values, axis=1, keepdims=True)
            sums += jnp.sum(values * scaling, axis=0, keepdims=True)
    out_ref[...] = sums


def assemble(high, low, arrived, listed, mass):
    rows, width = high.shape
    columns = arrived.shape[0]
    return pl.pallas_call(
        functools.partial(assemble_kernel, 1.5 / math.sqrt(width)),
        out_shape=(
            jax.ShapeDtypeStruct((rows, columns), F32),
            jax.ShapeDtypeStruct((1, columns), F32),
        ),
        in_specs=[whole()] * 5,
        out_specs=(whole(), whole()),
        name="assemble",
        cost_estimate=pl.CostEstimate(
            flops=6 * rows * columns * width,
            bytes_accessed=4 * rows * width + 4 * columns * width + 4 * rows * columns,
            transcendentals=rows * columns,
        ),
        compiler_params=pltpu.CompilerParams(vmem_limit_bytes=VMEM_LIMIT),
    )(high, low, arrived, listed, mass)


def iterate_kernel(peers, kernel_ref, same_ref, slot_mass_ref, spare_ref, mass_ref, *refs):
    rows, (out_ref, *log_refs) = refs[:peers], refs[peers:]
    col_sums = rows[0][...] * same_ref[0]
    for turn in range(1, peers):
        col_sums += rows[turn][...] * same_ref[turn]
    target_scaling = slot_mass_ref[...] / (col_sums + spare_ref[...])
    sums = jnp.zeros_like(target_scaling)
    for start in range(0, kernel_ref.shape[0], RB):
        inner = pl.ds(start, RB)
        values = kernel_ref[inner, :]
        scaling = mass_ref[inner, :] / jnp.sum(values * target_scaling, axis=1, keepdims=True)
        sums += jnp.sum(values * scaling, axis=0, keepdims=True)
        for log_ref in log_refs:
            log_ref[inner, :] = jnp.log(scaling)
    out_ref[...] = sums


def iterate(kernel, notes, same, slot_mass, spare, mass, last):
    rows, columns = kernel.shape
    out_shape = [jax.ShapeDtypeStruct((1, columns), F32)]
    if last:
        out_shape.append(jax.ShapeDtypeStruct((rows, 1), F32))
    return pl.pallas_call(
        functools.partial(iterate_kernel, len(notes)),
        out_shape=out_shape,
        in_specs=[whole()] * (5 + len(notes)),
        out_specs=[whole()] * len(out_shape),
        name="iterate",
        cost_estimate=pl.CostEstimate(
            flops=4 * rows * columns, bytes_accessed=4 * rows * columns, transcendentals=0
        ),
        compiler_params=pltpu.CompilerParams(vmem_limit_bytes=VMEM_LIMIT),
    )(kernel, same, slot_mass, spare, mass, *notes)


def finish_kernel(peers, own_ref, mass_ref, *refs):
    rows, out_ref = refs[:peers], refs[peers]
    total = rows[0][...] * own_ref[0]
    for turn in range(1, peers):
        total += rows[turn][...] * own_ref[turn]
    folded = total[:, :LANES]
    for start in range(LANES, total.shape[1], LANES):
        folded += total[:, start : start + LANES]
    step = LANES // 2
    while step >= CB:
        folded += pltpu.roll(folded, step, 1)
        step //= 2
    blocks = folded.shape[0]
    lane = lax.broadcasted_iota(jnp.int32, (blocks, LANES), 1)
    block = lax.broadcasted_iota(jnp.int32, (blocks, LANES), 0)
    col_sums = jnp.sum(jnp.where(lane // CB == block, folded, 0.0), axis=0, keepdims=True)
    out_ref[...] = jnp.log(mass_ref[...] / col_sums)


def finish(notes, own, mass):
    return pl.pallas_call(
        functools.partial(finish_kernel, len(notes)),
        out_shape=jax.ShapeDtypeStruct(mass.shape, F32),
        in_specs=[whole()] * (2 + len(notes)),
        out_specs=whole(),
        name="finish",
        compiler_params=pltpu.CompilerParams(vmem_limit_bytes=VMEM_LIMIT),
    )(own, mass, *notes)


def local(
    pool_emb,
    target_emb,
    pool_mass,
    target_mass,
    fetch_table,
    pair_pool,
    listed_pair_slot,
    pair_count,
):
    peers = lax.axis_size("clus")
    me = lax.axis_index("clus")
    width = pool_emb.shape[1]
    pool_count = pool_emb.shape[0] // RB
    targets = target_emb.shape[0]
    target_count = targets // CB
    columns = peers * CB

    table_width = -(-peers // LANES) * LANES
    note = jnp.concatenate(
        [
            target_mass[None],
            jnp.pad(fetch_table.astype(F32), ((0, 0), (0, table_width - peers))),
        ],
        axis=1,
    )
    notes = exchange(note)
    outgoing = pick_blocks(
        me.astype(jnp.int32)[None], notes, targets, target_emb.reshape(target_count, CB, width)
    )
    arrived = lax.all_to_all(
        outgoing, "clus", split_axis=0, concat_axis=0, tiled=True
    ).reshape(columns, width)

    table = fetch_table[0]
    tables = notes[:, 0, targets : targets + peers].astype(jnp.int32)
    masses = notes[:, 0, :targets].reshape(peers, target_count, CB)
    valid = table >= 0
    chosen = table[:, None] == jnp.arange(target_count)[None, :]
    slot_mass = jnp.sum(jnp.where(chosen[:, :, None], masses, 0.0), axis=1).reshape(1, columns)
    spare = jnp.repeat(jnp.where(valid, 0.0, 1.0), CB).reshape(1, columns)
    order = partner(me, jnp.arange(peers), peers)
    same = jnp.repeat((tables[order] == table[None, :]).astype(F32), CB, axis=1)[:, None, :]
    asked = lax.dynamic_index_in_dim(tables, me, 1, keepdims=False)[order]
    own = (
        (asked[:, None, None] == jnp.arange(target_count)[None, :, None])
        & ((jnp.arange(columns) // CB == me)[None, None, :])
    ).astype(F32)
    live = jnp.arange(pair_pool.shape[1]) < pair_count[0]
    pool_hot = (pair_pool[0][None, :] == jnp.arange(pool_count)[:, None]).astype(BF16)
    slot_hot = (
        (listed_pair_slot[0][:, None] == (jnp.arange(columns) // CB)[None, :]) & live[:, None]
    ).astype(BF16)
    listed = jnp.dot(pool_hot, slot_hot, preferred_element_type=F32)
    mass = pool_mass[:, None]

    high, low = split(pool_emb)
    kernel, sums = assemble(high, low, arrived, listed, mass)
    for step in range(1, ITERS):
        sums, *logs = iterate(kernel, swap_rows(sums), same, slot_mass, spare, mass, step == ITERS - 1)
    log_target = finish(swap_rows(sums), own, target_mass[None])
    return (logs[0].reshape(-1), log_target.reshape(-1))


def solution(mesh):
    return jax.shard_map(
        local,
        mesh=mesh,
        in_specs=(
            P(("groups", "clus"), None),
            P(("groups", "clus"), None),
            P(("groups", "clus")),
            P(("groups", "clus")),
            P(("groups", "clus"), None),
            P(("groups", "clus"), None),
            P(("groups", "clus"), None),
            P(("groups", "clus")),
        ),
        out_specs=(P(("groups", "clus")), P(("groups", "clus"))),
        check_vma=False,
    )
```

```python
import functools
import math

import jax
import jax.numpy as jnp
from jax import lax
from jax.experimental import pallas as pl
from jax.experimental.pallas import tpu as pltpu
from jax.sharding import PartitionSpec as P

RB = 64
CB = 16
ITERS = 3
LANES = 128
VMEM_LIMIT = 48 * 1024 * 1024

F32 = jnp.float32
BF16 = jnp.bfloat16


def whole(space=pltpu.VMEM):
    return pl.BlockSpec(memory_space=space)


def exchange(row):
    return lax.all_gather(row, "clus", axis=0, tiled=True)


def pick_kernel(column, me_ref, notes_ref, emb_ref, out_ref, sems):
    peers = out_ref.shape[0]

    def copy(d):
        block = jnp.maximum(notes_ref[d, column + me_ref[0]].astype(jnp.int32), 0)
        return pltpu.make_async_copy(emb_ref.at[block], out_ref.at[d], sems.at[d])

    @pl.loop(0, peers)
    def _(d):
        copy(d).start()

    @pl.loop(0, peers)
    def _(d):
        copy(d).wait()


def pick_blocks(me, notes, column, blocks):
    peers = notes.shape[0]
    return pl.pallas_call(
        functools.partial(pick_kernel, column),
        out_shape=jax.ShapeDtypeStruct((peers,) + blocks.shape[1:], F32),
        in_specs=[whole(pltpu.SMEM), whole(pltpu.SMEM), whole()],
        out_specs=whole(pl.ANY),
        scratch_shapes=[pltpu.SemaphoreType.DMA((peers,))],
        name="pick_blocks",
    )(me, notes, blocks)


def split_kernel(x_ref, high_ref, low_ref):
    x = x_ref[...]
    high = x.astype(BF16)
    high_ref[...] = high
    low_ref[...] = (x - high.astype(F32)).astype(BF16)


def split(x):
    return pl.pallas_call(
        split_kernel,
        out_shape=(jax.ShapeDtypeStruct(x.shape, BF16),) * 2,
        in_specs=[whole()],
        out_specs=(whole(), whole()),
        name="split_pool",
        cost_estimate=pl.CostEstimate(
            flops=3 * x.size, bytes_accessed=8 * x.size, transcendentals=0
        ),
        compiler_params=pltpu.CompilerParams(vmem_limit_bytes=VMEM_LIMIT),
    )(x)


def assemble_kernel(
    scale, high_ref, low_ref, arrived_ref, listed_ref, mass_ref, kernel_ref, out_ref
):
    q = arrived_ref[...]
    q_high = q.astype(BF16)
    q_low = (q - q_high.astype(F32)).astype(BF16)

    def product(a, b):
        return lax.dot_general(a, b, (((1,), (1,)), ((), ())), preferred_element_type=F32)

    sums = jnp.zeros((1, kernel_ref.shape[1]), F32)
    rows = 256 if kernel_ref.shape[0] % 256 == 0 else RB
    for start in range(0, kernel_ref.shape[0], rows):
        part = pl.ds(start, rows)
        high = high_ref[part, :]
        scores = product(high, q_high) + (product(high, q_low) + product(low_ref[part, :], q_high))
        for block in range(rows // RB):
            inner = pl.ds(start + block * RB, RB)
            at = start // RB + block
            listed = listed_ref[at : at + 1, :] > 0
            values = jnp.where(
                listed, jnp.exp(scores[block * RB : (block + 1) * RB] * scale), 0.0
            )
            kernel_ref[inner, :] = values
            scaling = mass_ref[inner, :] / jnp.sum(values, axis=1, keepdims=True)
            sums += jnp.sum(values * scaling, axis=0, keepdims=True)
    out_ref[...] = sums


def assemble(high, low, arrived, listed, mass):
    rows, width = high.shape
    columns = arrived.shape[0]
    return pl.pallas_call(
        functools.partial(assemble_kernel, 1.5 / math.sqrt(width)),
        out_shape=(
            jax.ShapeDtypeStruct((rows, columns), F32),
            jax.ShapeDtypeStruct((1, columns), F32),
        ),
        in_specs=[whole()] * 5,
        out_specs=(whole(), whole()),
        name="assemble",
        cost_estimate=pl.CostEstimate(
            flops=6 * rows * columns * width,
            bytes_accessed=4 * rows * width + 4 * columns * width + 4 * rows * columns,
            transcendentals=rows * columns,
        ),
        compiler_params=pltpu.CompilerParams(vmem_limit_bytes=VMEM_LIMIT),
    )(high, low, arrived, listed, mass)


def iterate_kernel(
    kernel_ref, notes_ref, same_ref, slot_mass_ref, spare_ref, mass_ref, out_ref, *log_refs
):
    col_sums = jnp.sum(notes_ref[...] * same_ref[...], axis=0, keepdims=True)
    target_scaling = slot_mass_ref[...] / (col_sums + spare_ref[...])
    sums = jnp.zeros_like(target_scaling)
    for start in range(0, kernel_ref.shape[0], RB):
        inner = pl.ds(start, RB)
        values = kernel_ref[inner, :]
        scaling = mass_ref[inner, :] / jnp.sum(values * target_scaling, axis=1, keepdims=True)
        sums += jnp.sum(values * scaling, axis=0, keepdims=True)
        for log_ref in log_refs:
            log_ref[inner, :] = jnp.log(scaling)
    out_ref[...] = sums


def iterate(kernel, notes, same, slot_mass, spare, mass, last):
    rows, columns = kernel.shape
    out_shape = [jax.ShapeDtypeStruct((1, columns), F32)]
    if last:
        out_shape.append(jax.ShapeDtypeStruct((rows, 1), F32))
    return pl.pallas_call(
        iterate_kernel,
        out_shape=out_shape,
        in_specs=[whole()] * 6,
        out_specs=[whole()] * len(out_shape),
        name="iterate",
        cost_estimate=pl.CostEstimate(
            flops=4 * rows * columns, bytes_accessed=4 * rows * columns, transcendentals=0
        ),
        compiler_params=pltpu.CompilerParams(vmem_limit_bytes=VMEM_LIMIT),
    )(kernel, notes, same, slot_mass, spare, mass)


def finish_kernel(notes_ref, own_ref, mass_ref, out_ref):
    notes = notes_ref[...]
    blocks = own_ref.shape[0]
    block = lax.broadcasted_iota(jnp.int32, (blocks, notes.shape[1]), 0)
    total = jnp.zeros((blocks, notes.shape[1]), F32)
    for at in range(blocks):
        sums = jnp.sum(notes * own_ref[at], axis=0, keepdims=True)
        total = jnp.where(block == at, sums, total)
    folded = total[:, :LANES]
    for start in range(LANES, total.shape[1], LANES):
        folded += total[:, start : start + LANES]
    step = LANES // 2
    while step >= CB:
        folded += pltpu.roll(folded, step, 1)
        step //= 2
    blocks = folded.shape[0]
    lane = lax.broadcasted_iota(jnp.int32, (blocks, LANES), 1)
    block = lax.broadcasted_iota(jnp.int32, (blocks, LANES), 0)
    col_sums = jnp.sum(jnp.where(lane // CB == block, folded, 0.0), axis=0, keepdims=True)
    out_ref[...] = jnp.log(mass_ref[...] / col_sums)


def finish(notes, own, mass):
    return pl.pallas_call(
        finish_kernel,
        out_shape=jax.ShapeDtypeStruct(mass.shape, F32),
        in_specs=[whole()] * 3,
        out_specs=whole(),
        name="finish",
        compiler_params=pltpu.CompilerParams(vmem_limit_bytes=VMEM_LIMIT),
    )(notes, own, mass)


def local(
    pool_emb,
    target_emb,
    pool_mass,
    target_mass,
    fetch_table,
    pair_pool,
    listed_pair_slot,
    pair_count,
):
    peers = lax.axis_size("clus")
    me = lax.axis_index("clus")
    width = pool_emb.shape[1]
    pool_count = pool_emb.shape[0] // RB
    targets = target_emb.shape[0]
    target_count = targets // CB
    columns = peers * CB

    table_width = -(-peers // LANES) * LANES
    note = jnp.concatenate(
        [
            target_mass[None],
            jnp.pad(fetch_table.astype(F32), ((0, 0), (0, table_width - peers))),
        ],
        axis=1,
    )
    notes = exchange(note)
    outgoing = pick_blocks(
        me.astype(jnp.int32)[None], notes, targets, target_emb.reshape(target_count, CB, width)
    )
    arrived = lax.all_to_all(
        outgoing, "clus", split_axis=0, concat_axis=0, tiled=True
    ).reshape(columns, width)

    table = fetch_table[0]
    tables = notes[:, targets : targets + peers].astype(jnp.int32)
    masses = notes[:, :targets].reshape(peers, target_count, CB)
    valid = table >= 0
    chosen = table[:, None] == jnp.arange(target_count)[None, :]
    slot_mass = jnp.sum(jnp.where(chosen[:, :, None], masses, 0.0), axis=1).reshape(1, columns)
    spare = jnp.repeat(jnp.where(valid, 0.0, 1.0), CB).reshape(1, columns)
    same = jnp.repeat((tables == table[None, :]).astype(F32), CB, axis=1)
    asked = lax.dynamic_index_in_dim(tables, me, 1, keepdims=False)
    own = (
        (asked[None, :, None] == jnp.arange(target_count)[:, None, None])
        & ((jnp.arange(columns) // CB == me)[None, None, :])
    ).astype(F32)
    live = jnp.arange(pair_pool.shape[1]) < pair_count[0]
    pool_hot = (pair_pool[0][None, :] == jnp.arange(pool_count)[:, None]).astype(BF16)
    slot_hot = (
        (listed_pair_slot[0][:, None] == (jnp.arange(columns) // CB)[None, :]) & live[:, None]
    ).astype(BF16)
    listed = jnp.dot(pool_hot, slot_hot, preferred_element_type=F32)
    mass = pool_mass[:, None]

    high, low = split(pool_emb)
    kernel, sums = assemble(high, low, arrived, listed, mass)
    for step in range(1, ITERS):
        sums, *logs = iterate(kernel, exchange(sums), same, slot_mass, spare, mass, step == ITERS - 1)
    log_target = finish(exchange(sums), own, target_mass[None])
    return (logs[0].reshape(-1), log_target.reshape(-1))


def solution(mesh):
    return jax.shard_map(
        local,
        mesh=mesh,
        in_specs=(
            P(("groups", "clus"), None),
            P(("groups", "clus"), None),
            P(("groups", "clus")),
            P(("groups", "clus")),
            P(("groups", "clus"), None),
            P(("groups", "clus"), None),
            P(("groups", "clus"), None),
            P(("groups", "clus")),
        ),
        out_specs=(P(("groups", "clus")), P(("groups", "clus"))),
        check_vma=False,
    )
```

```python
import functools
import math

import jax
import jax.numpy as jnp
from jax import lax
from jax.experimental import pallas as pl
from jax.experimental.pallas import tpu as pltpu
from jax.sharding import PartitionSpec as P

RB = 64
CB = 16
ITERS = 3
LANES = 128
VMEM_LIMIT = 48 * 1024 * 1024

F32 = jnp.float32
BF16 = jnp.bfloat16


def whole(space=pltpu.VMEM):
    return pl.BlockSpec(memory_space=space)


def call(kernel, name, out_shape, in_specs, out_specs=None, cost=(0, 0, 0), scratch_shapes=()):
    flops, bytes_accessed, transcendentals = cost
    return pl.pallas_call(
        kernel,
        name=name,
        out_shape=out_shape,
        in_specs=in_specs,
        out_specs=jax.tree.map(lambda _: whole(), out_shape) if out_specs is None else out_specs,
        scratch_shapes=scratch_shapes,
        cost_estimate=pl.CostEstimate(
            flops=flops, bytes_accessed=bytes_accessed, transcendentals=transcendentals
        ),
        compiler_params=pltpu.CompilerParams(vmem_limit_bytes=VMEM_LIMIT),
    )


def exchange(rows):
    return lax.all_to_all(rows, "clus", split_axis=0, concat_axis=0, tiled=True)


def note_kernel(mass_ref, table_ref, out_ref):
    targets, peers = mass_ref.shape[0], table_ref.shape[1]
    shape = (out_ref.shape[0], 1)
    out_ref[:, :, :targets] = jnp.broadcast_to(mass_ref[...][None, None], shape + (targets,))
    out_ref[:, :, targets:] = jnp.zeros(shape + (out_ref.shape[2] - targets,), F32)
    out_ref[:, :, targets : targets + peers] = jnp.broadcast_to(
        table_ref[...].astype(F32)[None], shape + (peers,)
    )


def make_note(mass, table):
    peers = table.shape[1]
    length = mass.shape[0] + -(-peers // LANES) * LANES
    return call(
        note_kernel,
        "make_note",
        jax.ShapeDtypeStruct((peers, 1, length), F32),
        [whole()] * 2,
    )(mass, table)


def pick_kernel(me_ref, notes_ref, emb_ref, out_ref, asked_ref, held_ref, sems):
    peers, count = out_ref.shape[0], emb_ref.shape[0]
    first = notes_ref.shape[2] - -(-peers // LANES) * LANES
    tables = notes_ref[:, 0, first:]
    lane = lax.broadcasted_iota(jnp.int32, tables.shape, 1)
    asked = jnp.sum(jnp.where(lane == me_ref[0], tables, 0.0), axis=1, keepdims=True)
    asked_ref[...] = jnp.broadcast_to(asked, asked_ref.shape)

    def copy(d):
        return pltpu.make_async_copy(held_ref.at[d], out_ref.at[d], sems.at[d])

    def pick(d):
        wanted = jnp.broadcast_to(asked_ref[pl.ds(d, 1), :], (CB, LANES))
        for start in range(0, emb_ref.shape[2], LANES):
            columns = pl.ds(start, LANES)
            block = emb_ref[0, :, columns]
            for t in range(1, count):
                block = jnp.where(wanted == t, emb_ref[t, :, columns], block)
            held_ref[d, :, columns] = block
        copy(d).start()

    if peers <= 16:
        for d in range(peers):
            pick(d)
    else:
        pl.loop(0, peers)(pick)

    @pl.loop(0, peers)
    def _(d):
        copy(d).wait()


def pick_blocks(me, notes, blocks):
    peers = notes.shape[0]
    shape = (peers,) + blocks.shape[1:]
    return call(
        pick_kernel,
        "pick_blocks",
        jax.ShapeDtypeStruct(shape, F32),
        [whole(pltpu.SMEM), whole(), whole()],
        whole(pl.ANY),
        scratch_shapes=[
            pltpu.VMEM((peers, LANES), F32),
            pltpu.VMEM(shape, F32),
            pltpu.SemaphoreType.DMA((peers,)),
        ],
    )(me, notes, blocks)


def send_out(row, out_ref):
    out_ref[...] = jnp.broadcast_to(row[None], out_ref.shape)


def halves(x):
    high = x.astype(BF16)
    return high, (x - high.astype(F32)).astype(BF16)


def product(a, b):
    return lax.dot_general(a, b, (((1,), (1,)), ((), ())), preferred_element_type=F32)


def assemble_kernel(scale, pool_ref, arrived_ref, listed_ref, mass_ref, kernel_ref, out_ref):
    q_high, q_low = halves(arrived_ref[...])
    sums = jnp.zeros((1, kernel_ref.shape[1]), F32)
    rows = 256 if kernel_ref.shape[0] % 256 == 0 else RB
    for start in range(0, kernel_ref.shape[0], rows):
        high, low = halves(pool_ref[pl.ds(start, rows), :])
        scores = product(high, q_high) + (product(high, q_low) + product(low, q_high))
        for block in range(rows // RB):
            inner = pl.ds(start + block * RB, RB)
            at = start // RB + block
            listed = listed_ref[at : at + 1, :] > 0
            values = jnp.where(
                listed, jnp.exp(scores[block * RB : (block + 1) * RB] * scale), 0.0
            )
            kernel_ref[inner, :] = values
            scaling = mass_ref[inner, :] / jnp.sum(values, axis=1, keepdims=True)
            sums += jnp.sum(values * scaling, axis=0, keepdims=True)
    send_out(sums, out_ref)


def assemble(pool, arrived, listed, mass, peers):
    rows, width = pool.shape
    columns = arrived.shape[0]
    return call(
        functools.partial(assemble_kernel, 1.5 / math.sqrt(width)),
        "assemble",
        (
            jax.ShapeDtypeStruct((rows, columns), F32),
            jax.ShapeDtypeStruct((peers, 1, columns), F32),
        ),
        [whole()] * 4,
        cost=(
            6 * rows * columns * width,
            4 * (rows * width + columns * width + rows * columns),
            rows * columns,
        ),
    )(pool, arrived, listed, mass)


def iterate_kernel(
    kernel_ref, notes_ref, same_ref, slot_mass_ref, spare_ref, mass_ref, out_ref, *log_refs
):
    col_sums = jnp.sum(notes_ref[...] * same_ref[...], axis=0)
    target_scaling = slot_mass_ref[...] / (col_sums + spare_ref[...])
    sums = jnp.zeros_like(target_scaling)
    diagonal = lax.broadcasted_iota(jnp.int32, (LANES, LANES), 0) == lax.broadcasted_iota(
        jnp.int32, (LANES, LANES), 1
    )
    for start in range(0, kernel_ref.shape[0], LANES):
        inner = pl.ds(start, LANES)
        values = kernel_ref[inner, :]
        scaling = mass_ref[inner, :] / jnp.sum(values * target_scaling, axis=1, keepdims=True)
        sums += jnp.sum(values * scaling, axis=0, keepdims=True)
        for log_ref in log_refs:
            row = jnp.sum(jnp.where(diagonal, scaling, 0.0), axis=0, keepdims=True)
            log_ref[inner] = jnp.log(row)[0]
    send_out(sums, out_ref)


def iterate(kernel, notes, same, slot_mass, spare, mass, last):
    rows, columns = kernel.shape
    out_shape = [jax.ShapeDtypeStruct(notes.shape, F32)]
    if last:
        out_shape.append(jax.ShapeDtypeStruct((rows,), F32))
    return call(
        iterate_kernel,
        "iterate",
        out_shape,
        [whole()] * 6,
        cost=(4 * rows * columns, 4 * rows * columns, 0),
    )(kernel, notes, same, slot_mass, spare, mass)


def finish_kernel(notes_ref, mine_ref, own_ref, mass_ref, out_ref):
    rows = notes_ref[:, 0, :] * mine_ref[...]
    folded = rows[:, :LANES]
    for start in range(LANES, rows.shape[1], LANES):
        folded += rows[:, start : start + LANES]
    step = LANES // 2
    while step >= CB:
        folded += pltpu.roll(folded, step, 1)
        step //= 2
    col_sums = jnp.sum(folded * own_ref[...], axis=0)
    out_ref[...] = jnp.log(mass_ref[...] / col_sums)


def finish(notes, mine, own, mass):
    return call(
        finish_kernel,
        "finish",
        jax.ShapeDtypeStruct(mass.shape, F32),
        [whole()] * 4,
    )(notes, mine, own, mass)


def local(
    pool_emb,
    target_emb,
    pool_mass,
    target_mass,
    fetch_table,
    pair_pool,
    listed_pair_slot,
    pair_count,
):
    peers = lax.axis_size("clus")
    me = lax.axis_index("clus")
    width = pool_emb.shape[1]
    pool_count = pool_emb.shape[0] // RB
    targets = target_emb.shape[0]
    target_count = targets // CB
    columns = peers * CB

    notes = exchange(make_note(target_mass, fetch_table))
    outgoing = pick_blocks(
        me.astype(jnp.int32)[None], notes, target_emb.reshape(target_count, CB, width)
    )
    arrived = exchange(outgoing).reshape(columns, width)

    table = fetch_table[0]
    tables = notes[:, 0, targets : targets + peers].astype(jnp.int32)
    masses = notes[:, 0, :targets].reshape(peers, target_count, CB)
    chosen = table[:, None] == jnp.arange(target_count)[None, :]
    slot_mass = jnp.sum(jnp.where(chosen[:, :, None], masses, 0.0), axis=1).reshape(1, columns)
    spare = jnp.repeat(jnp.where(table >= 0, 0.0, 1.0), CB).reshape(1, columns)
    same = jnp.repeat((tables == table[None, :]).astype(F32), CB, axis=1)[:, None, :]
    asked = lax.dynamic_index_in_dim(tables, me, 1, keepdims=False)
    own = (asked[:, None] == (jnp.arange(targets) // CB)[None, :]).astype(F32)
    mine = (jnp.arange(columns) // CB == me).astype(F32)[None]
    live = jnp.arange(pair_pool.shape[1]) < pair_count[0]
    pool_hot = (pair_pool[0][None, :] == jnp.arange(pool_count)[:, None]).astype(BF16)
    slot_hot = (
        (listed_pair_slot[0][:, None] == (jnp.arange(columns) // CB)[None, :]) & live[:, None]
    ).astype(BF16)
    listed = jnp.dot(pool_hot, slot_hot, preferred_element_type=F32)
    mass = pool_mass[:, None]
    arrived, slot_mass, spare, same, own, mine, listed, mass, pool_emb, target_mass = (
        lax.optimization_barrier(
            (arrived, slot_mass, spare, same, own, mine, listed, mass, pool_emb, target_mass)
        )
    )

    kernel, sums = assemble(pool_emb, arrived, listed, mass, peers)
    for step in range(1, ITERS):
        sums, *logs = iterate(
            kernel, exchange(sums), same, slot_mass, spare, mass, step == ITERS - 1
        )
    return logs[0], finish(exchange(sums), mine, own, target_mass)


def solution(mesh):
    return jax.shard_map(
        local,
        mesh=mesh,
        in_specs=(
            P(("groups", "clus"), None),
            P(("groups", "clus"), None),
            P(("groups", "clus")),
            P(("groups", "clus")),
            P(("groups", "clus"), None),
            P(("groups", "clus"), None),
            P(("groups", "clus"), None),
            P(("groups", "clus")),
        ),
        out_specs=(P(("groups", "clus")), P(("groups", "clus"))),
        check_vma=False,
    )
```

```python
import functools
import math

import jax
import jax.numpy as jnp
from jax import lax
from jax.experimental import pallas as pl
from jax.experimental.pallas import tpu as pltpu
from jax.sharding import PartitionSpec as P

RB = 64
CB = 16
ITERS = 3
LANES = 128
VMEM_LIMIT = 48 * 1024 * 1024

F32 = jnp.float32
BF16 = jnp.bfloat16


def whole(space=pltpu.VMEM):
    return pl.BlockSpec(memory_space=space)


def call(kernel, name, out_shape, in_specs, out_specs=None, cost=(0, 0, 0), scratch_shapes=()):
    flops, bytes_accessed, transcendentals = cost
    return pl.pallas_call(
        kernel,
        name=name,
        out_shape=out_shape,
        in_specs=in_specs,
        out_specs=jax.tree.map(lambda _: whole(), out_shape) if out_specs is None else out_specs,
        scratch_shapes=scratch_shapes,
        cost_estimate=pl.CostEstimate(
            flops=flops, bytes_accessed=bytes_accessed, transcendentals=transcendentals
        ),
        compiler_params=pltpu.CompilerParams(vmem_limit_bytes=VMEM_LIMIT),
    )


def exchange(rows, groups=None):
    return lax.all_to_all(
        rows, "clus", split_axis=0, concat_axis=0, tiled=True, axis_index_groups=groups
    )


def note_kernel(mass_hbm, table_hbm, out_ref, mass_ref, table_ref, sems):
    copies = [
        pltpu.make_async_copy(mass_hbm, mass_ref, sems.at[0]),
        pltpu.make_async_copy(table_hbm, table_ref, sems.at[1]),
    ]
    for copy in copies:
        copy.start()
    for copy in copies:
        copy.wait()
    targets, peers = mass_ref.shape[1], table_ref.shape[1]
    shape = (out_ref.shape[0], 1)
    out_ref[:, :, :targets] = jnp.broadcast_to(mass_ref[...][None], shape + (targets,))
    out_ref[:, :, targets:] = jnp.zeros(shape + (out_ref.shape[2] - targets,), F32)
    out_ref[:, :, targets : targets + peers] = jnp.broadcast_to(
        table_ref[...].astype(F32)[None], shape + (peers,)
    )


def make_note(mass, table):
    peers = table.shape[1]
    length = mass.shape[1] + -(-peers // LANES) * LANES
    return call(
        note_kernel,
        "make_note",
        jax.ShapeDtypeStruct((peers, 1, length), F32),
        [whole(pl.ANY)] * 2,
        scratch_shapes=[
            pltpu.VMEM(mass.shape, F32),
            pltpu.VMEM(table.shape, jnp.int32),
            pltpu.SemaphoreType.DMA((2,)),
        ],
    )(mass, table)


def hold_kernel(x_hbm, out_ref, sem):
    copy = pltpu.make_async_copy(x_hbm, out_ref, sem)
    copy.start()
    copy.wait()


def hold(x):
    return call(
        hold_kernel,
        "hold",
        jax.ShapeDtypeStruct(x.shape, x.dtype),
        [whole(pl.ANY)],
        cost=(0, 8 * x.size, 0),
        scratch_shapes=[pltpu.SemaphoreType.DMA],
    )(x)


def pick_kernel(place_ref, notes_ref, own_ref, other_ref, out_ref, asked_ref, held_ref, sems):
    peers, sides = out_ref.shape[:2]
    count = own_ref.shape[0]
    first = notes_ref.shape[2] - -(-notes_ref.shape[0] // LANES) * LANES
    me = place_ref[0]
    side = me // peers
    tables = notes_ref[pl.ds(side * peers, peers), 0, first:]
    lane = lax.broadcasted_iota(jnp.int32, tables.shape, 1)
    for turn in range(sides):
        owner = me if turn == 0 else jnp.where(side == 0, me + peers, me - peers)
        asked = jnp.sum(jnp.where(lane == owner, tables, 0.0), axis=1, keepdims=True)
        asked_ref[turn] = jnp.broadcast_to(asked, asked_ref.shape[1:])

    def copy(d):
        return pltpu.make_async_copy(held_ref.at[d], out_ref.at[d], sems.at[d])

    def pick(d):
        for turn, emb_ref in enumerate((own_ref, other_ref)[:sides]):
            at = side if turn == 0 else 1 - side
            wanted = jnp.broadcast_to(asked_ref[turn, pl.ds(d, 1), :], (CB, LANES))
            for start in range(0, own_ref.shape[2], LANES):
                columns = pl.ds(start, LANES)
                block = emb_ref[0, :, columns]
                for t in range(1, count):
                    block = jnp.where(wanted == t, emb_ref[t, :, columns], block)
                held_ref[d, at, :, columns] = block
        copy(d).start()

    if peers <= 16:
        for d in range(peers):
            pick(d)
    else:
        pl.loop(0, peers)(pick)

    @pl.loop(0, peers)
    def _(d):
        copy(d).wait()


def pick_blocks(me, notes, own, other, sides):
    peers = notes.shape[0] // sides
    shape = (peers, sides) + own.shape[1:]
    return call(
        pick_kernel,
        "pick_blocks",
        jax.ShapeDtypeStruct(shape, F32),
        [whole(pltpu.SMEM)] + [whole()] * 3,
        whole(pl.ANY),
        scratch_shapes=[
            pltpu.VMEM((sides, peers, LANES), F32),
            pltpu.VMEM(shape, F32),
            pltpu.SemaphoreType.DMA((peers,)),
        ],
    )(me, notes, own, other)


def send_out(row, out_ref):
    out_ref[...] = jnp.broadcast_to(row[None], out_ref.shape)


def halves(x):
    high = x.astype(BF16)
    return high, (x - high.astype(F32)).astype(BF16)


def product(a, b):
    return lax.dot_general(a, b, (((1,), (1,)), ((), ())), preferred_element_type=F32)


def assemble_kernel(scale, pool_ref, arrived_ref, listed_ref, mass_ref, kernel_ref, out_ref):
    q_high, q_low = halves(arrived_ref[...])
    sums = jnp.zeros((1, kernel_ref.shape[1]), F32)
    rows = 256 if kernel_ref.shape[0] % 256 == 0 else RB
    for start in range(0, kernel_ref.shape[0], rows):
        high, low = halves(pool_ref[pl.ds(start, rows), :])
        scores = product(high, q_high) + (product(high, q_low) + product(low, q_high))
        for block in range(rows // RB):
            inner = pl.ds(start + block * RB, RB)
            at = start // RB + block
            listed = listed_ref[at : at + 1, :] > 0
            values = jnp.where(
                listed, jnp.exp(scores[block * RB : (block + 1) * RB] * scale), 0.0
            )
            kernel_ref[inner, :] = values
            scaling = mass_ref[inner, :] / jnp.sum(values, axis=1, keepdims=True)
            sums += jnp.sum(values * scaling, axis=0, keepdims=True)
    send_out(sums, out_ref)


def assemble(pool, arrived, listed, mass, peers):
    rows, width = pool.shape
    columns = arrived.shape[0]
    return call(
        functools.partial(assemble_kernel, 1.5 / math.sqrt(width)),
        "assemble",
        (
            jax.ShapeDtypeStruct((rows, columns), F32),
            jax.ShapeDtypeStruct((peers, 1, columns), F32),
        ),
        [whole()] * 4,
        cost=(
            6 * rows * columns * width,
            4 * (rows * width + columns * width + rows * columns),
            rows * columns,
        ),
    )(pool, arrived, listed, mass)


def iterate_kernel(
    kernel_ref, notes_ref, same_ref, slot_mass_ref, spare_ref, mass_ref, out_ref, *scaling_refs
):
    col_sums = jnp.sum(notes_ref[...] * same_ref[...], axis=0)
    target_scaling = slot_mass_ref[...] / (col_sums + spare_ref[...])
    sums = jnp.zeros_like(target_scaling)
    diagonal = lax.broadcasted_iota(jnp.int32, (LANES, LANES), 0) == lax.broadcasted_iota(
        jnp.int32, (LANES, LANES), 1
    )
    for start in range(0, kernel_ref.shape[0], LANES):
        inner = pl.ds(start, LANES)
        values = kernel_ref[inner, :]
        scaling = mass_ref[inner, :] / jnp.sum(values * target_scaling, axis=1, keepdims=True)
        sums += jnp.sum(values * scaling, axis=0, keepdims=True)
        for scaling_ref in scaling_refs:
            scaling_ref[:, inner] = jnp.sum(
                jnp.where(diagonal, scaling, 0.0), axis=0, keepdims=True
            )
    send_out(sums, out_ref)


def iterate(kernel, notes, same, slot_mass, spare, mass, last):
    rows, columns = kernel.shape
    out_shape = [jax.ShapeDtypeStruct(notes.shape, F32)]
    if last:
        out_shape.append(jax.ShapeDtypeStruct((1, rows), F32))
    return call(
        iterate_kernel,
        "iterate",
        out_shape,
        [whole()] * 6,
        cost=(4 * rows * columns, 4 * rows * columns, 0),
    )(kernel, notes, same, slot_mass, spare, mass)


def finish_kernel(
    notes_ref, mine_ref, own_ref, mass_ref, scaling_ref, pool_hbm, target_hbm, pool_ref, target_ref, sems
):
    pool_ref[...] = jnp.log(scaling_ref[0])
    pool_copy = pltpu.make_async_copy(pool_ref, pool_hbm, sems.at[0])
    pool_copy.start()
    rows = notes_ref[:, 0, :] * mine_ref[...]
    folded = rows[:, :LANES]
    for start in range(LANES, rows.shape[1], LANES):
        folded += rows[:, start : start + LANES]
    step = LANES // 2
    while step >= CB:
        folded += pltpu.roll(folded, step, 1)
        step //= 2
    col_sums = jnp.sum(folded * own_ref[...], axis=0)
    target_ref[...] = jnp.log(mass_ref[...] / col_sums)
    target_copy = pltpu.make_async_copy(target_ref, target_hbm, sems.at[1])
    target_copy.start()
    pool_copy.wait()
    target_copy.wait()


def finish(notes, mine, own, mass, scaling):
    shapes = (scaling.shape[1:], mass.shape)
    return call(
        finish_kernel,
        "finish",
        tuple(jax.ShapeDtypeStruct(shape, F32) for shape in shapes),
        [whole()] * 5,
        (whole(pl.ANY),) * 2,
        scratch_shapes=[pltpu.VMEM(shape, F32) for shape in shapes]
        + [pltpu.SemaphoreType.DMA((2,))],
    )(notes, mine, own, mass, scaling)


def local(
    pool_emb,
    target_emb,
    pool_mass,
    target_mass,
    fetch_table,
    pair_pool,
    listed_pair_slot,
    pair_count,
):
    peers = lax.axis_size("clus")
    me = lax.axis_index("clus").astype(jnp.int32)
    width = pool_emb.shape[1]
    pool_count = pool_emb.shape[0] // RB
    targets = target_emb.shape[0]
    target_count = targets // CB
    columns = peers * CB
    sides = 2 if peers % 2 == 0 else 1
    half = peers // sides
    slots = jnp.arange(peers)
    slots = slots % sides * half + slots // sides
    places = jnp.repeat(slots, CB)

    blocks = target_emb.reshape(target_count, CB, width)
    other = lax.ppermute(blocks, "clus", [(i, (i + half) % peers) for i in range(peers)])
    notes = exchange(make_note(target_mass[None], fetch_table))
    outgoing = pick_blocks(me[None], notes, hold(blocks), other, sides)
    groups = [list(range(side * half, side * half + half)) for side in range(sides)]
    arrived = exchange(outgoing, groups).reshape(columns, width)

    table = fetch_table[0]
    tables = notes[:, 0, targets : targets + peers].astype(jnp.int32)
    masses = notes[:, 0, :targets].reshape(peers, target_count, CB)
    chosen = table[:, None] == jnp.arange(target_count)[None, :]
    slot_mass = jnp.sum(jnp.where(chosen[:, :, None], masses, 0.0), axis=1)
    slot_mass = slot_mass.reshape(sides, half, CB).swapaxes(0, 1).reshape(1, columns)
    same = (tables == table[None, :]).reshape(peers, sides, half).swapaxes(1, 2)
    same = jnp.repeat(same.reshape(peers, peers).astype(F32), CB, axis=1)[:, None, :]
    spare = jnp.where(table >= 0, 0.0, 1.0).reshape(sides, half).swapaxes(0, 1)
    spare = jnp.repeat(spare.reshape(-1), CB).reshape(1, columns)
    asked = lax.dynamic_index_in_dim(tables, me, 1, keepdims=False)
    own = (asked[:, None] == (jnp.arange(targets) // CB)[None, :]).astype(F32)
    mine = (places == me).astype(F32)[None]
    live = jnp.arange(pair_pool.shape[1]) < pair_count[0]
    pool_hot = (pair_pool[0][None, :] == jnp.arange(pool_count)[:, None]).astype(BF16)
    slot_hot = ((listed_pair_slot[0][:, None] == places[None, :]) & live[:, None]).astype(BF16)
    listed = jnp.dot(pool_hot, slot_hot, preferred_element_type=F32)
    mass = pool_mass[:, None]
    arrived, slot_mass, spare, same, own, mine, listed, mass, pool_emb, target_mass = (
        lax.optimization_barrier(
            (arrived, slot_mass, spare, same, own, mine, listed, mass, pool_emb, target_mass)
        )
    )

    kernel, sums = assemble(pool_emb, arrived, listed, mass, peers)
    for step in range(1, ITERS):
        sums, *scalings = iterate(
            kernel, exchange(sums), same, slot_mass, spare, mass, step == ITERS - 1
        )
    return finish(exchange(sums), mine, own, target_mass, scalings[0])


def solution(mesh):
    return jax.shard_map(
        local,
        mesh=mesh,
        in_specs=(
            P(("groups", "clus"), None),
            P(("groups", "clus"), None),
            P(("groups", "clus")),
            P(("groups", "clus")),
            P(("groups", "clus"), None),
            P(("groups", "clus"), None),
            P(("groups", "clus"), None),
            P(("groups", "clus")),
        ),
        out_specs=(P(("groups", "clus")), P(("groups", "clus"))),
        check_vma=False,
    )
```

```python
import functools
import math

import jax
import jax.numpy as jnp
from jax import lax
from jax.experimental import pallas as pl
from jax.experimental.pallas import tpu as pltpu
from jax.sharding import PartitionSpec as P

RB = 64
CB = 16
ITERS = 3
LANES = 128
VMEM_LIMIT = 48 * 1024 * 1024

F32 = jnp.float32
BF16 = jnp.bfloat16


def whole(space=pltpu.VMEM):
    return pl.BlockSpec(memory_space=space)


def call(kernel, name, out_shape, in_specs, out_specs=None, cost=(0, 0, 0), scratch_shapes=()):
    flops, bytes_accessed, transcendentals = cost
    return pl.pallas_call(
        kernel,
        name=name,
        out_shape=out_shape,
        in_specs=in_specs,
        out_specs=jax.tree.map(lambda _: whole(), out_shape) if out_specs is None else out_specs,
        scratch_shapes=scratch_shapes,
        cost_estimate=pl.CostEstimate(
            flops=flops, bytes_accessed=bytes_accessed, transcendentals=transcendentals
        ),
        compiler_params=pltpu.CompilerParams(vmem_limit_bytes=VMEM_LIMIT),
    )


def exchange(rows, groups=None):
    return lax.all_to_all(
        rows, "clus", split_axis=0, concat_axis=0, tiled=True, axis_index_groups=groups
    )


def note_kernel(mass_hbm, table_hbm, out_ref, mass_ref, table_ref, sems):
    copies = [
        pltpu.make_async_copy(mass_hbm, mass_ref, sems.at[0]),
        pltpu.make_async_copy(table_hbm, table_ref, sems.at[1]),
    ]
    for copy in copies:
        copy.start()
    for copy in copies:
        copy.wait()
    targets, peers = mass_ref.shape[1], table_ref.shape[1]
    shape = (out_ref.shape[0], 1)
    out_ref[:, :, :targets] = jnp.broadcast_to(mass_ref[...][None], shape + (targets,))
    out_ref[:, :, targets:] = jnp.zeros(shape + (out_ref.shape[2] - targets,), F32)
    out_ref[:, :, targets : targets + peers] = jnp.broadcast_to(
        table_ref[...].astype(F32)[None], shape + (peers,)
    )


def make_note(mass, table):
    peers = table.shape[1]
    length = mass.shape[1] + -(-peers // LANES) * LANES
    return call(
        note_kernel,
        "make_note",
        jax.ShapeDtypeStruct((peers, 1, length), F32),
        [whole(pl.ANY)] * 2,
        scratch_shapes=[
            pltpu.VMEM(mass.shape, F32),
            pltpu.VMEM(table.shape, jnp.int32),
            pltpu.SemaphoreType.DMA((2,)),
        ],
    )(mass, table)


def hold_kernel(x_hbm, _, out_ref, sem):
    copy = pltpu.make_async_copy(x_hbm, out_ref, sem)
    copy.start()
    copy.wait()


def hold(x, after):
    return call(
        hold_kernel,
        "hold",
        jax.ShapeDtypeStruct(x.shape, x.dtype),
        [whole(pl.ANY)] * 2,
        cost=(2**35, 8 * x.size, 0),
        scratch_shapes=[pltpu.SemaphoreType.DMA],
    )(x, after)


def pick_kernel(place_ref, notes_ref, own_ref, other_ref, out_ref, asked_ref, held_ref, sems):
    peers, sides = out_ref.shape[:2]
    count = own_ref.shape[0]
    first = notes_ref.shape[2] - -(-notes_ref.shape[0] // LANES) * LANES
    me = place_ref[0]
    side = me // peers
    tables = notes_ref[pl.ds(side * peers, peers), 0, first:]
    lane = lax.broadcasted_iota(jnp.int32, tables.shape, 1)
    for turn in range(sides):
        owner = me if turn == 0 else jnp.where(side == 0, me + peers, me - peers)
        asked = jnp.sum(jnp.where(lane == owner, tables, 0.0), axis=1, keepdims=True)
        asked_ref[turn] = jnp.broadcast_to(asked, asked_ref.shape[1:])

    def copy(d):
        return pltpu.make_async_copy(held_ref.at[d], out_ref.at[d], sems.at[d])

    def pick(d):
        for turn, emb_ref in enumerate((own_ref, other_ref)[:sides]):
            at = side if turn == 0 else 1 - side
            wanted = jnp.broadcast_to(asked_ref[turn, pl.ds(d, 1), :], (CB, LANES))
            for start in range(0, own_ref.shape[2], LANES):
                columns = pl.ds(start, LANES)
                block = emb_ref[0, :, columns]
                for t in range(1, count):
                    block = jnp.where(wanted == t, emb_ref[t, :, columns], block)
                held_ref[d, at, :, columns] = block
        copy(d).start()

    if peers <= 16:
        for d in range(peers):
            pick(d)
    else:
        pl.loop(0, peers)(pick)

    @pl.loop(0, peers)
    def _(d):
        copy(d).wait()


def pick_blocks(me, notes, own, other, sides):
    peers = notes.shape[0] // sides
    shape = (peers, sides) + own.shape[1:]
    return call(
        pick_kernel,
        "pick_blocks",
        jax.ShapeDtypeStruct(shape, F32),
        [whole(pltpu.SMEM)] + [whole()] * 3,
        whole(pl.ANY),
        scratch_shapes=[
            pltpu.VMEM((sides, peers, LANES), F32),
            pltpu.VMEM(shape, F32),
            pltpu.SemaphoreType.DMA((peers,)),
        ],
    )(me, notes, own, other)


def send_out(row, out_ref):
    out_ref[...] = jnp.broadcast_to(row[None], out_ref.shape)


def halves(x):
    high = x.astype(BF16)
    return high, (x - high.astype(F32)).astype(BF16)


def product(a, b):
    return lax.dot_general(a, b, (((1,), (1,)), ((), ())), preferred_element_type=F32)


def assemble_kernel(scale, pool_ref, arrived_ref, listed_ref, mass_ref, kernel_ref, out_ref):
    q_high, q_low = halves(arrived_ref[...])
    sums = jnp.zeros((1, kernel_ref.shape[1]), F32)
    rows = 256 if kernel_ref.shape[0] % 256 == 0 else RB
    for start in range(0, kernel_ref.shape[0], rows):
        high, low = halves(pool_ref[pl.ds(start, rows), :])
        scores = product(high, q_high) + (product(high, q_low) + product(low, q_high))
        for block in range(rows // RB):
            inner = pl.ds(start + block * RB, RB)
            at = start // RB + block
            listed = listed_ref[at : at + 1, :] > 0
            values = jnp.where(
                listed, jnp.exp(scores[block * RB : (block + 1) * RB] * scale), 0.0
            )
            kernel_ref[inner, :] = values
            scaling = mass_ref[inner, :] / jnp.sum(values, axis=1, keepdims=True)
            sums += jnp.sum(values * scaling, axis=0, keepdims=True)
    send_out(sums, out_ref)


def assemble(pool, arrived, listed, mass, peers):
    rows, width = pool.shape
    columns = arrived.shape[0]
    return call(
        functools.partial(assemble_kernel, 1.5 / math.sqrt(width)),
        "assemble",
        (
            jax.ShapeDtypeStruct((rows, columns), F32),
            jax.ShapeDtypeStruct((peers, 1, columns), F32),
        ),
        [whole()] * 4,
        cost=(
            6 * rows * columns * width,
            4 * (rows * width + columns * width + rows * columns),
            rows * columns,
        ),
    )(pool, arrived, listed, mass)


def iterate_kernel(
    kernel_ref, notes_ref, same_ref, slot_mass_ref, spare_ref, mass_ref, out_ref, *scaling_refs
):
    col_sums = jnp.sum(notes_ref[...] * same_ref[...], axis=0)
    target_scaling = slot_mass_ref[...] / (col_sums + spare_ref[...])
    sums = jnp.zeros_like(target_scaling)
    diagonal = lax.broadcasted_iota(jnp.int32, (LANES, LANES), 0) == lax.broadcasted_iota(
        jnp.int32, (LANES, LANES), 1
    )
    for start in range(0, kernel_ref.shape[0], LANES):
        inner = pl.ds(start, LANES)
        values = kernel_ref[inner, :]
        scaling = mass_ref[inner, :] / jnp.sum(values * target_scaling, axis=1, keepdims=True)
        sums += jnp.sum(values * scaling, axis=0, keepdims=True)
        for scaling_ref in scaling_refs:
            scaling_ref[:, inner] = jnp.sum(
                jnp.where(diagonal, scaling, 0.0), axis=0, keepdims=True
            )
    send_out(sums, out_ref)


def iterate(kernel, notes, same, slot_mass, spare, mass, last):
    rows, columns = kernel.shape
    out_shape = [jax.ShapeDtypeStruct(notes.shape, F32)]
    if last:
        out_shape.append(jax.ShapeDtypeStruct((1, rows), F32))
    return call(
        iterate_kernel,
        "iterate",
        out_shape,
        [whole()] * 6,
        cost=(4 * rows * columns, 4 * rows * columns, 0),
    )(kernel, notes, same, slot_mass, spare, mass)


def finish_kernel(
    notes_ref, mine_ref, own_ref, mass_ref, scaling_ref, pool_hbm, target_hbm, pool_ref, target_ref, sems
):
    pool_ref[...] = jnp.log(scaling_ref[0])
    pool_copy = pltpu.make_async_copy(pool_ref, pool_hbm, sems.at[0])
    pool_copy.start()
    rows = notes_ref[:, 0, :] * mine_ref[...]
    folded = rows[:, :LANES]
    for start in range(LANES, rows.shape[1], LANES):
        folded += rows[:, start : start + LANES]
    step = LANES // 2
    while step >= CB:
        folded += pltpu.roll(folded, step, 1)
        step //= 2
    col_sums = jnp.sum(folded * own_ref[...], axis=0)
    target_ref[...] = jnp.log(mass_ref[...] / col_sums)
    target_copy = pltpu.make_async_copy(target_ref, target_hbm, sems.at[1])
    target_copy.start()
    pool_copy.wait()
    target_copy.wait()


def finish(notes, mine, own, mass, scaling):
    shapes = (scaling.shape[1:], mass.shape)
    return call(
        finish_kernel,
        "finish",
        tuple(jax.ShapeDtypeStruct(shape, F32) for shape in shapes),
        [whole()] * 5,
        (whole(pl.ANY),) * 2,
        scratch_shapes=[pltpu.VMEM(shape, F32) for shape in shapes]
        + [pltpu.SemaphoreType.DMA((2,))],
    )(notes, mine, own, mass, scaling)


def local(
    pool_emb,
    target_emb,
    pool_mass,
    target_mass,
    fetch_table,
    pair_pool,
    listed_pair_slot,
    pair_count,
):
    peers = lax.axis_size("clus")
    me = lax.axis_index("clus").astype(jnp.int32)
    width = pool_emb.shape[1]
    pool_count = pool_emb.shape[0] // RB
    targets = target_emb.shape[0]
    target_count = targets // CB
    columns = peers * CB
    sides = 2 if peers % 2 == 0 else 1
    half = peers // sides
    slots = jnp.arange(peers)
    slots = slots % sides * half + slots // sides
    places = jnp.repeat(slots, CB)

    blocks = target_emb.reshape(target_count, CB, width)
    other = lax.ppermute(blocks, "clus", [(i, (i + half) % peers) for i in range(peers)])
    notes = exchange(make_note(target_mass[None], fetch_table))
    outgoing = pick_blocks(me[None], notes, hold(blocks, other), other, sides)
    groups = [list(range(side * half, side * half + half)) for side in range(sides)]
    arrived = exchange(outgoing, groups).reshape(columns, width)

    table = fetch_table[0]
    tables = notes[:, 0, targets : targets + peers].astype(jnp.int32)
    masses = notes[:, 0, :targets].reshape(peers, target_count, CB)
    chosen = table[:, None] == jnp.arange(target_count)[None, :]
    slot_mass = jnp.sum(jnp.where(chosen[:, :, None], masses, 0.0), axis=1)
    slot_mass = slot_mass.reshape(sides, half, CB).swapaxes(0, 1).reshape(1, columns)
    same = (tables == table[None, :]).reshape(peers, sides, half).swapaxes(1, 2)
    same = jnp.repeat(same.reshape(peers, peers).astype(F32), CB, axis=1)[:, None, :]
    spare = jnp.where(table >= 0, 0.0, 1.0).reshape(sides, half).swapaxes(0, 1)
    spare = jnp.repeat(spare.reshape(-1), CB).reshape(1, columns)
    asked = lax.dynamic_index_in_dim(tables, me, 1, keepdims=False)
    own = (asked[:, None] == (jnp.arange(targets) // CB)[None, :]).astype(F32)
    mine = (places == me).astype(F32)[None]
    live = jnp.arange(pair_pool.shape[1]) < pair_count[0]
    pool_hot = (pair_pool[0][None, :] == jnp.arange(pool_count)[:, None]).astype(BF16)
    slot_hot = ((listed_pair_slot[0][:, None] == places[None, :]) & live[:, None]).astype(BF16)
    listed = jnp.dot(pool_hot, slot_hot, preferred_element_type=F32)
    mass = pool_mass[:, None]
    arrived, slot_mass, spare, same, own, mine, listed, mass, pool_emb, target_mass = (
        lax.optimization_barrier(
            (arrived, slot_mass, spare, same, own, mine, listed, mass, pool_emb, target_mass)
        )
    )

    kernel, sums = assemble(pool_emb, arrived, listed, mass, peers)
    for step in range(1, ITERS):
        sums, *scalings = iterate(
            kernel, exchange(sums), same, slot_mass, spare, mass, step == ITERS - 1
        )
    return finish(exchange(sums), mine, own, target_mass, scalings[0])


def solution(mesh):
    return jax.shard_map(
        local,
        mesh=mesh,
        in_specs=(
            P(("groups", "clus"), None),
            P(("groups", "clus"), None),
            P(("groups", "clus")),
            P(("groups", "clus")),
            P(("groups", "clus"), None),
            P(("groups", "clus"), None),
            P(("groups", "clus"), None),
            P(("groups", "clus")),
        ),
        out_specs=(P(("groups", "clus")), P(("groups", "clus"))),
        check_vma=False,
    )
```

```python
import functools
import math

import jax
import jax.numpy as jnp
from jax import lax
from jax.experimental import pallas as pl
from jax.experimental.pallas import tpu as pltpu
from jax.sharding import PartitionSpec as P

RB = 64
CB = 16
ITERS = 3
LANES = 128
VMEM_LIMIT = 48 * 1024 * 1024

F32 = jnp.float32
BF16 = jnp.bfloat16


def whole(space=pltpu.VMEM):
    return pl.BlockSpec(memory_space=space)


def call(kernel, name, out_shape, in_specs, out_specs=None, cost=(0, 0, 0), scratch_shapes=()):
    flops, bytes_accessed, transcendentals = cost
    return pl.pallas_call(
        kernel,
        name=name,
        out_shape=out_shape,
        in_specs=in_specs,
        out_specs=jax.tree.map(lambda _: whole(), out_shape) if out_specs is None else out_specs,
        scratch_shapes=scratch_shapes,
        cost_estimate=pl.CostEstimate(
            flops=flops, bytes_accessed=bytes_accessed, transcendentals=transcendentals
        ),
        compiler_params=pltpu.CompilerParams(vmem_limit_bytes=VMEM_LIMIT),
    )


def exchange(rows, groups=None):
    return lax.all_to_all(
        rows, "clus", split_axis=0, concat_axis=0, tiled=True, axis_index_groups=groups
    )


def note_kernel(mass_hbm, table_hbm, out_ref, mass_ref, table_ref, sems):
    copies = [
        pltpu.make_async_copy(mass_hbm, mass_ref, sems.at[0]),
        pltpu.make_async_copy(table_hbm, table_ref, sems.at[1]),
    ]
    for copy in copies:
        copy.start()
    for copy in copies:
        copy.wait()
    targets, peers = mass_ref.shape[1], table_ref.shape[1]
    shape = (out_ref.shape[0], 1)
    out_ref[:, :, :targets] = jnp.broadcast_to(mass_ref[...][None], shape + (targets,))
    out_ref[:, :, targets:] = jnp.zeros(shape + (out_ref.shape[2] - targets,), F32)
    out_ref[:, :, targets : targets + peers] = jnp.broadcast_to(
        table_ref[...].astype(F32)[None], shape + (peers,)
    )


def make_note(mass, table):
    peers = table.shape[1]
    length = mass.shape[1] + -(-peers // LANES) * LANES
    return call(
        note_kernel,
        "make_note",
        jax.ShapeDtypeStruct((peers, 1, length), F32),
        [whole(pl.ANY)] * 2,
        scratch_shapes=[
            pltpu.VMEM(mass.shape, F32),
            pltpu.VMEM(table.shape, jnp.int32),
            pltpu.SemaphoreType.DMA((2,)),
        ],
    )(mass, table)


def hold_kernel(x_hbm, out_ref, sem):
    copy = pltpu.make_async_copy(x_hbm, out_ref, sem)
    copy.start()
    copy.wait()


def hold(x):
    return call(
        hold_kernel,
        "hold",
        jax.ShapeDtypeStruct(x.shape, x.dtype),
        [whole(pl.ANY)],
        cost=(0, 8 * x.size, 0),
        scratch_shapes=[pltpu.SemaphoreType.DMA],
    )(x)


def pick_kernel(other_ref, own_ref, notes_ref, place_ref, out_ref, asked_ref, held_ref, sems):
    peers, sides = out_ref.shape[:2]
    count = own_ref.shape[0]
    first = notes_ref.shape[2] - -(-notes_ref.shape[0] // LANES) * LANES
    me = place_ref[0]
    side = me // peers
    tables = notes_ref[pl.ds(side * peers, peers), 0, first:]
    lane = lax.broadcasted_iota(jnp.int32, tables.shape, 1)
    for turn in range(sides):
        owner = me if turn == 0 else jnp.where(side == 0, me + peers, me - peers)
        asked = jnp.sum(jnp.where(lane == owner, tables, 0.0), axis=1, keepdims=True)
        asked_ref[turn] = jnp.broadcast_to(asked, asked_ref.shape[1:])

    def copy(d):
        return pltpu.make_async_copy(held_ref.at[d], out_ref.at[d], sems.at[d])

    def pick(d):
        for turn, emb_ref in enumerate((own_ref, other_ref)[:sides]):
            at = side if turn == 0 else 1 - side
            wanted = jnp.broadcast_to(asked_ref[turn, pl.ds(d, 1), :], (CB, LANES))
            for start in range(0, own_ref.shape[2], LANES):
                columns = pl.ds(start, LANES)
                block = emb_ref[0, :, columns]
                for t in range(1, count):
                    block = jnp.where(wanted == t, emb_ref[t, :, columns], block)
                held_ref[d, at, :, columns] = block
        copy(d).start()

    if peers <= 16:
        for d in range(peers):
            pick(d)
    else:
        pl.loop(0, peers)(pick)

    @pl.loop(0, peers)
    def _(d):
        copy(d).wait()


def pick_blocks(me, notes, own, other, sides):
    peers = notes.shape[0] // sides
    shape = (peers, sides) + own.shape[1:]
    return call(
        pick_kernel,
        "pick_blocks",
        jax.ShapeDtypeStruct(shape, F32),
        [whole()] * 3 + [whole(pltpu.SMEM)],
        whole(pl.ANY),
        scratch_shapes=[
            pltpu.VMEM((sides, peers, LANES), F32),
            pltpu.VMEM(shape, F32),
            pltpu.SemaphoreType.DMA((peers,)),
        ],
    )(other, own, notes, me)


def send_out(row, out_ref):
    out_ref[...] = jnp.broadcast_to(row[None], out_ref.shape)


def halves(x):
    high = x.astype(BF16)
    return high, (x - high.astype(F32)).astype(BF16)


def product(a, b):
    return lax.dot_general(a, b, (((1,), (1,)), ((), ())), preferred_element_type=F32)


def assemble_kernel(scale, pool_ref, arrived_ref, listed_ref, mass_ref, kernel_ref, out_ref):
    q_high, q_low = halves(arrived_ref[...])
    sums = jnp.zeros((1, kernel_ref.shape[1]), F32)
    rows = 256 if kernel_ref.shape[0] % 256 == 0 else RB
    for start in range(0, kernel_ref.shape[0], rows):
        high, low = halves(pool_ref[pl.ds(start, rows), :])
        scores = product(high, q_high) + (product(high, q_low) + product(low, q_high))
        for block in range(rows // RB):
            inner = pl.ds(start + block * RB, RB)
            at = start // RB + block
            listed = listed_ref[at : at + 1, :] > 0
            values = jnp.where(
                listed, jnp.exp(scores[block * RB : (block + 1) * RB] * scale), 0.0
            )
            kernel_ref[inner, :] = values
            scaling = mass_ref[inner, :] / jnp.sum(values, axis=1, keepdims=True)
            sums += jnp.sum(values * scaling, axis=0, keepdims=True)
    send_out(sums, out_ref)


def assemble(pool, arrived, listed, mass, peers):
    rows, width = pool.shape
    columns = arrived.shape[0]
    return call(
        functools.partial(assemble_kernel, 1.5 / math.sqrt(width)),
        "assemble",
        (
            jax.ShapeDtypeStruct((rows, columns), F32),
            jax.ShapeDtypeStruct((peers, 1, columns), F32),
        ),
        [whole()] * 4,
        cost=(
            6 * rows * columns * width,
            4 * (rows * width + columns * width + rows * columns),
            rows * columns,
        ),
    )(pool, arrived, listed, mass)


def iterate_kernel(
    kernel_ref, notes_ref, same_ref, slot_mass_ref, spare_ref, mass_ref, out_ref, *scaling_refs
):
    col_sums = jnp.sum(notes_ref[...] * same_ref[...], axis=0)
    target_scaling = slot_mass_ref[...] / (col_sums + spare_ref[...])
    sums = jnp.zeros_like(target_scaling)
    diagonal = lax.broadcasted_iota(jnp.int32, (LANES, LANES), 0) == lax.broadcasted_iota(
        jnp.int32, (LANES, LANES), 1
    )
    for start in range(0, kernel_ref.shape[0], LANES):
        inner = pl.ds(start, LANES)
        values = kernel_ref[inner, :]
        scaling = mass_ref[inner, :] / jnp.sum(values * target_scaling, axis=1, keepdims=True)
        sums += jnp.sum(values * scaling, axis=0, keepdims=True)
        for scaling_ref in scaling_refs:
            scaling_ref[:, inner] = jnp.sum(
                jnp.where(diagonal, scaling, 0.0), axis=0, keepdims=True
            )
    send_out(sums, out_ref)


def iterate(kernel, notes, same, slot_mass, spare, mass, last):
    rows, columns = kernel.shape
    out_shape = [jax.ShapeDtypeStruct(notes.shape, F32)]
    if last:
        out_shape.append(jax.ShapeDtypeStruct((1, rows), F32))
    return call(
        iterate_kernel,
        "iterate",
        out_shape,
        [whole()] * 6,
        cost=(4 * rows * columns, 4 * rows * columns, 0),
    )(kernel, notes, same, slot_mass, spare, mass)


def finish_kernel(
    notes_ref, mine_ref, own_ref, mass_ref, scaling_ref, pool_hbm, target_hbm, pool_ref, target_ref, sems
):
    pool_ref[...] = jnp.log(scaling_ref[0])
    pool_copy = pltpu.make_async_copy(pool_ref, pool_hbm, sems.at[0])
    pool_copy.start()
    rows = notes_ref[:, 0, :] * mine_ref[...]
    folded = rows[:, :LANES]
    for start in range(LANES, rows.shape[1], LANES):
        folded += rows[:, start : start + LANES]
    step = LANES // 2
    while step >= CB:
        folded += pltpu.roll(folded, step, 1)
        step //= 2
    col_sums = jnp.sum(folded * own_ref[...], axis=0)
    target_ref[...] = jnp.log(mass_ref[...] / col_sums)
    target_copy = pltpu.make_async_copy(target_ref, target_hbm, sems.at[1])
    target_copy.start()
    pool_copy.wait()
    target_copy.wait()


def finish(notes, mine, own, mass, scaling):
    shapes = (scaling.shape[1:], mass.shape)
    return call(
        finish_kernel,
        "finish",
        tuple(jax.ShapeDtypeStruct(shape, F32) for shape in shapes),
        [whole()] * 5,
        (whole(pl.ANY),) * 2,
        scratch_shapes=[pltpu.VMEM(shape, F32) for shape in shapes]
        + [pltpu.SemaphoreType.DMA((2,))],
    )(notes, mine, own, mass, scaling)


def local(
    pool_emb,
    target_emb,
    pool_mass,
    target_mass,
    fetch_table,
    pair_pool,
    listed_pair_slot,
    pair_count,
):
    peers = lax.axis_size("clus")
    me = lax.axis_index("clus").astype(jnp.int32)
    width = pool_emb.shape[1]
    pool_count = pool_emb.shape[0] // RB
    targets = target_emb.shape[0]
    target_count = targets // CB
    columns = peers * CB
    sides = 2 if peers % 2 == 0 else 1
    half = peers // sides
    slots = jnp.arange(peers)
    slots = slots % sides * half + slots // sides
    places = jnp.repeat(slots, CB)

    blocks = target_emb.reshape(target_count, CB, width)
    other = lax.ppermute(blocks, "clus", [(i, (i + half) % peers) for i in range(peers)])
    notes = exchange(make_note(target_mass[None], fetch_table))
    outgoing = pick_blocks(me[None], notes, hold(blocks), other, sides)
    groups = [list(range(side * half, side * half + half)) for side in range(sides)]
    arrived = exchange(outgoing, groups).reshape(columns, width)

    table = fetch_table[0]
    tables = notes[:, 0, targets : targets + peers].astype(jnp.int32)
    masses = notes[:, 0, :targets].reshape(peers, target_count, CB)
    chosen = table[:, None] == jnp.arange(target_count)[None, :]
    slot_mass = jnp.sum(jnp.where(chosen[:, :, None], masses, 0.0), axis=1)
    slot_mass = slot_mass.reshape(sides, half, CB).swapaxes(0, 1).reshape(1, columns)
    same = (tables == table[None, :]).reshape(peers, sides, half).swapaxes(1, 2)
    same = jnp.repeat(same.reshape(peers, peers).astype(F32), CB, axis=1)[:, None, :]
    spare = jnp.where(table >= 0, 0.0, 1.0).reshape(sides, half).swapaxes(0, 1)
    spare = jnp.repeat(spare.reshape(-1), CB).reshape(1, columns)
    asked = lax.dynamic_index_in_dim(tables, me, 1, keepdims=False)
    own = (asked[:, None] == (jnp.arange(targets) // CB)[None, :]).astype(F32)
    mine = (places == me).astype(F32)[None]
    live = jnp.arange(pair_pool.shape[1]) < pair_count[0]
    pool_hot = (pair_pool[0][None, :] == jnp.arange(pool_count)[:, None]).astype(BF16)
    slot_hot = ((listed_pair_slot[0][:, None] == places[None, :]) & live[:, None]).astype(BF16)
    listed = jnp.dot(pool_hot, slot_hot, preferred_element_type=F32)
    mass = pool_mass[:, None]
    arrived, slot_mass, spare, same, own, mine, listed, mass, pool_emb, target_mass = (
        lax.optimization_barrier(
            (arrived, slot_mass, spare, same, own, mine, listed, mass, pool_emb, target_mass)
        )
    )

    kernel, sums = assemble(pool_emb, arrived, listed, mass, peers)
    for step in range(1, ITERS):
        sums, *scalings = iterate(
            kernel, exchange(sums), same, slot_mass, spare, mass, step == ITERS - 1
        )
    return finish(exchange(sums), mine, own, target_mass, scalings[0])


def solution(mesh):
    return jax.shard_map(
        local,
        mesh=mesh,
        in_specs=(
            P(("groups", "clus"), None),
            P(("groups", "clus"), None),
            P(("groups", "clus")),
            P(("groups", "clus")),
            P(("groups", "clus"), None),
            P(("groups", "clus"), None),
            P(("groups", "clus"), None),
            P(("groups", "clus")),
        ),
        out_specs=(P(("groups", "clus")), P(("groups", "clus"))),
        check_vma=False,
    )
```

```python
import functools
import math

import jax
import jax.numpy as jnp
from jax import lax
from jax.experimental import pallas as pl
from jax.experimental.pallas import tpu as pltpu
from jax.sharding import PartitionSpec as P

RB = 64
CB = 16
ITERS = 3
LANES = 128
VMEM_LIMIT = 48 * 1024 * 1024

F32 = jnp.float32
BF16 = jnp.bfloat16


def whole(space=pltpu.VMEM):
    return pl.BlockSpec(memory_space=space)


def call(kernel, name, out_shape, in_specs, out_specs=None, cost=(0, 0, 0), scratch_shapes=()):
    flops, bytes_accessed, transcendentals = cost
    return pl.pallas_call(
        kernel,
        name=name,
        out_shape=out_shape,
        in_specs=in_specs,
        out_specs=jax.tree.map(lambda _: whole(), out_shape) if out_specs is None else out_specs,
        scratch_shapes=scratch_shapes,
        cost_estimate=pl.CostEstimate(
            flops=flops, bytes_accessed=bytes_accessed, transcendentals=transcendentals
        ),
        compiler_params=pltpu.CompilerParams(vmem_limit_bytes=VMEM_LIMIT),
    )


def exchange(rows, groups=None):
    return lax.all_to_all(
        rows, "clus", split_axis=0, concat_axis=0, tiled=True, axis_index_groups=groups
    )


def note_kernel(mass_hbm, table_hbm, out_ref, mass_ref, table_ref, sems):
    copies = [
        pltpu.make_async_copy(mass_hbm, mass_ref, sems.at[0]),
        pltpu.make_async_copy(table_hbm, table_ref, sems.at[1]),
    ]
    for copy in copies:
        copy.start()
    for copy in copies:
        copy.wait()
    targets, peers = mass_ref.shape[1], table_ref.shape[1]
    shape = (out_ref.shape[0], 1)
    out_ref[:, :, :targets] = jnp.broadcast_to(mass_ref[...][None], shape + (targets,))
    out_ref[:, :, targets:] = jnp.zeros(shape + (out_ref.shape[2] - targets,), F32)
    out_ref[:, :, targets : targets + peers] = jnp.broadcast_to(
        table_ref[...].astype(F32)[None], shape + (peers,)
    )


def make_note(mass, table):
    peers = table.shape[1]
    length = mass.shape[1] + -(-peers // LANES) * LANES
    return call(
        note_kernel,
        "make_note",
        jax.ShapeDtypeStruct((peers, 1, length), F32),
        [whole(pl.ANY)] * 2,
        scratch_shapes=[
            pltpu.VMEM(mass.shape, F32),
            pltpu.VMEM(table.shape, jnp.int32),
            pltpu.SemaphoreType.DMA((2,)),
        ],
    )(mass, table)


def hold_kernel(x_hbm, out_ref, sem):
    copy = pltpu.make_async_copy(x_hbm, out_ref, sem)
    copy.start()
    copy.wait()


def hold(x):
    return call(
        hold_kernel,
        "hold",
        jax.ShapeDtypeStruct(x.shape, x.dtype),
        [whole(pl.ANY)],
        cost=(0, 8 * x.size, 0),
        scratch_shapes=[pltpu.SemaphoreType.DMA],
    )(x)


def pick_kernel(other_ref, own_ref, notes_ref, place_ref, out_ref, asked_ref, held_ref, sems):
    peers, sides = out_ref.shape[:2]
    count = own_ref.shape[0]
    first = notes_ref.shape[2] - -(-notes_ref.shape[0] // LANES) * LANES
    me = place_ref[0]
    side = me // peers
    tables = notes_ref[pl.ds(side * peers, peers), 0, first:]
    lane = lax.broadcasted_iota(jnp.int32, tables.shape, 1)
    for turn in range(sides):
        owner = me if turn == 0 else jnp.where(side == 0, me + peers, me - peers)
        asked = jnp.sum(jnp.where(lane == owner, tables, 0.0), axis=1, keepdims=True)
        asked_ref[turn] = jnp.broadcast_to(asked, asked_ref.shape[1:])

    def copy(d):
        return pltpu.make_async_copy(held_ref.at[d], out_ref.at[d], sems.at[d])

    def pick(d):
        for turn, emb_ref in enumerate((own_ref, other_ref)[:sides]):
            at = side if turn == 0 else 1 - side
            wanted = jnp.broadcast_to(asked_ref[turn, pl.ds(d, 1), :], (CB, LANES))
            for start in range(0, own_ref.shape[2], LANES):
                columns = pl.ds(start, LANES)
                block = emb_ref[0, :, columns]
                for t in range(1, count):
                    block = jnp.where(wanted == t, emb_ref[t, :, columns], block)
                held_ref[d, at, :, columns] = block
        copy(d).start()

    if peers <= 16:
        for d in range(peers):
            pick(d)
    else:
        pl.loop(0, peers)(pick)

    @pl.loop(0, peers)
    def _(d):
        copy(d).wait()


def pick_blocks(me, notes, own, other, sides):
    peers = notes.shape[0] // sides
    shape = (peers, sides) + own.shape[1:]
    return call(
        pick_kernel,
        "pick_blocks",
        jax.ShapeDtypeStruct(shape, F32),
        [whole()] * 3 + [whole(pltpu.SMEM)],
        whole(pl.ANY),
        scratch_shapes=[
            pltpu.VMEM((sides, peers, LANES), F32),
            pltpu.VMEM(shape, F32),
            pltpu.SemaphoreType.DMA((peers,)),
        ],
    )(other, own, notes, me)


def send_out(row, out_ref):
    out_ref[...] = jnp.broadcast_to(row[None], out_ref.shape)


def halves(x):
    high = x.astype(BF16)
    return high, (x - high.astype(F32)).astype(BF16)


def product(a, b):
    return lax.dot_general(a, b, (((1,), (1,)), ((), ())), preferred_element_type=F32)


def assemble_kernel(scale, pool_ref, arrived_ref, listed_ref, mass_ref, kernel_ref, out_ref):
    q_high, q_low = halves(arrived_ref[...])
    sums = jnp.zeros((1, kernel_ref.shape[1]), F32)
    rows = 256 if kernel_ref.shape[0] % 256 == 0 else RB
    for start in range(0, kernel_ref.shape[0], rows):
        high, low = halves(pool_ref[pl.ds(start, rows), :])
        scores = product(high, q_high) + (product(high, q_low) + product(low, q_high))
        for block in range(rows // RB):
            inner = pl.ds(start + block * RB, RB)
            at = start // RB + block
            listed = listed_ref[at : at + 1, :] > 0
            values = jnp.where(
                listed, jnp.exp(scores[block * RB : (block + 1) * RB] * scale), 0.0
            )
            kernel_ref[inner, :] = values
            scaling = mass_ref[inner, :] / jnp.sum(values, axis=1, keepdims=True)
            sums += jnp.sum(values * scaling, axis=0, keepdims=True)
    send_out(sums, out_ref)


def assemble(pool, arrived, listed, mass, peers):
    rows, width = pool.shape
    columns = arrived.shape[0]
    return call(
        functools.partial(assemble_kernel, 1.5 / math.sqrt(width)),
        "assemble",
        (
            jax.ShapeDtypeStruct((rows, columns), F32),
            jax.ShapeDtypeStruct((peers, 1, columns), F32),
        ),
        [whole()] * 4,
        cost=(
            6 * rows * columns * width,
            4 * (rows * width + columns * width + rows * columns),
            rows * columns,
        ),
    )(pool, arrived, listed, mass)


def iterate_kernel(
    kernel_ref, notes_ref, same_ref, slot_mass_ref, spare_ref, mass_ref, out_ref, *scaling_refs
):
    col_sums = jnp.sum(notes_ref[...] * same_ref[...], axis=0)
    target_scaling = slot_mass_ref[...] / (col_sums + spare_ref[...])
    sums = jnp.zeros_like(target_scaling)
    diagonal = lax.broadcasted_iota(jnp.int32, (LANES, LANES), 0) == lax.broadcasted_iota(
        jnp.int32, (LANES, LANES), 1
    )
    for start in range(0, kernel_ref.shape[0], LANES):
        inner = pl.ds(start, LANES)
        values = kernel_ref[inner, :]
        scaling = mass_ref[inner, :] / jnp.sum(values * target_scaling, axis=1, keepdims=True)
        sums += jnp.sum(values * scaling, axis=0, keepdims=True)
        for scaling_ref in scaling_refs:
            scaling_ref[:, inner] = jnp.sum(
                jnp.where(diagonal, scaling, 0.0), axis=0, keepdims=True
            )
    send_out(sums, out_ref)


def iterate(kernel, notes, same, slot_mass, spare, mass, last):
    rows, columns = kernel.shape
    out_shape = [jax.ShapeDtypeStruct(notes.shape, F32)]
    if last:
        out_shape.append(jax.ShapeDtypeStruct((1, rows), F32))
    return call(
        iterate_kernel,
        "iterate",
        out_shape,
        [whole()] * 6,
        cost=(4 * rows * columns, 4 * rows * columns, 0),
    )(kernel, notes, same, slot_mass, spare, mass)


def finish_kernel(
    notes_ref, mine_ref, own_ref, mass_ref, scaling_ref, pool_hbm, target_hbm, pool_ref, target_ref, sems
):
    pool_ref[...] = jnp.log(scaling_ref[0])
    pool_copy = pltpu.make_async_copy(pool_ref, pool_hbm, sems.at[0])
    pool_copy.start()
    rows = notes_ref[:, 0, :] * mine_ref[...]
    folded = rows[:, :LANES]
    for start in range(LANES, rows.shape[1], LANES):
        folded += rows[:, start : start + LANES]
    step = LANES // 2
    while step >= CB:
        folded += pltpu.roll(folded, step, 1)
        step //= 2
    col_sums = jnp.sum(folded * own_ref[...], axis=0)
    target_ref[...] = jnp.log(mass_ref[...] / col_sums)
    target_copy = pltpu.make_async_copy(target_ref, target_hbm, sems.at[1])
    target_copy.start()
    pool_copy.wait()
    target_copy.wait()


def finish(notes, mine, own, mass, scaling):
    shapes = (scaling.shape[1:], mass.shape)
    return call(
        finish_kernel,
        "finish",
        tuple(jax.ShapeDtypeStruct(shape, F32) for shape in shapes),
        [whole()] * 5,
        (whole(pl.ANY),) * 2,
        scratch_shapes=[pltpu.VMEM(shape, F32) for shape in shapes]
        + [pltpu.SemaphoreType.DMA((2,))],
    )(notes, mine, own, mass, scaling)


def local(
    pool_emb,
    target_emb,
    pool_mass,
    target_mass,
    fetch_table,
    pair_pool,
    listed_pair_slot,
    pair_count,
):
    peers = lax.axis_size("clus")
    me = lax.axis_index("clus").astype(jnp.int32)
    width = pool_emb.shape[1]
    pool_count = pool_emb.shape[0] // RB
    targets = target_emb.shape[0]
    target_count = targets // CB
    columns = peers * CB
    sides = 2 if peers % 2 == 0 else 1
    half = peers // sides
    slots = jnp.arange(peers)
    slots = slots % sides * half + slots // sides
    places = jnp.repeat(slots, CB)

    blocks = target_emb.reshape(target_count, CB, width)
    other = lax.ppermute(blocks, "clus", [(i, (i + half) % peers) for i in range(peers)])
    note = make_note(target_mass[None], fetch_table)
    notes = lax.cond(me < peers, exchange, jnp.zeros_like, note)
    outgoing = pick_blocks(me[None], notes, hold(blocks), other, sides)
    groups = [list(range(side * half, side * half + half)) for side in range(sides)]
    arrived = exchange(outgoing, groups).reshape(columns, width)

    table = fetch_table[0]
    tables = notes[:, 0, targets : targets + peers].astype(jnp.int32)
    masses = notes[:, 0, :targets].reshape(peers, target_count, CB)
    chosen = table[:, None] == jnp.arange(target_count)[None, :]
    slot_mass = jnp.sum(jnp.where(chosen[:, :, None], masses, 0.0), axis=1)
    slot_mass = slot_mass.reshape(sides, half, CB).swapaxes(0, 1).reshape(1, columns)
    same = (tables == table[None, :]).reshape(peers, sides, half).swapaxes(1, 2)
    same = jnp.repeat(same.reshape(peers, peers).astype(F32), CB, axis=1)[:, None, :]
    spare = jnp.where(table >= 0, 0.0, 1.0).reshape(sides, half).swapaxes(0, 1)
    spare = jnp.repeat(spare.reshape(-1), CB).reshape(1, columns)
    asked = lax.dynamic_index_in_dim(tables, me, 1, keepdims=False)
    own = (asked[:, None] == (jnp.arange(targets) // CB)[None, :]).astype(F32)
    mine = (places == me).astype(F32)[None]
    live = jnp.arange(pair_pool.shape[1]) < pair_count[0]
    pool_hot = (pair_pool[0][None, :] == jnp.arange(pool_count)[:, None]).astype(BF16)
    slot_hot = ((listed_pair_slot[0][:, None] == places[None, :]) & live[:, None]).astype(BF16)
    listed = jnp.dot(pool_hot, slot_hot, preferred_element_type=F32)
    mass = pool_mass[:, None]
    arrived, slot_mass, spare, same, own, mine, listed, mass, pool_emb, target_mass = (
        lax.optimization_barrier(
            (arrived, slot_mass, spare, same, own, mine, listed, mass, pool_emb, target_mass)
        )
    )

    kernel, sums = assemble(pool_emb, arrived, listed, mass, peers)
    for step in range(1, ITERS):
        sums, *scalings = iterate(
            kernel, exchange(sums), same, slot_mass, spare, mass, step == ITERS - 1
        )
    return finish(exchange(sums), mine, own, target_mass, scalings[0])


def solution(mesh):
    return jax.shard_map(
        local,
        mesh=mesh,
        in_specs=(
            P(("groups", "clus"), None),
            P(("groups", "clus"), None),
            P(("groups", "clus")),
            P(("groups", "clus")),
            P(("groups", "clus"), None),
            P(("groups", "clus"), None),
            P(("groups", "clus"), None),
            P(("groups", "clus")),
        ),
        out_specs=(P(("groups", "clus")), P(("groups", "clus"))),
        check_vma=False,
    )
```

```python
import functools
import math

import jax
import jax.numpy as jnp
from jax import lax
from jax.experimental import pallas as pl
from jax.experimental.pallas import tpu as pltpu
from jax.sharding import PartitionSpec as P

RB = 64
CB = 16
ITERS = 3
SIDES = 2
LANES = 128
VMEM_LIMIT = 48 * 1024 * 1024

F32 = jnp.float32
BF16 = jnp.bfloat16


def whole(space=pltpu.VMEM):
    return pl.BlockSpec(memory_space=space)


def call(kernel, name, out_shape, in_specs, out_specs=None, cost=(0, 0, 0), scratch_shapes=()):
    flops, bytes_accessed, transcendentals = cost
    return pl.pallas_call(
        kernel,
        name=name,
        out_shape=out_shape,
        in_specs=in_specs,
        out_specs=jax.tree.map(lambda _: whole(), out_shape) if out_specs is None else out_specs,
        scratch_shapes=scratch_shapes,
        cost_estimate=pl.CostEstimate(
            flops=flops, bytes_accessed=bytes_accessed, transcendentals=transcendentals
        ),
        compiler_params=pltpu.CompilerParams(vmem_limit_bytes=VMEM_LIMIT),
    )


def exchange(rows, groups=None):
    return lax.all_to_all(
        rows, "clus", split_axis=0, concat_axis=0, tiled=True, axis_index_groups=groups
    )


def note_kernel(mass_hbm, table_hbm, emb_hbm, out_ref, held_ref, mass_ref, table_ref, sems):
    copies = [
        pltpu.make_async_copy(mass_hbm, mass_ref, sems.at[0]),
        pltpu.make_async_copy(table_hbm, table_ref, sems.at[1]),
        pltpu.make_async_copy(emb_hbm, held_ref, sems.at[2]),
    ]
    for copy in copies:
        copy.start()
    for copy in copies[:2]:
        copy.wait()
    targets, peers = mass_ref.shape[1], table_ref.shape[1]
    shape = (out_ref.shape[0], 1)
    out_ref[:, :, :targets] = jnp.broadcast_to(mass_ref[...][None], shape + (targets,))
    out_ref[:, :, targets:] = jnp.zeros(shape + (out_ref.shape[2] - targets,), F32)
    out_ref[:, :, targets : targets + peers] = jnp.broadcast_to(
        table_ref[...].astype(F32)[None], shape + (peers,)
    )
    copies[2].wait()


def make_note(mass, table, blocks):
    peers = table.shape[1]
    length = mass.shape[1] + -(-peers // LANES) * LANES
    return call(
        note_kernel,
        "make_note",
        (
            jax.ShapeDtypeStruct((peers, 1, length), F32),
            jax.ShapeDtypeStruct(blocks.shape, F32),
        ),
        [whole(pltpu.HBM)] * 3,
        scratch_shapes=[
            pltpu.VMEM(mass.shape, F32),
            pltpu.VMEM(table.shape, jnp.int32),
            pltpu.SemaphoreType.DMA((3,)),
        ],
    )(mass, table, blocks)


def pick_kernel(sides, place_ref, notes_ref, *refs):
    emb_refs, (out_ref, token_ref, asked_ref, held_ref, sems) = refs[:sides], refs[sides:]
    peers = out_ref.shape[0]
    count, _, width = emb_refs[0].shape
    first = notes_ref.shape[2] - -(-notes_ref.shape[0] // LANES) * LANES
    me = place_ref[0]
    side = me // peers
    tables = notes_ref[pl.ds(side * peers, peers), 0, first:]
    lane = lax.broadcasted_iota(jnp.int32, tables.shape, 1)
    for turn in range(sides):
        owner = me if turn == 0 else jnp.where(side == 0, me + peers, me - peers)
        asked = jnp.sum(jnp.where(lane == owner, tables, 0.0), axis=1, keepdims=True)
        asked_ref[turn] = jnp.broadcast_to(asked, asked_ref.shape[1:])

    def copy(d):
        return pltpu.make_async_copy(held_ref.at[d], out_ref.at[d], sems.at[d])

    def pick(d):
        for turn, emb_ref in enumerate(emb_refs):
            at = side if turn == 0 else 1 - side
            wanted = jnp.broadcast_to(asked_ref[turn, pl.ds(d, 1), :], (CB, LANES))
            for start in range(0, width, LANES):
                columns = pl.ds(start, LANES)
                block = emb_ref[0, :, columns]
                for t in range(1, count):
                    block = jnp.where(wanted == t, emb_ref[t, :, columns], block)
                held_ref[d, at, :, columns] = block
        copy(d).start()

    if peers <= 16:
        for d in range(peers):
            pick(d)
    else:
        pl.loop(0, peers)(pick)
    token_ref[...] = jnp.zeros_like(token_ref)

    @pl.loop(0, peers)
    def _(d):
        copy(d).wait()


def pick_blocks(me, notes, sources):
    sides = len(sources)
    peers = notes.shape[0] // sides
    shape = (peers, sides) + sources[0].shape[1:]
    return call(
        functools.partial(pick_kernel, sides),
        "pick_blocks",
        (jax.ShapeDtypeStruct(shape, F32), jax.ShapeDtypeStruct((8, LANES), F32)),
        [whole(pltpu.SMEM)] + [whole()] * (1 + sides),
        (whole(pl.ANY), whole()),
        scratch_shapes=[
            pltpu.VMEM((sides, peers, LANES), F32),
            pltpu.VMEM(shape, F32),
            pltpu.SemaphoreType.DMA((peers,)),
        ],
    )(me, notes, *sources)


def iota(shape, dimension):
    return lax.broadcasted_iota(jnp.int32, shape, dimension)


def slot_at(column, half, sides):
    block = column // CB
    return block % sides * half + block // sides


def product(a, b):
    return lax.dot_general(a, b, (((1,), (1,)), ((), ())), preferred_element_type=F32)


def prepare_kernel(
    sides,
    place_ref,
    notes_ref,
    table_ref,
    pools_ref,
    slots_ref,
    pool_mass_ref,
    _,
    listed_ref,
    same_ref,
    spare_ref,
    slot_mass_ref,
    mine_ref,
    own_ref,
    mass_ref,
):
    me, live = place_ref[0], place_ref[1]
    peers, columns = own_ref.shape[0], listed_ref.shape[1]
    half = peers // sides
    targets = own_ref.shape[1]
    pairs = pools_ref.shape[1]

    def hot(rows, values):
        return (rows == values).astype(F32).astype(BF16)

    column_slot = slot_at(iota((columns, 1), 0), half, sides)
    slot = slot_at(iota((1, columns), 1), half, sides)
    mine_ref[...] = (slot == me).astype(F32)
    listing = iota((1, pairs), 1) < live
    pool_hot = hot(iota((listed_ref.shape[0], pairs), 0), pools_ref[...])
    slot_hot = hot(column_slot, jnp.where(listing, slots_ref[...], -1))
    listed_ref[...] = product(pool_hot, slot_hot)

    spread = hot(column_slot, iota((columns, peers), 1))
    tables = notes_ref[:, 0, targets : targets + peers]
    table = table_ref[...].astype(F32)
    wide_tables = product(tables.astype(BF16), spread)
    wide_table = product(table.astype(BF16), spread)
    same_ref[...] = (wide_tables == wide_table).astype(F32)
    spare_ref[...] = (wide_table < 0).astype(F32)

    square = iota((peers, peers), 0), iota((peers, peers), 1)
    asked = jnp.sum(jnp.where(square[1] == me, tables, 0.0), axis=1, keepdims=True)
    block = (iota((peers, targets), 1) // CB).astype(F32)
    own_ref[...] = (asked == block).astype(F32)

    wanted = jnp.sum(jnp.where(square[0] == square[1], table, 0.0), axis=1, keepdims=True)
    masses = jnp.where(wanted == block, notes_ref[:, 0, :targets], 0.0)
    masses = fold(masses)
    slot_mass = [
        jnp.sum(
            jnp.where(
                iota((peers, LANES), 0) == slot_at(iota((peers, LANES), 1) + start, half, sides),
                masses,
                0.0,
            ),
            axis=0,
            keepdims=True,
        )
        for start in range(0, columns, LANES)
    ]
    slot_mass_ref[...] = jnp.concatenate(slot_mass, axis=1)

    diagonal = iota((LANES, LANES), 0) == iota((LANES, LANES), 1)
    for start in range(0, mass_ref.shape[0], LANES):
        row = pool_mass_ref[:, pl.ds(start, LANES)]
        mass_ref[pl.ds(start, LANES), :] = jnp.sum(
            jnp.where(diagonal, row, 0.0), axis=1, keepdims=True
        )


def prepare(place, notes, table, pools, slots, pool_mass, token, pool_count, targets, sides):
    peers = notes.shape[0]
    columns = peers * CB
    shapes = [
        (pool_count, columns),
        (peers, columns),
        (1, columns),
        (1, columns),
        (1, columns),
        (peers, targets),
        (pool_mass.shape[1], 1),
    ]
    return call(
        functools.partial(prepare_kernel, sides),
        "prepare",
        [jax.ShapeDtypeStruct(shape, F32) for shape in shapes],
        [whole(pltpu.SMEM)] + [whole()] * 6,
    )(place, notes, table, pools, slots, pool_mass, token)


def fold(rows):
    folded = rows[:, :LANES]
    for start in range(LANES, rows.shape[1], LANES):
        folded += rows[:, start : start + LANES]
    step = LANES // 2
    while step >= CB:
        folded += pltpu.roll(folded, step, 1)
        step //= 2
    return folded


def send_out(row, out_ref):
    out_ref[...] = jnp.broadcast_to(row[None], out_ref.shape)


def halves(x):
    high = x.astype(BF16)
    return high, (x - high.astype(F32)).astype(BF16)


def assemble_kernel(scale, pool_ref, arrived_ref, listed_ref, mass_ref, kernel_ref, out_ref):
    q_high, q_low = halves(arrived_ref[...])
    sums = jnp.zeros((1, kernel_ref.shape[1]), F32)
    rows = 256 if kernel_ref.shape[0] % 256 == 0 else RB
    for start in range(0, kernel_ref.shape[0], rows):
        high, low = halves(pool_ref[pl.ds(start, rows), :])
        scores = product(high, q_high) + (product(high, q_low) + product(low, q_high))
        for block in range(rows // RB):
            inner = pl.ds(start + block * RB, RB)
            at = start // RB + block
            listed = listed_ref[at : at + 1, :] > 0
            values = jnp.where(
                listed, jnp.exp(scores[block * RB : (block + 1) * RB] * scale), 0.0
            )
            kernel_ref[inner, :] = values
            scaling = mass_ref[inner, :] / jnp.sum(values, axis=1, keepdims=True)
            sums += jnp.sum(values * scaling, axis=0, keepdims=True)
    send_out(sums, out_ref)


def assemble(pool, arrived, listed, mass, peers):
    rows, width = pool.shape
    columns = arrived.shape[0]
    return call(
        functools.partial(assemble_kernel, 1.5 / math.sqrt(width)),
        "assemble",
        (
            jax.ShapeDtypeStruct((rows, columns), F32),
            jax.ShapeDtypeStruct((peers, 1, columns), F32),
        ),
        [whole()] * 4,
        cost=(
            6 * rows * columns * width,
            4 * (rows * width + columns * width + rows * columns),
            rows * columns,
        ),
    )(pool, arrived, listed, mass)


def iterate_kernel(
    kernel_ref, notes_ref, same_ref, slot_mass_ref, spare_ref, mass_ref, out_ref, *scaling_refs
):
    col_sums = jnp.sum(notes_ref[:, 0, :] * same_ref[...], axis=0, keepdims=True)
    target_scaling = slot_mass_ref[...] / (col_sums + spare_ref[...])
    sums = jnp.zeros_like(target_scaling)
    diagonal = lax.broadcasted_iota(jnp.int32, (LANES, LANES), 0) == lax.broadcasted_iota(
        jnp.int32, (LANES, LANES), 1
    )
    for start in range(0, kernel_ref.shape[0], LANES):
        inner = pl.ds(start, LANES)
        values = kernel_ref[inner, :]
        scaling = mass_ref[inner, :] / jnp.sum(values * target_scaling, axis=1, keepdims=True)
        sums += jnp.sum(values * scaling, axis=0, keepdims=True)
        for scaling_ref in scaling_refs:
            scaling_ref[:, inner] = jnp.sum(
                jnp.where(diagonal, scaling, 0.0), axis=0, keepdims=True
            )
    send_out(sums, out_ref)


def iterate(kernel, notes, same, slot_mass, spare, mass, last):
    rows, columns = kernel.shape
    out_shape = [jax.ShapeDtypeStruct(notes.shape, F32)]
    if last:
        out_shape.append(jax.ShapeDtypeStruct((1, rows), F32))
    return call(
        iterate_kernel,
        "iterate",
        out_shape,
        [whole()] * 6,
        cost=(4 * rows * columns, 4 * rows * columns, 0),
    )(kernel, notes, same, slot_mass, spare, mass)


def finish_kernel(
    notes_ref,
    mine_ref,
    own_ref,
    mass_ref,
    scaling_ref,
    pool_hbm,
    target_hbm,
    pool_ref,
    target_ref,
    sems,
):
    pool_ref[...] = jnp.log(scaling_ref[0])
    pool_copy = pltpu.make_async_copy(pool_ref, pool_hbm, sems.at[0])
    pool_copy.start()
    col_sums = jnp.sum(fold(notes_ref[:, 0, :] * mine_ref[...]) * own_ref[...], axis=0)
    target_ref[...] = jnp.log(mass_ref[...] / col_sums)
    target_copy = pltpu.make_async_copy(target_ref, target_hbm, sems.at[1])
    target_copy.start()
    pool_copy.wait()
    target_copy.wait()


def finish(notes, mine, own, mass, scaling):
    shapes = (scaling.shape[1:], mass.shape)
    return call(
        finish_kernel,
        "finish",
        tuple(jax.ShapeDtypeStruct(shape, F32) for shape in shapes),
        [whole()] * 5,
        (whole(pl.ANY),) * 2,
        scratch_shapes=[pltpu.VMEM(shape, F32) for shape in shapes]
        + [pltpu.SemaphoreType.DMA((2,))],
    )(notes, mine, own, mass, scaling)


def local(
    pool_emb,
    target_emb,
    pool_mass,
    target_mass,
    fetch_table,
    pair_pool,
    listed_pair_slot,
    pair_count,
):
    peers = lax.axis_size("clus")
    me = lax.axis_index("clus").astype(jnp.int32)
    targets, width = target_emb.shape
    pool_count = pool_emb.shape[0] // RB
    columns = peers * CB
    sides = SIDES if peers % SIDES == 0 else 1
    half = peers // sides

    blocks = target_emb.reshape(targets // CB, CB, width)
    sources = []
    if sides == 2:
        sources = [lax.ppermute(blocks, "clus", [(i, (i + half) % peers) for i in range(peers)])]
    note, held = make_note(target_mass[None], fetch_table, blocks)
    notes = lax.cond(me < peers, exchange, jnp.zeros_like, note)
    outgoing, token = pick_blocks(me[None], notes, [held] + sources)
    groups = [list(range(side * half, side * half + half)) for side in range(sides)]
    arrived = exchange(outgoing, groups).reshape(columns, width)
    listed, same, spare, slot_mass, mine, own, mass = prepare(
        jnp.concatenate([me[None], pair_count]),
        notes,
        fetch_table,
        pair_pool,
        listed_pair_slot,
        pool_mass[None],
        token,
        pool_count,
        targets,
        sides,
    )

    kernel, sums = assemble(pool_emb, arrived, listed, mass, peers)
    for step in range(1, ITERS):
        sums, *scalings = iterate(
            kernel, exchange(sums), same, slot_mass, spare, mass, step == ITERS - 1
        )
    return finish(exchange(sums), mine, own, target_mass, scalings[0])


def solution(mesh):
    return jax.shard_map(
        local,
        mesh=mesh,
        in_specs=(
            P(("groups", "clus"), None),
            P(("groups", "clus"), None),
            P(("groups", "clus")),
            P(("groups", "clus")),
            P(("groups", "clus"), None),
            P(("groups", "clus"), None),
            P(("groups", "clus"), None),
            P(("groups", "clus")),
        ),
        out_specs=(P(("groups", "clus")), P(("groups", "clus"))),
        check_vma=False,
    )
```

```python
import functools
import math

import jax
import jax.numpy as jnp
from jax import lax
from jax.experimental import pallas as pl
from jax.experimental.pallas import tpu as pltpu
from jax.sharding import PartitionSpec as P

RB = 64
CB = 16
ITERS = 3
SIDES = 1
LANES = 128
VMEM_LIMIT = 48 * 1024 * 1024

F32 = jnp.float32
BF16 = jnp.bfloat16


def whole(space=pltpu.VMEM):
    return pl.BlockSpec(memory_space=space)


def call(kernel, name, out_shape, in_specs, out_specs=None, cost=(0, 0, 0), scratch_shapes=()):
    flops, bytes_accessed, transcendentals = cost
    return pl.pallas_call(
        kernel,
        name=name,
        out_shape=out_shape,
        in_specs=in_specs,
        out_specs=jax.tree.map(lambda _: whole(), out_shape) if out_specs is None else out_specs,
        scratch_shapes=scratch_shapes,
        cost_estimate=pl.CostEstimate(
            flops=flops, bytes_accessed=bytes_accessed, transcendentals=transcendentals
        ),
        compiler_params=pltpu.CompilerParams(vmem_limit_bytes=VMEM_LIMIT),
    )


def exchange(rows, groups=None):
    return lax.all_to_all(
        rows, "clus", split_axis=0, concat_axis=0, tiled=True, axis_index_groups=groups
    )


def note_kernel(mass_hbm, table_hbm, emb_hbm, out_ref, held_ref, mass_ref, table_ref, sems):
    copies = [
        pltpu.make_async_copy(mass_hbm, mass_ref, sems.at[0]),
        pltpu.make_async_copy(table_hbm, table_ref, sems.at[1]),
        pltpu.make_async_copy(emb_hbm, held_ref, sems.at[2]),
    ]
    for copy in copies:
        copy.start()
    for copy in copies[:2]:
        copy.wait()
    targets, peers = mass_ref.shape[1], table_ref.shape[1]
    shape = (out_ref.shape[0], 1)
    out_ref[:, :, :targets] = jnp.broadcast_to(mass_ref[...][None], shape + (targets,))
    out_ref[:, :, targets:] = jnp.zeros(shape + (out_ref.shape[2] - targets,), F32)
    out_ref[:, :, targets : targets + peers] = jnp.broadcast_to(
        table_ref[...].astype(F32)[None], shape + (peers,)
    )
    copies[2].wait()


def make_note(mass, table, blocks):
    peers = table.shape[1]
    length = mass.shape[1] + -(-peers // LANES) * LANES
    return call(
        note_kernel,
        "make_note",
        (
            jax.ShapeDtypeStruct((peers, 1, length), F32),
            jax.ShapeDtypeStruct(blocks.shape, F32),
        ),
        [whole(pltpu.HBM)] * 3,
        scratch_shapes=[
            pltpu.VMEM(mass.shape, F32),
            pltpu.VMEM(table.shape, jnp.int32),
            pltpu.SemaphoreType.DMA((3,)),
        ],
    )(mass, table, blocks)


def pick_kernel(sides, place_ref, notes_ref, *refs):
    emb_refs, (out_ref, token_ref, asked_ref, held_ref, sems) = refs[:sides], refs[sides:]
    peers = out_ref.shape[0]
    count, _, width = emb_refs[0].shape
    first = notes_ref.shape[2] - -(-notes_ref.shape[0] // LANES) * LANES
    me = place_ref[0]
    side = me // peers
    tables = notes_ref[pl.ds(side * peers, peers), 0, first:]
    lane = lax.broadcasted_iota(jnp.int32, tables.shape, 1)
    for turn in range(sides):
        owner = me if turn == 0 else jnp.where(side == 0, me + peers, me - peers)
        asked = jnp.sum(jnp.where(lane == owner, tables, 0.0), axis=1, keepdims=True)
        asked_ref[turn] = jnp.broadcast_to(asked, asked_ref.shape[1:])

    def copy(d):
        return pltpu.make_async_copy(held_ref.at[d], out_ref.at[d], sems.at[d])

    def pick(d):
        for turn, emb_ref in enumerate(emb_refs):
            at = side if turn == 0 else 1 - side
            wanted = jnp.broadcast_to(asked_ref[turn, pl.ds(d, 1), :], (CB, LANES))
            for start in range(0, width, LANES):
                columns = pl.ds(start, LANES)
                block = emb_ref[0, :, columns]
                for t in range(1, count):
                    block = jnp.where(wanted == t, emb_ref[t, :, columns], block)
                held_ref[d, at, :, columns] = block
        copy(d).start()

    if peers <= 16:
        for d in range(peers):
            pick(d)
    else:
        pl.loop(0, peers)(pick)
    token_ref[...] = jnp.zeros_like(token_ref)

    @pl.loop(0, peers)
    def _(d):
        copy(d).wait()


def pick_blocks(me, notes, sources):
    sides = len(sources)
    peers = notes.shape[0] // sides
    shape = (peers, sides) + sources[0].shape[1:]
    return call(
        functools.partial(pick_kernel, sides),
        "pick_blocks",
        (jax.ShapeDtypeStruct(shape, F32), jax.ShapeDtypeStruct((8, LANES), F32)),
        [whole(pltpu.SMEM)] + [whole()] * (1 + sides),
        (whole(pl.ANY), whole()),
        scratch_shapes=[
            pltpu.VMEM((sides, peers, LANES), F32),
            pltpu.VMEM(shape, F32),
            pltpu.SemaphoreType.DMA((peers,)),
        ],
    )(me, notes, *sources)


def iota(shape, dimension):
    return lax.broadcasted_iota(jnp.int32, shape, dimension)


def slot_at(column, half, sides):
    block = column // CB
    return block % sides * half + block // sides


def product(a, b):
    return lax.dot_general(a, b, (((1,), (1,)), ((), ())), preferred_element_type=F32)


def prepare_kernel(
    sides,
    place_ref,
    notes_ref,
    table_ref,
    pools_ref,
    slots_ref,
    pool_mass_ref,
    _,
    listed_ref,
    same_ref,
    spare_ref,
    slot_mass_ref,
    mine_ref,
    own_ref,
    mass_ref,
):
    me, live = place_ref[0], place_ref[1]
    peers, columns = own_ref.shape[0], listed_ref.shape[1]
    half = peers // sides
    targets = own_ref.shape[1]
    pairs = pools_ref.shape[1]

    def hot(rows, values):
        return (rows == values).astype(F32).astype(BF16)

    column_slot = slot_at(iota((columns, 1), 0), half, sides)
    slot = slot_at(iota((1, columns), 1), half, sides)
    mine_ref[...] = (slot == me).astype(F32)
    listing = iota((1, pairs), 1) < live
    pool_hot = hot(iota((listed_ref.shape[0], pairs), 0), pools_ref[...])
    slot_hot = hot(column_slot, jnp.where(listing, slots_ref[...], -1))
    listed_ref[...] = product(pool_hot, slot_hot)

    spread = hot(column_slot, iota((columns, peers), 1))
    tables = notes_ref[:, 0, targets : targets + peers]
    table = table_ref[...].astype(F32)
    wide_tables = product(tables.astype(BF16), spread)
    wide_table = product(table.astype(BF16), spread)
    same_ref[...] = (wide_tables == wide_table).astype(F32)
    spare_ref[...] = (wide_table < 0).astype(F32)

    square = iota((peers, peers), 0), iota((peers, peers), 1)
    asked = jnp.sum(jnp.where(square[1] == me, tables, 0.0), axis=1, keepdims=True)
    block = (iota((peers, targets), 1) // CB).astype(F32)
    own_ref[...] = (asked == block).astype(F32)

    wanted = jnp.sum(jnp.where(square[0] == square[1], table, 0.0), axis=1, keepdims=True)
    masses = jnp.where(wanted == block, notes_ref[:, 0, :targets], 0.0)
    masses = fold(masses)
    slot_mass = [
        jnp.sum(
            jnp.where(
                iota((peers, LANES), 0) == slot_at(iota((peers, LANES), 1) + start, half, sides),
                masses,
                0.0,
            ),
            axis=0,
            keepdims=True,
        )
        for start in range(0, columns, LANES)
    ]
    slot_mass_ref[...] = jnp.concatenate(slot_mass, axis=1)

    diagonal = iota((LANES, LANES), 0) == iota((LANES, LANES), 1)
    for start in range(0, mass_ref.shape[0], LANES):
        row = pool_mass_ref[:, pl.ds(start, LANES)]
        mass_ref[pl.ds(start, LANES), :] = jnp.sum(
            jnp.where(diagonal, row, 0.0), axis=1, keepdims=True
        )


def prepare(place, notes, table, pools, slots, pool_mass, token, pool_count, targets, sides):
    peers = notes.shape[0]
    columns = peers * CB
    shapes = [
        (pool_count, columns),
        (peers, columns),
        (1, columns),
        (1, columns),
        (1, columns),
        (peers, targets),
        (pool_mass.shape[1], 1),
    ]
    return call(
        functools.partial(prepare_kernel, sides),
        "prepare",
        [jax.ShapeDtypeStruct(shape, F32) for shape in shapes],
        [whole(pltpu.SMEM)] + [whole()] * 6,
    )(place, notes, table, pools, slots, pool_mass, token)


def fold(rows):
    folded = rows[:, :LANES]
    for start in range(LANES, rows.shape[1], LANES):
        folded += rows[:, start : start + LANES]
    step = LANES // 2
    while step >= CB:
        folded += pltpu.roll(folded, step, 1)
        step //= 2
    return folded


def send_out(row, out_ref):
    out_ref[...] = jnp.broadcast_to(row[None], out_ref.shape)


def halves(x):
    high = x.astype(BF16)
    return high, (x - high.astype(F32)).astype(BF16)


def assemble_kernel(scale, pool_ref, arrived_ref, listed_ref, mass_ref, kernel_ref, out_ref):
    q_high, q_low = halves(arrived_ref[...])
    sums = jnp.zeros((1, kernel_ref.shape[1]), F32)
    rows = 256 if kernel_ref.shape[0] % 256 == 0 else RB
    for start in range(0, kernel_ref.shape[0], rows):
        high, low = halves(pool_ref[pl.ds(start, rows), :])
        scores = product(high, q_high) + (product(high, q_low) + product(low, q_high))
        for block in range(rows // RB):
            inner = pl.ds(start + block * RB, RB)
            at = start // RB + block
            listed = listed_ref[at : at + 1, :] > 0
            values = jnp.where(
                listed, jnp.exp(scores[block * RB : (block + 1) * RB] * scale), 0.0
            )
            kernel_ref[inner, :] = values
            scaling = mass_ref[inner, :] / jnp.sum(values, axis=1, keepdims=True)
            sums += jnp.sum(values * scaling, axis=0, keepdims=True)
    send_out(sums, out_ref)


def assemble(pool, arrived, listed, mass, peers):
    rows, width = pool.shape
    columns = arrived.shape[0]
    return call(
        functools.partial(assemble_kernel, 1.5 / math.sqrt(width)),
        "assemble",
        (
            jax.ShapeDtypeStruct((rows, columns), F32),
            jax.ShapeDtypeStruct((peers, 1, columns), F32),
        ),
        [whole()] * 4,
        cost=(
            6 * rows * columns * width,
            4 * (rows * width + columns * width + rows * columns),
            rows * columns,
        ),
    )(pool, arrived, listed, mass)


def iterate_kernel(
    kernel_ref, notes_ref, same_ref, slot_mass_ref, spare_ref, mass_ref, out_ref, *scaling_refs
):
    col_sums = jnp.sum(notes_ref[:, 0, :] * same_ref[...], axis=0, keepdims=True)
    target_scaling = slot_mass_ref[...] / (col_sums + spare_ref[...])
    sums = jnp.zeros_like(target_scaling)
    diagonal = lax.broadcasted_iota(jnp.int32, (LANES, LANES), 0) == lax.broadcasted_iota(
        jnp.int32, (LANES, LANES), 1
    )
    for start in range(0, kernel_ref.shape[0], LANES):
        inner = pl.ds(start, LANES)
        values = kernel_ref[inner, :]
        scaling = mass_ref[inner, :] / jnp.sum(values * target_scaling, axis=1, keepdims=True)
        sums += jnp.sum(values * scaling, axis=0, keepdims=True)
        for scaling_ref in scaling_refs:
            scaling_ref[:, inner] = jnp.sum(
                jnp.where(diagonal, scaling, 0.0), axis=0, keepdims=True
            )
    send_out(sums, out_ref)


def iterate(kernel, notes, same, slot_mass, spare, mass, last):
    rows, columns = kernel.shape
    out_shape = [jax.ShapeDtypeStruct(notes.shape, F32)]
    if last:
        out_shape.append(jax.ShapeDtypeStruct((1, rows), F32))
    return call(
        iterate_kernel,
        "iterate",
        out_shape,
        [whole()] * 6,
        cost=(4 * rows * columns, 4 * rows * columns, 0),
    )(kernel, notes, same, slot_mass, spare, mass)


def finish_kernel(
    notes_ref,
    mine_ref,
    own_ref,
    mass_ref,
    scaling_ref,
    pool_hbm,
    target_hbm,
    pool_ref,
    target_ref,
    sems,
):
    pool_ref[...] = jnp.log(scaling_ref[0])
    pool_copy = pltpu.make_async_copy(pool_ref, pool_hbm, sems.at[0])
    pool_copy.start()
    col_sums = jnp.sum(fold(notes_ref[:, 0, :] * mine_ref[...]) * own_ref[...], axis=0)
    target_ref[...] = jnp.log(mass_ref[...] / col_sums)
    target_copy = pltpu.make_async_copy(target_ref, target_hbm, sems.at[1])
    target_copy.start()
    pool_copy.wait()
    target_copy.wait()


def finish(notes, mine, own, mass, scaling):
    shapes = (scaling.shape[1:], mass.shape)
    return call(
        finish_kernel,
        "finish",
        tuple(jax.ShapeDtypeStruct(shape, F32) for shape in shapes),
        [whole()] * 5,
        (whole(pl.ANY),) * 2,
        scratch_shapes=[pltpu.VMEM(shape, F32) for shape in shapes]
        + [pltpu.SemaphoreType.DMA((2,))],
    )(notes, mine, own, mass, scaling)


def local(
    pool_emb,
    target_emb,
    pool_mass,
    target_mass,
    fetch_table,
    pair_pool,
    listed_pair_slot,
    pair_count,
):
    peers = lax.axis_size("clus")
    me = lax.axis_index("clus").astype(jnp.int32)
    targets, width = target_emb.shape
    pool_count = pool_emb.shape[0] // RB
    columns = peers * CB
    sides = SIDES if peers % SIDES == 0 else 1
    half = peers // sides

    blocks = target_emb.reshape(targets // CB, CB, width)
    sources = []
    if sides == 2:
        sources = [lax.ppermute(blocks, "clus", [(i, (i + half) % peers) for i in range(peers)])]
    note, held = make_note(target_mass[None], fetch_table, blocks)
    notes = exchange(note)
    outgoing, token = pick_blocks(me[None], notes, [held] + sources)
    groups = [list(range(side * half, side * half + half)) for side in range(sides)]
    arrived = exchange(outgoing, groups).reshape(columns, width)
    listed, same, spare, slot_mass, mine, own, mass = prepare(
        jnp.concatenate([me[None], pair_count]),
        notes,
        fetch_table,
        pair_pool,
        listed_pair_slot,
        pool_mass[None],
        token,
        pool_count,
        targets,
        sides,
    )

    kernel, sums = assemble(pool_emb, arrived, listed, mass, peers)
    for step in range(1, ITERS):
        sums, *scalings = iterate(
            kernel, exchange(sums), same, slot_mass, spare, mass, step == ITERS - 1
        )
    return finish(exchange(sums), mine, own, target_mass, scalings[0])


def solution(mesh):
    return jax.shard_map(
        local,
        mesh=mesh,
        in_specs=(
            P(("groups", "clus"), None),
            P(("groups", "clus"), None),
            P(("groups", "clus")),
            P(("groups", "clus")),
            P(("groups", "clus"), None),
            P(("groups", "clus"), None),
            P(("groups", "clus"), None),
            P(("groups", "clus")),
        ),
        out_specs=(P(("groups", "clus")), P(("groups", "clus"))),
        check_vma=False,
    )
```

```python
import functools
import math

import jax
import jax.numpy as jnp
from jax import lax
from jax.experimental import pallas as pl
from jax.experimental.pallas import tpu as pltpu
from jax.sharding import PartitionSpec as P

RB = 64
CB = 16
ITERS = 3
SIDES = 2
LANES = 128
VMEM_LIMIT = 48 * 1024 * 1024

F32 = jnp.float32
BF16 = jnp.bfloat16


def whole(space=pltpu.VMEM):
    return pl.BlockSpec(memory_space=space)


def call(kernel, name, out_shape, in_specs, out_specs=None, cost=(0, 0, 0), scratch_shapes=()):
    flops, bytes_accessed, transcendentals = cost
    return pl.pallas_call(
        kernel,
        name=name,
        out_shape=out_shape,
        in_specs=in_specs,
        out_specs=jax.tree.map(lambda _: whole(), out_shape) if out_specs is None else out_specs,
        scratch_shapes=scratch_shapes,
        cost_estimate=pl.CostEstimate(
            flops=flops, bytes_accessed=bytes_accessed, transcendentals=transcendentals
        ),
        compiler_params=pltpu.CompilerParams(vmem_limit_bytes=VMEM_LIMIT),
    )


def exchange(rows, groups=None):
    return lax.all_to_all(
        rows, "clus", split_axis=0, concat_axis=0, tiled=True, axis_index_groups=groups
    )


def note_kernel(mass_hbm, table_hbm, emb_hbm, out_ref, held_ref, mass_ref, table_ref, sems):
    copies = [
        pltpu.make_async_copy(mass_hbm, mass_ref, sems.at[0]),
        pltpu.make_async_copy(table_hbm, table_ref, sems.at[1]),
        pltpu.make_async_copy(emb_hbm, held_ref, sems.at[2]),
    ]
    for copy in copies:
        copy.start()
    for copy in copies[:2]:
        copy.wait()
    targets, peers = mass_ref.shape[1], table_ref.shape[1]
    shape = (out_ref.shape[0], 1)
    out_ref[:, :, :targets] = jnp.broadcast_to(mass_ref[...][None], shape + (targets,))
    out_ref[:, :, targets:] = jnp.zeros(shape + (out_ref.shape[2] - targets,), F32)
    out_ref[:, :, targets : targets + peers] = jnp.broadcast_to(
        table_ref[...].astype(F32)[None], shape + (peers,)
    )
    copies[2].wait()


def make_note(mass, table, blocks):
    peers = table.shape[1]
    length = mass.shape[1] + -(-peers // LANES) * LANES
    return call(
        note_kernel,
        "make_note",
        (
            jax.ShapeDtypeStruct((peers, 1, length), F32),
            jax.ShapeDtypeStruct(blocks.shape, F32),
        ),
        [whole(pltpu.HBM)] * 3,
        scratch_shapes=[
            pltpu.VMEM(mass.shape, F32),
            pltpu.VMEM(table.shape, jnp.int32),
            pltpu.SemaphoreType.DMA((3,)),
        ],
    )(mass, table, blocks)


def pick_kernel(sides, place_ref, notes_ref, *refs):
    emb_refs, (out_ref, token_ref, asked_ref, held_ref, sems) = refs[:sides], refs[sides:]
    peers = out_ref.shape[0]
    count, _, width = emb_refs[0].shape
    first = notes_ref.shape[2] - -(-notes_ref.shape[0] // LANES) * LANES
    me = place_ref[0]
    side = me // peers
    tables = notes_ref[pl.ds(side * peers, peers), 0, first:]
    lane = lax.broadcasted_iota(jnp.int32, tables.shape, 1)
    for turn in range(sides):
        owner = me if turn == 0 else jnp.where(side == 0, me + peers, me - peers)
        asked = jnp.sum(jnp.where(lane == owner, tables, 0.0), axis=1, keepdims=True)
        asked_ref[turn] = jnp.broadcast_to(asked, asked_ref.shape[1:])

    def copy(d):
        return pltpu.make_async_copy(held_ref.at[d], out_ref.at[d], sems.at[d])

    def pick(d):
        for turn, emb_ref in enumerate(emb_refs):
            at = side if turn == 0 else 1 - side
            wanted = jnp.broadcast_to(asked_ref[turn, pl.ds(d, 1), :], (CB, LANES))
            for start in range(0, width, LANES):
                columns = pl.ds(start, LANES)
                block = emb_ref[0, :, columns]
                for t in range(1, count):
                    block = jnp.where(wanted == t, emb_ref[t, :, columns], block)
                held_ref[d, at, :, columns] = block
        copy(d).start()

    if peers <= 16:
        for d in range(peers):
            pick(d)
    else:
        pl.loop(0, peers)(pick)
    token_ref[...] = jnp.zeros_like(token_ref)

    @pl.loop(0, peers)
    def _(d):
        copy(d).wait()


def pick_blocks(me, notes, sources):
    sides = len(sources)
    peers = notes.shape[0] // sides
    shape = (peers, sides) + sources[0].shape[1:]
    return call(
        functools.partial(pick_kernel, sides),
        "pick_blocks",
        (jax.ShapeDtypeStruct(shape, F32), jax.ShapeDtypeStruct((8, LANES), F32)),
        [whole(pltpu.SMEM)] + [whole()] * (1 + sides),
        (whole(pl.ANY), whole()),
        scratch_shapes=[
            pltpu.VMEM((sides, peers, LANES), F32),
            pltpu.VMEM(shape, F32),
            pltpu.SemaphoreType.DMA((peers,)),
        ],
    )(me, notes, *sources)


def iota(shape, dimension):
    return lax.broadcasted_iota(jnp.int32, shape, dimension)


def slot_at(column, half, sides):
    block = column // CB
    return block % sides * half + block // sides


def product(a, b):
    return lax.dot_general(a, b, (((1,), (1,)), ((), ())), preferred_element_type=F32)


def prepare_kernel(
    sides,
    place_ref,
    notes_ref,
    table_ref,
    pools_ref,
    slots_ref,
    pool_mass_ref,
    _,
    listed_ref,
    same_ref,
    spare_ref,
    slot_mass_ref,
    mine_ref,
    own_ref,
    mass_ref,
):
    me, live = place_ref[0], place_ref[1]
    peers, columns = own_ref.shape[0], listed_ref.shape[1]
    half = peers // sides
    targets = own_ref.shape[1]
    pairs = pools_ref.shape[1]

    def hot(rows, values):
        return (rows == values).astype(F32).astype(BF16)

    column_slot = slot_at(iota((columns, 1), 0), half, sides)
    slot = slot_at(iota((1, columns), 1), half, sides)
    mine_ref[...] = (slot == me).astype(F32)
    listing = iota((1, pairs), 1) < live
    pool_hot = hot(iota((listed_ref.shape[0], pairs), 0), pools_ref[...])
    slot_hot = hot(column_slot, jnp.where(listing, slots_ref[...], -1))
    listed_ref[...] = product(pool_hot, slot_hot)

    spread = hot(column_slot, iota((columns, peers), 1))
    tables = notes_ref[:, 0, targets : targets + peers]
    table = table_ref[...].astype(F32)
    wide_tables = product(tables.astype(BF16), spread)
    wide_table = product(table.astype(BF16), spread)
    same_ref[...] = (wide_tables == wide_table).astype(F32)
    spare_ref[...] = (wide_table < 0).astype(F32)

    square = iota((peers, peers), 0), iota((peers, peers), 1)
    asked = jnp.sum(jnp.where(square[1] == me, tables, 0.0), axis=1, keepdims=True)
    block = (iota((peers, targets), 1) // CB).astype(F32)
    own_ref[...] = (asked == block).astype(F32)

    wanted = jnp.sum(jnp.where(square[0] == square[1], table, 0.0), axis=1, keepdims=True)
    masses = jnp.where(wanted == block, notes_ref[:, 0, :targets], 0.0)
    masses = fold(masses)
    slot_mass = [
        jnp.sum(
            jnp.where(
                iota((peers, LANES), 0) == slot_at(iota((peers, LANES), 1) + start, half, sides),
                masses,
                0.0,
            ),
            axis=0,
            keepdims=True,
        )
        for start in range(0, columns, LANES)
    ]
    slot_mass_ref[...] = jnp.concatenate(slot_mass, axis=1)

    diagonal = iota((LANES, LANES), 0) == iota((LANES, LANES), 1)
    for start in range(0, mass_ref.shape[0], LANES):
        row = pool_mass_ref[:, pl.ds(start, LANES)]
        mass_ref[pl.ds(start, LANES), :] = jnp.sum(
            jnp.where(diagonal, row, 0.0), axis=1, keepdims=True
        )


def prepare(place, notes, table, pools, slots, pool_mass, token, pool_count, targets, sides):
    peers = notes.shape[0]
    columns = peers * CB
    shapes = [
        (pool_count, columns),
        (peers, columns),
        (1, columns),
        (1, columns),
        (1, columns),
        (peers, targets),
        (pool_mass.shape[1], 1),
    ]
    return call(
        functools.partial(prepare_kernel, sides),
        "prepare",
        [jax.ShapeDtypeStruct(shape, F32) for shape in shapes],
        [whole(pltpu.SMEM)] + [whole()] * 6,
    )(place, notes, table, pools, slots, pool_mass, token)


def fold(rows):
    folded = rows[:, :LANES]
    for start in range(LANES, rows.shape[1], LANES):
        folded += rows[:, start : start + LANES]
    step = LANES // 2
    while step >= CB:
        folded += pltpu.roll(folded, step, 1)
        step //= 2
    return folded


def send_out(row, me, out_ref):
    out_ref[...] = jnp.where(iota(out_ref.shape, 0) == me, row, 0.0)


def halves(x):
    high = x.astype(BF16)
    return high, (x - high.astype(F32)).astype(BF16)


def assemble_kernel(scale, place_ref, pool_ref, arrived_ref, listed_ref, mass_ref, kernel_ref, out_ref):
    q_high, q_low = halves(arrived_ref[...])
    sums = jnp.zeros((1, kernel_ref.shape[1]), F32)
    rows = 256 if kernel_ref.shape[0] % 256 == 0 else RB
    for start in range(0, kernel_ref.shape[0], rows):
        high, low = halves(pool_ref[pl.ds(start, rows), :])
        scores = product(high, q_high) + (product(high, q_low) + product(low, q_high))
        for block in range(rows // RB):
            inner = pl.ds(start + block * RB, RB)
            at = start // RB + block
            listed = listed_ref[at : at + 1, :] > 0
            values = jnp.where(
                listed, jnp.exp(scores[block * RB : (block + 1) * RB] * scale), 0.0
            )
            kernel_ref[inner, :] = values
            scaling = mass_ref[inner, :] / jnp.sum(values, axis=1, keepdims=True)
            sums += jnp.sum(values * scaling, axis=0, keepdims=True)
    send_out(sums, place_ref[0], out_ref)


def assemble(place, pool, arrived, listed, mass, peers):
    rows, width = pool.shape
    columns = arrived.shape[0]
    return call(
        functools.partial(assemble_kernel, 1.5 / math.sqrt(width)),
        "assemble",
        (
            jax.ShapeDtypeStruct((rows, columns), F32),
            jax.ShapeDtypeStruct((peers, columns), F32),
        ),
        [whole(pltpu.SMEM)] + [whole()] * 4,
        cost=(
            6 * rows * columns * width,
            4 * (rows * width + columns * width + rows * columns),
            rows * columns,
        ),
    )(place, pool, arrived, listed, mass)


def iterate_kernel(
    place_ref, kernel_ref, notes_ref, same_ref, slot_mass_ref, spare_ref, mass_ref, out_ref, *scaling_refs
):
    col_sums = jnp.sum(notes_ref[...] * same_ref[...], axis=0, keepdims=True)
    target_scaling = slot_mass_ref[...] / (col_sums + spare_ref[...])
    sums = jnp.zeros_like(target_scaling)
    diagonal = lax.broadcasted_iota(jnp.int32, (LANES, LANES), 0) == lax.broadcasted_iota(
        jnp.int32, (LANES, LANES), 1
    )
    for start in range(0, kernel_ref.shape[0], LANES):
        inner = pl.ds(start, LANES)
        values = kernel_ref[inner, :]
        scaling = mass_ref[inner, :] / jnp.sum(values * target_scaling, axis=1, keepdims=True)
        sums += jnp.sum(values * scaling, axis=0, keepdims=True)
        for scaling_ref in scaling_refs:
            scaling_ref[:, inner] = jnp.sum(
                jnp.where(diagonal, scaling, 0.0), axis=0, keepdims=True
            )
    send_out(sums, place_ref[0], out_ref)


def iterate(place, kernel, notes, same, slot_mass, spare, mass, last):
    rows, columns = kernel.shape
    out_shape = [jax.ShapeDtypeStruct(notes.shape, F32)]
    if last:
        out_shape.append(jax.ShapeDtypeStruct((1, rows), F32))
    return call(
        iterate_kernel,
        "iterate",
        out_shape,
        [whole(pltpu.SMEM)] + [whole()] * 6,
        cost=(4 * rows * columns, 4 * rows * columns, 0),
    )(place, kernel, notes, same, slot_mass, spare, mass)


def finish_kernel(
    notes_ref,
    mine_ref,
    own_ref,
    mass_ref,
    scaling_ref,
    pool_hbm,
    target_hbm,
    pool_ref,
    target_ref,
    sems,
):
    pool_ref[...] = jnp.log(scaling_ref[0])
    pool_copy = pltpu.make_async_copy(pool_ref, pool_hbm, sems.at[0])
    pool_copy.start()
    col_sums = jnp.sum(fold(notes_ref[...] * mine_ref[...]) * own_ref[...], axis=0)
    target_ref[...] = jnp.log(mass_ref[...] / col_sums)
    target_copy = pltpu.make_async_copy(target_ref, target_hbm, sems.at[1])
    target_copy.start()
    pool_copy.wait()
    target_copy.wait()


def finish(notes, mine, own, mass, scaling):
    shapes = (scaling.shape[1:], mass.shape)
    return call(
        finish_kernel,
        "finish",
        tuple(jax.ShapeDtypeStruct(shape, F32) for shape in shapes),
        [whole()] * 5,
        (whole(pl.ANY),) * 2,
        scratch_shapes=[pltpu.VMEM(shape, F32) for shape in shapes]
        + [pltpu.SemaphoreType.DMA((2,))],
    )(notes, mine, own, mass, scaling)


def local(
    pool_emb,
    target_emb,
    pool_mass,
    target_mass,
    fetch_table,
    pair_pool,
    listed_pair_slot,
    pair_count,
):
    peers = lax.axis_size("clus")
    me = lax.axis_index("clus").astype(jnp.int32)
    targets, width = target_emb.shape
    pool_count = pool_emb.shape[0] // RB
    columns = peers * CB
    sides = SIDES if peers % SIDES == 0 else 1
    half = peers // sides

    blocks = target_emb.reshape(targets // CB, CB, width)
    sources = []
    if sides == 2:
        sources = [lax.ppermute(blocks, "clus", [(i, (i + half) % peers) for i in range(peers)])]
    note, held = make_note(target_mass[None], fetch_table, blocks)
    notes = lax.cond(me < peers, exchange, jnp.zeros_like, note)
    outgoing, token = pick_blocks(me[None], notes, [held] + sources)
    groups = [list(range(side * half, side * half + half)) for side in range(sides)]
    arrived = exchange(outgoing, groups).reshape(columns, width)
    place = jnp.concatenate([me[None], pair_count])
    listed, same, spare, slot_mass, mine, own, mass = prepare(
        place,
        notes,
        fetch_table,
        pair_pool,
        listed_pair_slot,
        pool_mass[None],
        token,
        pool_count,
        targets,
        sides,
    )

    kernel, sums = assemble(place, pool_emb, arrived, listed, mass, peers)
    for step in range(1, ITERS):
        sums, *scalings = iterate(
            place, kernel, lax.pmax(sums, "clus"), same, slot_mass, spare, mass, step == ITERS - 1
        )
    return finish(lax.pmax(sums, "clus"), mine, own, target_mass, scalings[0])


def solution(mesh):
    return jax.shard_map(
        local,
        mesh=mesh,
        in_specs=(
            P(("groups", "clus"), None),
            P(("groups", "clus"), None),
            P(("groups", "clus")),
            P(("groups", "clus")),
            P(("groups", "clus"), None),
            P(("groups", "clus"), None),
            P(("groups", "clus"), None),
            P(("groups", "clus")),
        ),
        out_specs=(P(("groups", "clus")), P(("groups", "clus"))),
        check_vma=False,
    )
```

```python
import functools
import math

import jax
import jax.numpy as jnp
from jax import lax
from jax.experimental import pallas as pl
from jax.experimental.pallas import tpu as pltpu
from jax.sharding import PartitionSpec as P

RB = 64
CB = 16
ITERS = 3
SIDES = 2
LANES = 128
VMEM_LIMIT = 48 * 1024 * 1024

F32 = jnp.float32
BF16 = jnp.bfloat16


def whole(space=pltpu.VMEM):
    return pl.BlockSpec(memory_space=space)


def call(kernel, name, out_shape, in_specs, out_specs=None, cost=(0, 0, 0), scratch_shapes=()):
    flops, bytes_accessed, transcendentals = cost
    return pl.pallas_call(
        kernel,
        name=name,
        out_shape=out_shape,
        in_specs=in_specs,
        out_specs=jax.tree.map(lambda _: whole(), out_shape) if out_specs is None else out_specs,
        scratch_shapes=scratch_shapes,
        cost_estimate=pl.CostEstimate(
            flops=flops, bytes_accessed=bytes_accessed, transcendentals=transcendentals
        ),
        compiler_params=pltpu.CompilerParams(vmem_limit_bytes=VMEM_LIMIT),
    )


def exchange(rows, groups=None):
    return lax.all_to_all(
        rows, "clus", split_axis=0, concat_axis=0, tiled=True, axis_index_groups=groups
    )


def note_kernel(mass_hbm, table_hbm, emb_hbm, out_ref, held_ref, mass_ref, table_ref, sems):
    copies = [
        pltpu.make_async_copy(mass_hbm, mass_ref, sems.at[0]),
        pltpu.make_async_copy(table_hbm, table_ref, sems.at[1]),
        pltpu.make_async_copy(emb_hbm, held_ref, sems.at[2]),
    ]
    for copy in copies:
        copy.start()
    for copy in copies[:2]:
        copy.wait()
    targets, peers = mass_ref.shape[1], table_ref.shape[1]
    shape = (out_ref.shape[0], 1)
    out_ref[:, :, :targets] = jnp.broadcast_to(mass_ref[...][None], shape + (targets,))
    out_ref[:, :, targets:] = jnp.zeros(shape + (out_ref.shape[2] - targets,), F32)
    out_ref[:, :, targets : targets + peers] = jnp.broadcast_to(
        table_ref[...].astype(F32)[None], shape + (peers,)
    )
    copies[2].wait()


def make_note(mass, table, blocks, readers):
    length = mass.shape[1] + -(-table.shape[1] // LANES) * LANES
    return call(
        note_kernel,
        "make_note",
        (
            jax.ShapeDtypeStruct((readers, 1, length), F32),
            jax.ShapeDtypeStruct(blocks.shape, F32),
        ),
        [whole(pltpu.HBM)] * 3,
        scratch_shapes=[
            pltpu.VMEM(mass.shape, F32),
            pltpu.VMEM(table.shape, jnp.int32),
            pltpu.SemaphoreType.DMA((3,)),
        ],
    )(mass, table, blocks)


def pick_kernel(sides, place_ref, notes_ref, *refs):
    emb_refs, (out_ref, read_ref, asked_ref, held_ref, sems) = refs[:sides], refs[sides:]
    peers = out_ref.shape[0]
    count, _, width = emb_refs[0].shape
    first = notes_ref.shape[2] - -(-peers * sides // LANES) * LANES
    me = place_ref[0]
    side = me // peers
    tables = notes_ref[:, 0, first:]
    lane = lax.broadcasted_iota(jnp.int32, tables.shape, 1)
    for turn in range(sides):
        owner = me if turn == 0 else jnp.where(side == 0, me + peers, me - peers)
        asked = jnp.sum(jnp.where(lane == owner, tables, 0.0), axis=1, keepdims=True)
        asked_ref[turn] = jnp.broadcast_to(asked, asked_ref.shape[1:])

    def copy(d):
        return pltpu.make_async_copy(held_ref.at[d], out_ref.at[d], sems.at[d])

    def pick(d):
        for turn, emb_ref in enumerate(emb_refs):
            at = side if turn == 0 else 1 - side
            wanted = jnp.broadcast_to(asked_ref[turn, pl.ds(d, 1), :], (CB, LANES))
            for start in range(0, width, LANES):
                columns = pl.ds(start, LANES)
                block = emb_ref[0, :, columns]
                for t in range(1, count):
                    block = jnp.where(wanted == t, emb_ref[t, :, columns], block)
                held_ref[d, at, :, columns] = block
        copy(d).start()

    if peers <= 16:
        for d in range(peers):
            pick(d)
    else:
        pl.loop(0, peers)(pick)
    read_ref[...] = notes_ref[...]

    @pl.loop(0, peers)
    def _(d):
        copy(d).wait()


def pick_blocks(me, notes, sources):
    sides = len(sources)
    peers = notes.shape[0]
    shape = (peers, sides) + sources[0].shape[1:]
    return call(
        functools.partial(pick_kernel, sides),
        "pick_blocks",
        (jax.ShapeDtypeStruct(shape, F32), jax.ShapeDtypeStruct(notes.shape, F32)),
        [whole(pltpu.SMEM)] + [whole()] * (1 + sides),
        (whole(pl.ANY), whole()),
        scratch_shapes=[
            pltpu.VMEM((sides, peers, LANES), F32),
            pltpu.VMEM(shape, F32),
            pltpu.SemaphoreType.DMA((peers,)),
        ],
    )(me, notes, *sources)


def iota(shape, dimension):
    return lax.broadcasted_iota(jnp.int32, shape, dimension)


def slot_at(column, half, sides):
    block = column // CB
    return block % sides * half + block // sides


def product(a, b):
    return lax.dot_general(a, b, (((1,), (1,)), ((), ())), preferred_element_type=F32)


def prepare_kernel(sides, place_ref, table_ref, pools_ref, slots_ref, pool_mass_ref, *refs):
    notes_refs, refs = refs[:sides], refs[sides:]
    listed_ref, same_ref, spare_ref, slot_mass_ref, mine_ref, own_ref, mass_ref = refs
    me, live = place_ref[0], place_ref[1]
    peers, columns = own_ref.shape[0], listed_ref.shape[1]
    half = peers // sides
    notes = notes_refs[0][:, 0, :]
    if sides == 2:
        other = notes_refs[1][:, 0, :]
        lower = me < half
        notes = jnp.concatenate(
            [jnp.where(lower, notes, other), jnp.where(lower, other, notes)], axis=0
        )
    targets = own_ref.shape[1]
    pairs = pools_ref.shape[1]

    def hot(rows, values):
        return (rows == values).astype(F32).astype(BF16)

    column_slot = slot_at(iota((columns, 1), 0), half, sides)
    slot = slot_at(iota((1, columns), 1), half, sides)
    mine_ref[...] = (slot == me).astype(F32)
    listing = iota((1, pairs), 1) < live
    pool_hot = hot(iota((listed_ref.shape[0], pairs), 0), pools_ref[...])
    slot_hot = hot(column_slot, jnp.where(listing, slots_ref[...], -1))
    listed_ref[...] = product(pool_hot, slot_hot)

    spread = hot(column_slot, iota((columns, peers), 1))
    tables = notes[:, targets : targets + peers]
    table = table_ref[...].astype(F32)
    wide_tables = product(tables.astype(BF16), spread)
    wide_table = product(table.astype(BF16), spread)
    same_ref[...] = (wide_tables == wide_table).astype(F32)
    spare_ref[...] = (wide_table < 0).astype(F32)

    square = iota((peers, peers), 0), iota((peers, peers), 1)
    asked = jnp.sum(jnp.where(square[1] == me, tables, 0.0), axis=1, keepdims=True)
    block = (iota((peers, targets), 1) // CB).astype(F32)
    own_ref[...] = (asked == block).astype(F32)

    wanted = jnp.sum(jnp.where(square[0] == square[1], table, 0.0), axis=1, keepdims=True)
    masses = jnp.where(wanted == block, notes[:, :targets], 0.0)
    masses = fold(masses)
    slot_mass = [
        jnp.sum(
            jnp.where(
                iota((peers, LANES), 0) == slot_at(iota((peers, LANES), 1) + start, half, sides),
                masses,
                0.0,
            ),
            axis=0,
            keepdims=True,
        )
        for start in range(0, columns, LANES)
    ]
    slot_mass_ref[...] = jnp.concatenate(slot_mass, axis=1)

    diagonal = iota((LANES, LANES), 0) == iota((LANES, LANES), 1)
    for start in range(0, mass_ref.shape[0], LANES):
        row = pool_mass_ref[:, pl.ds(start, LANES)]
        mass_ref[pl.ds(start, LANES), :] = jnp.sum(
            jnp.where(diagonal, row, 0.0), axis=1, keepdims=True
        )


def prepare(place, table, pools, slots, pool_mass, notes, pool_count, targets):
    peers = table.shape[1]
    columns = peers * CB
    shapes = [
        (pool_count, columns),
        (peers, columns),
        (1, columns),
        (1, columns),
        (1, columns),
        (peers, targets),
        (pool_mass.shape[1], 1),
    ]
    return call(
        functools.partial(prepare_kernel, len(notes)),
        "prepare",
        [jax.ShapeDtypeStruct(shape, F32) for shape in shapes],
        [whole(pltpu.SMEM)] + [whole()] * (4 + len(notes)),
    )(place, table, pools, slots, pool_mass, *notes)


def fold(rows):
    folded = rows[:, :LANES]
    for start in range(LANES, rows.shape[1], LANES):
        folded += rows[:, start : start + LANES]
    step = LANES // 2
    while step >= CB:
        folded += pltpu.roll(folded, step, 1)
        step //= 2
    return folded


def send_out(row, out_ref):
    out_ref[...] = jnp.broadcast_to(row[None], out_ref.shape)


def halves(x):
    high = x.astype(BF16)
    return high, (x - high.astype(F32)).astype(BF16)


def assemble_kernel(scale, pool_ref, arrived_ref, listed_ref, mass_ref, kernel_ref, out_ref):
    q_high, q_low = halves(arrived_ref[...])
    sums = jnp.zeros((1, kernel_ref.shape[1]), F32)
    rows = 256 if kernel_ref.shape[0] % 256 == 0 else RB
    for start in range(0, kernel_ref.shape[0], rows):
        high, low = halves(pool_ref[pl.ds(start, rows), :])
        scores = product(high, q_high) + (product(high, q_low) + product(low, q_high))
        for block in range(rows // RB):
            inner = pl.ds(start + block * RB, RB)
            at = start // RB + block
            listed = listed_ref[at : at + 1, :] > 0
            values = jnp.where(
                listed, jnp.exp(scores[block * RB : (block + 1) * RB] * scale), 0.0
            )
            kernel_ref[inner, :] = values
            scaling = mass_ref[inner, :] / jnp.sum(values, axis=1, keepdims=True)
            sums += jnp.sum(values * scaling, axis=0, keepdims=True)
    send_out(sums, out_ref)


def assemble(pool, arrived, listed, mass, peers):
    rows, width = pool.shape
    columns = arrived.shape[0]
    return call(
        functools.partial(assemble_kernel, 1.5 / math.sqrt(width)),
        "assemble",
        (
            jax.ShapeDtypeStruct((rows, columns), F32),
            jax.ShapeDtypeStruct((peers, 1, columns), F32),
        ),
        [whole()] * 4,
        cost=(
            6 * rows * columns * width,
            4 * (rows * width + columns * width + rows * columns),
            rows * columns,
        ),
    )(pool, arrived, listed, mass)


def iterate_kernel(
    kernel_ref, notes_ref, same_ref, slot_mass_ref, spare_ref, mass_ref, out_ref, *scaling_refs
):
    col_sums = jnp.sum(notes_ref[:, 0, :] * same_ref[...], axis=0, keepdims=True)
    target_scaling = slot_mass_ref[...] / (col_sums + spare_ref[...])
    sums = jnp.zeros_like(target_scaling)
    diagonal = lax.broadcasted_iota(jnp.int32, (LANES, LANES), 0) == lax.broadcasted_iota(
        jnp.int32, (LANES, LANES), 1
    )
    for start in range(0, kernel_ref.shape[0], LANES):
        inner = pl.ds(start, LANES)
        values = kernel_ref[inner, :]
        scaling = mass_ref[inner, :] / jnp.sum(values * target_scaling, axis=1, keepdims=True)
        sums += jnp.sum(values * scaling, axis=0, keepdims=True)
        for scaling_ref in scaling_refs:
            scaling_ref[:, inner] = jnp.sum(
                jnp.where(diagonal, scaling, 0.0), axis=0, keepdims=True
            )
    send_out(sums, out_ref)


def iterate(kernel, notes, same, slot_mass, spare, mass, last):
    rows, columns = kernel.shape
    out_shape = [jax.ShapeDtypeStruct(notes.shape, F32)]
    if last:
        out_shape.append(jax.ShapeDtypeStruct((1, rows), F32))
    return call(
        iterate_kernel,
        "iterate",
        out_shape,
        [whole()] * 6,
        cost=(4 * rows * columns, 4 * rows * columns, 0),
    )(kernel, notes, same, slot_mass, spare, mass)


def finish_kernel(
    notes_ref,
    mine_ref,
    own_ref,
    mass_ref,
    scaling_ref,
    pool_hbm,
    target_hbm,
    pool_ref,
    target_ref,
    sems,
):
    pool_ref[...] = jnp.log(scaling_ref[0])
    pool_copy = pltpu.make_async_copy(pool_ref, pool_hbm, sems.at[0])
    pool_copy.start()
    col_sums = jnp.sum(fold(notes_ref[:, 0, :] * mine_ref[...]) * own_ref[...], axis=0)
    target_ref[...] = jnp.log(mass_ref[...] / col_sums)
    target_copy = pltpu.make_async_copy(target_ref, target_hbm, sems.at[1])
    target_copy.start()
    pool_copy.wait()
    target_copy.wait()


def finish(notes, mine, own, mass, scaling):
    shapes = (scaling.shape[1:], mass.shape)
    return call(
        finish_kernel,
        "finish",
        tuple(jax.ShapeDtypeStruct(shape, F32) for shape in shapes),
        [whole()] * 5,
        (whole(pl.ANY),) * 2,
        scratch_shapes=[pltpu.VMEM(shape, F32) for shape in shapes]
        + [pltpu.SemaphoreType.DMA((2,))],
    )(notes, mine, own, mass, scaling)


def local(
    pool_emb,
    target_emb,
    pool_mass,
    target_mass,
    fetch_table,
    pair_pool,
    listed_pair_slot,
    pair_count,
):
    peers = lax.axis_size("clus")
    me = lax.axis_index("clus").astype(jnp.int32)
    targets, width = target_emb.shape
    pool_count = pool_emb.shape[0] // RB
    columns = peers * CB
    sides = SIDES if peers % SIDES == 0 else 1
    half = peers // sides

    blocks = target_emb.reshape(targets // CB, CB, width)
    groups = [list(range(side * half, side * half + half)) for side in range(sides)]

    def partner(x):
        return lax.ppermute(x, "clus", [(i, (i + half) % peers) for i in range(peers)])

    sources = [partner(blocks)] if sides == 2 else []
    note, held = make_note(target_mass[None], fetch_table, blocks, half)
    notes = lax.cond(me < peers, lambda rows: exchange(rows, groups), jnp.zeros_like, note)
    outgoing, notes = pick_blocks(me[None], notes, [held] + sources)
    arrived = exchange(outgoing, groups).reshape(columns, width)
    listed, same, spare, slot_mass, mine, own, mass = prepare(
        jnp.concatenate([me[None], pair_count]),
        fetch_table,
        pair_pool,
        listed_pair_slot,
        pool_mass[None],
        [notes] + ([partner(notes)] if sides == 2 else []),
        pool_count,
        targets,
    )

    kernel, sums = assemble(pool_emb, arrived, listed, mass, peers)
    for step in range(1, ITERS):
        sums, *scalings = iterate(
            kernel, exchange(sums), same, slot_mass, spare, mass, step == ITERS - 1
        )
    return finish(exchange(sums), mine, own, target_mass, scalings[0])


def solution(mesh):
    return jax.shard_map(
        local,
        mesh=mesh,
        in_specs=(
            P(("groups", "clus"), None),
            P(("groups", "clus"), None),
            P(("groups", "clus")),
            P(("groups", "clus")),
            P(("groups", "clus"), None),
            P(("groups", "clus"), None),
            P(("groups", "clus"), None),
            P(("groups", "clus")),
        ),
        out_specs=(P(("groups", "clus")), P(("groups", "clus"))),
        check_vma=False,
    )
```

```python
import functools
import math

import jax
import jax.numpy as jnp
from jax import lax
from jax.experimental import pallas as pl
from jax.experimental.pallas import tpu as pltpu
from jax.sharding import PartitionSpec as P

RB = 64
CB = 16
ITERS = 3
SIDES = 2
LANES = 128
VMEM_LIMIT = 48 * 1024 * 1024

F32 = jnp.float32
BF16 = jnp.bfloat16


def whole(space=pltpu.VMEM):
    return pl.BlockSpec(memory_space=space)


def call(kernel, name, out_shape, in_specs, out_specs=None, cost=(0, 0, 0), scratch_shapes=()):
    flops, bytes_accessed, transcendentals = cost
    return pl.pallas_call(
        kernel,
        name=name,
        out_shape=out_shape,
        in_specs=in_specs,
        out_specs=jax.tree.map(lambda _: whole(), out_shape) if out_specs is None else out_specs,
        scratch_shapes=scratch_shapes,
        cost_estimate=pl.CostEstimate(
            flops=flops, bytes_accessed=bytes_accessed, transcendentals=transcendentals
        ),
        compiler_params=pltpu.CompilerParams(vmem_limit_bytes=VMEM_LIMIT),
    )


def exchange(rows, groups=None):
    return lax.all_to_all(
        rows, "clus", split_axis=0, concat_axis=0, tiled=True, axis_index_groups=groups
    )


def note_kernel(mass_hbm, table_hbm, emb_hbm, out_ref, held_ref, mass_ref, table_ref, sems):
    copies = [
        pltpu.make_async_copy(mass_hbm, mass_ref, sems.at[0]),
        pltpu.make_async_copy(table_hbm, table_ref, sems.at[1]),
        pltpu.make_async_copy(emb_hbm, held_ref, sems.at[2]),
    ]
    for copy in copies:
        copy.start()
    for copy in copies[:2]:
        copy.wait()
    targets, peers = mass_ref.shape[1], table_ref.shape[1]
    shape = (out_ref.shape[0], 1)
    out_ref[:, :, :targets] = jnp.broadcast_to(mass_ref[...][None], shape + (targets,))
    out_ref[:, :, targets:] = jnp.zeros(shape + (out_ref.shape[2] - targets,), F32)
    out_ref[:, :, targets : targets + peers] = jnp.broadcast_to(
        table_ref[...].astype(F32)[None], shape + (peers,)
    )
    copies[2].wait()


def make_note(mass, table, blocks, readers):
    length = mass.shape[1] + -(-table.shape[1] // LANES) * LANES
    return call(
        note_kernel,
        "make_note",
        (
            jax.ShapeDtypeStruct((readers, 1, length), F32),
            jax.ShapeDtypeStruct(blocks.shape, F32),
        ),
        [whole(pltpu.HBM)] * 3,
        scratch_shapes=[
            pltpu.VMEM(mass.shape, F32),
            pltpu.VMEM(table.shape, jnp.int32),
            pltpu.SemaphoreType.DMA((3,)),
        ],
    )(mass, table, blocks)


def pick_kernel(sides, place_ref, notes_ref, *refs):
    emb_refs, (out_ref, read_ref, asked_ref, held_ref, sems) = refs[:sides], refs[sides:]
    peers = out_ref.shape[0]
    count, _, width = emb_refs[0].shape
    first = notes_ref.shape[2] - -(-peers * sides // LANES) * LANES
    me = place_ref[0]
    side = me // peers
    tables = notes_ref[:, 0, first:]
    lane = lax.broadcasted_iota(jnp.int32, tables.shape, 1)
    for turn in range(sides):
        owner = me if turn == 0 else jnp.where(side == 0, me + peers, me - peers)
        asked = jnp.sum(jnp.where(lane == owner, tables, 0.0), axis=1, keepdims=True)
        asked_ref[turn] = jnp.broadcast_to(asked, asked_ref.shape[1:])

    def copy(d):
        return pltpu.make_async_copy(held_ref.at[d], out_ref.at[d], sems.at[d])

    def pick(d):
        for turn, emb_ref in enumerate(emb_refs):
            at = side if turn == 0 else 1 - side
            wanted = jnp.broadcast_to(asked_ref[turn, pl.ds(d, 1), :], (CB, LANES))
            for start in range(0, width, LANES):
                columns = pl.ds(start, LANES)
                block = emb_ref[0, :, columns]
                for t in range(1, count):
                    block = jnp.where(wanted == t, emb_ref[t, :, columns], block)
                held_ref[d, at, :, columns] = block
        copy(d).start()

    if peers <= 16:
        for d in range(peers):
            pick(d)
    else:
        pl.loop(0, peers)(pick)
    read_ref[...] = notes_ref[...]

    @pl.loop(0, peers)
    def _(d):
        copy(d).wait()


def pick_blocks(me, notes, sources):
    sides = len(sources)
    peers = notes.shape[0]
    shape = (peers, sides) + sources[0].shape[1:]
    return call(
        functools.partial(pick_kernel, sides),
        "pick_blocks",
        (jax.ShapeDtypeStruct(shape, F32), jax.ShapeDtypeStruct(notes.shape, F32)),
        [whole(pltpu.SMEM)] + [whole()] * (1 + sides),
        (whole(pl.ANY), whole()),
        scratch_shapes=[
            pltpu.VMEM((sides, peers, LANES), F32),
            pltpu.VMEM(shape, F32),
            pltpu.SemaphoreType.DMA((peers,)),
        ],
    )(me, notes, *sources)


def iota(shape, dimension):
    return lax.broadcasted_iota(jnp.int32, shape, dimension)


def slot_at(column, half, sides):
    block = column // CB
    return block % sides * half + block // sides


def product(a, b):
    return lax.dot_general(a, b, (((1,), (1,)), ((), ())), preferred_element_type=F32)


def prepare_kernel(
    sides, place_ref, pools_ref, slots_ref, pool_mass_ref, _, listed_ref, mine_ref, mass_ref
):
    me, live = place_ref[0], place_ref[1]
    columns = listed_ref.shape[1]
    half = columns // CB // sides
    pairs = pools_ref.shape[1]
    slot = slot_at(iota((1, columns), 1), half, sides)
    mine_ref[...] = (slot == me).astype(F32)
    listing = iota((1, pairs), 1) < live
    pool_hot = hot(iota((listed_ref.shape[0], pairs), 0), pools_ref[...])
    slot_hot = hot(
        slot_at(iota((columns, 1), 0), half, sides), jnp.where(listing, slots_ref[...], -1)
    )
    listed_ref[...] = product(pool_hot, slot_hot)
    diagonal = iota((LANES, LANES), 0) == iota((LANES, LANES), 1)
    for start in range(0, mass_ref.shape[0], LANES):
        row = pool_mass_ref[:, pl.ds(start, LANES)]
        mass_ref[pl.ds(start, LANES), :] = jnp.sum(
            jnp.where(diagonal, row, 0.0), axis=1, keepdims=True
        )


def prepare(place, pools, slots, pool_mass, after, pool_count, columns, sides):
    shapes = [(pool_count, columns), (1, columns), (pool_mass.shape[1], 1)]
    return call(
        functools.partial(prepare_kernel, sides),
        "prepare",
        [jax.ShapeDtypeStruct(shape, F32) for shape in shapes],
        [whole(pltpu.SMEM)] + [whole()] * 4,
    )(place, pools, slots, pool_mass, after)


def hot(rows, values):
    return (rows == values).astype(F32).astype(BF16)


def relate(sides, me, table, notes, columns):
    peers = table.shape[1]
    half = peers // sides
    if sides == 2:
        lower = me < half
        notes = jnp.concatenate(
            [jnp.where(lower, notes[0], notes[1]), jnp.where(lower, notes[1], notes[0])], axis=0
        )
    else:
        notes = notes[0]
    targets = notes.shape[1] - -(-peers // LANES) * LANES
    tables = notes[:, targets : targets + peers]
    table = table.astype(F32)
    spread = hot(slot_at(iota((columns, 1), 0), half, sides), iota((columns, peers), 1))
    wide_tables = product(tables.astype(BF16), spread)
    wide_table = product(table.astype(BF16), spread)
    same = (wide_tables == wide_table).astype(F32)
    spare = (wide_table < 0).astype(F32)

    row, column = iota((peers, peers), 0), iota((peers, peers), 1)
    asked = jnp.sum(jnp.where(column == me, tables, 0.0), axis=1, keepdims=True)
    block = (iota((peers, targets), 1) // CB).astype(F32)
    own = (asked == block).astype(F32)

    wanted = jnp.sum(jnp.where(row == column, table, 0.0), axis=1, keepdims=True)
    masses = fold(jnp.where(wanted == block, notes[:, :targets], 0.0))
    row = iota((peers, LANES), 0)
    slot_mass = [
        jnp.sum(
            jnp.where(
                row == slot_at(iota((peers, LANES), 1) + start, half, sides), masses, 0.0
            ),
            axis=0,
            keepdims=True,
        )
        for start in range(0, columns, LANES)
    ]
    return same, spare, jnp.concatenate(slot_mass, axis=1), own


def fold(rows):
    folded = rows[:, :LANES]
    for start in range(LANES, rows.shape[1], LANES):
        folded += rows[:, start : start + LANES]
    step = LANES // 2
    while step >= CB:
        folded += pltpu.roll(folded, step, 1)
        step //= 2
    return folded


def send_out(row, out_ref):
    out_ref[...] = jnp.broadcast_to(row[None], out_ref.shape)


def halves(x):
    high = x.astype(BF16)
    return high, (x - high.astype(F32)).astype(BF16)


def assemble_kernel(scale, pool_ref, arrived_ref, listed_ref, mass_ref, kernel_ref, out_ref):
    q_high, q_low = halves(arrived_ref[...])
    sums = jnp.zeros((1, kernel_ref.shape[1]), F32)
    rows = 256 if kernel_ref.shape[0] % 256 == 0 else RB
    for start in range(0, kernel_ref.shape[0], rows):
        high, low = halves(pool_ref[pl.ds(start, rows), :])
        scores = product(high, q_high) + (product(high, q_low) + product(low, q_high))
        for block in range(rows // RB):
            inner = pl.ds(start + block * RB, RB)
            at = start // RB + block
            listed = listed_ref[at : at + 1, :] > 0
            values = jnp.where(
                listed, jnp.exp(scores[block * RB : (block + 1) * RB] * scale), 0.0
            )
            kernel_ref[inner, :] = values
            scaling = mass_ref[inner, :] / jnp.sum(values, axis=1, keepdims=True)
            sums += jnp.sum(values * scaling, axis=0, keepdims=True)
    send_out(sums, out_ref)


def assemble(pool, arrived, listed, mass, peers):
    rows, width = pool.shape
    columns = arrived.shape[0]
    return call(
        functools.partial(assemble_kernel, 1.5 / math.sqrt(width)),
        "assemble",
        (
            jax.ShapeDtypeStruct((rows, columns), F32),
            jax.ShapeDtypeStruct((peers, 1, columns), F32),
        ),
        [whole()] * 4,
        cost=(
            6 * rows * columns * width,
            4 * (rows * width + columns * width + rows * columns),
            rows * columns,
        ),
    )(pool, arrived, listed, mass)


def iteration(kernel_ref, notes_ref, same, spare, slot_mass, mass_ref, out_ref, scaling_ref=None):
    col_sums = jnp.sum(notes_ref[:, 0, :] * same, axis=0, keepdims=True)
    target_scaling = slot_mass / (col_sums + spare)
    sums = jnp.zeros_like(target_scaling)
    diagonal = iota((LANES, LANES), 0) == iota((LANES, LANES), 1)
    for start in range(0, kernel_ref.shape[0], LANES):
        inner = pl.ds(start, LANES)
        values = kernel_ref[inner, :]
        scaling = mass_ref[inner, :] / jnp.sum(values * target_scaling, axis=1, keepdims=True)
        sums += jnp.sum(values * scaling, axis=0, keepdims=True)
        if scaling_ref is not None:
            scaling_ref[:, inner] = jnp.sum(
                jnp.where(diagonal, scaling, 0.0), axis=0, keepdims=True
            )
    send_out(sums, out_ref)


def first_kernel(sides, place_ref, kernel_ref, notes_ref, mass_ref, table_ref, *refs):
    peer_refs, (out_ref, *related_refs) = refs[:sides], refs[sides:]
    related = relate(
        sides,
        place_ref[0],
        table_ref[...],
        [ref[:, 0, :] for ref in peer_refs],
        kernel_ref.shape[1],
    )
    for ref, value in zip(related_refs, related):
        ref[...] = value
    iteration(kernel_ref, notes_ref, *related[:3], mass_ref, out_ref)


def first_iteration(place, kernel, notes, mass, table, peer_notes, targets):
    peers, columns = notes.shape[0], kernel.shape[1]
    shapes = [notes.shape, (peers, columns), (1, columns), (1, columns), (peers, targets)]
    return call(
        functools.partial(first_kernel, len(peer_notes)),
        "first_iteration",
        [jax.ShapeDtypeStruct(shape, F32) for shape in shapes],
        [whole(pltpu.SMEM)] + [whole()] * (4 + len(peer_notes)),
        cost=(4 * kernel.size, 4 * kernel.size, 0),
    )(place, kernel, notes, mass, table, *peer_notes)


def later_kernel(kernel_ref, notes_ref, same_ref, spare_ref, slot_mass_ref, *refs):
    iteration(kernel_ref, notes_ref, same_ref[...], spare_ref[...], slot_mass_ref[...], *refs)


def later_iteration(kernel, notes, same, spare, slot_mass, mass, last):
    shapes = [notes.shape] + [(1, kernel.shape[0])] * last
    return call(
        later_kernel,
        "later_iteration",
        [jax.ShapeDtypeStruct(shape, F32) for shape in shapes],
        [whole()] * 6,
        cost=(4 * kernel.size, 4 * kernel.size, 0),
    )(kernel, notes, same, spare, slot_mass, mass)


def finish_kernel(
    notes_ref,
    mine_ref,
    own_ref,
    mass_ref,
    scaling_ref,
    pool_hbm,
    target_hbm,
    pool_ref,
    target_ref,
    sems,
):
    pool_ref[...] = jnp.log(scaling_ref[0])
    pool_copy = pltpu.make_async_copy(pool_ref, pool_hbm, sems.at[0])
    pool_copy.start()
    col_sums = jnp.sum(fold(notes_ref[:, 0, :] * mine_ref[...]) * own_ref[...], axis=0)
    target_ref[...] = jnp.log(mass_ref[...] / col_sums)
    target_copy = pltpu.make_async_copy(target_ref, target_hbm, sems.at[1])
    target_copy.start()
    pool_copy.wait()
    target_copy.wait()


def finish(notes, mine, own, mass, scaling):
    shapes = (scaling.shape[1:], mass.shape)
    return call(
        finish_kernel,
        "finish",
        tuple(jax.ShapeDtypeStruct(shape, F32) for shape in shapes),
        [whole()] * 5,
        (whole(pl.ANY),) * 2,
        scratch_shapes=[pltpu.VMEM(shape, F32) for shape in shapes]
        + [pltpu.SemaphoreType.DMA((2,))],
    )(notes, mine, own, mass, scaling)


def local(
    pool_emb,
    target_emb,
    pool_mass,
    target_mass,
    fetch_table,
    pair_pool,
    listed_pair_slot,
    pair_count,
):
    peers = lax.axis_size("clus")
    me = lax.axis_index("clus").astype(jnp.int32)
    targets, width = target_emb.shape
    pool_count = pool_emb.shape[0] // RB
    columns = peers * CB
    sides = SIDES if peers % SIDES == 0 else 1
    half = peers // sides

    blocks = target_emb.reshape(targets // CB, CB, width)
    groups = [list(range(side * half, side * half + half)) for side in range(sides)]

    def partner(x):
        return lax.ppermute(x, "clus", [(i, (i + half) % peers) for i in range(peers)])

    sources = [partner(blocks)] if sides == 2 else []
    note, held = make_note(target_mass[None], fetch_table, blocks, half)
    notes = lax.cond(me < peers, lambda rows: exchange(rows, groups), jnp.zeros_like, note)
    outgoing, notes = pick_blocks(me[None], notes, [held] + sources)
    arrived = exchange(outgoing, groups).reshape(columns, width)
    peer_notes = [notes] + ([partner(notes)] if sides == 2 else [])
    place = jnp.concatenate([me[None], pair_count])
    listed, mine, mass = prepare(
        place,
        pair_pool,
        listed_pair_slot,
        pool_mass[None],
        notes,
        pool_count,
        columns,
        sides,
    )

    kernel, sums = assemble(pool_emb, arrived, listed, mass, peers)
    sums, *related, own = first_iteration(
        place, kernel, exchange(sums), mass, fetch_table, peer_notes, targets
    )
    for step in range(2, ITERS):
        sums, *scalings = later_iteration(
            kernel, exchange(sums), *related, mass, step == ITERS - 1
        )
    return finish(exchange(sums), mine, own, target_mass, scalings[0])


def solution(mesh):
    return jax.shard_map(
        local,
        mesh=mesh,
        in_specs=(
            P(("groups", "clus"), None),
            P(("groups", "clus"), None),
            P(("groups", "clus")),
            P(("groups", "clus")),
            P(("groups", "clus"), None),
            P(("groups", "clus"), None),
            P(("groups", "clus"), None),
            P(("groups", "clus")),
        ),
        out_specs=(P(("groups", "clus")), P(("groups", "clus"))),
        check_vma=False,
    )
```

```python
import functools
import math

import jax
import jax.numpy as jnp
from jax import lax
from jax.experimental import pallas as pl
from jax.experimental.pallas import tpu as pltpu
from jax.sharding import PartitionSpec as P

RB = 64
CB = 16
ITERS = 3
LANES = 128
VMEM_LIMIT = 48 * 1024 * 1024

F32 = jnp.float32
BF16 = jnp.bfloat16


def whole(space=pltpu.VMEM):
    return pl.BlockSpec(memory_space=space)


def call(kernel, name, out_shape, in_specs, out_specs=None, cost=(0, 0, 0), scratch_shapes=()):
    flops, bytes_accessed, transcendentals = cost
    return pl.pallas_call(
        kernel,
        name=name,
        out_shape=out_shape,
        in_specs=in_specs,
        out_specs=jax.tree.map(lambda _: whole(), out_shape) if out_specs is None else out_specs,
        scratch_shapes=scratch_shapes,
        cost_estimate=pl.CostEstimate(
            flops=flops, bytes_accessed=bytes_accessed, transcendentals=transcendentals
        ),
        compiler_params=pltpu.CompilerParams(vmem_limit_bytes=VMEM_LIMIT),
    )


def exchange(rows, groups=None):
    return lax.all_to_all(
        rows, "clus", split_axis=0, concat_axis=0, tiled=True, axis_index_groups=groups
    )


def note_kernel(mass_hbm, table_hbm, emb_hbm, out_ref, held_ref, mass_ref, table_ref, sems):
    copies = [
        pltpu.make_async_copy(mass_hbm, mass_ref, sems.at[0]),
        pltpu.make_async_copy(table_hbm, table_ref, sems.at[1]),
        pltpu.make_async_copy(emb_hbm, held_ref, sems.at[2]),
    ]
    for copy in copies:
        copy.start()
    for copy in copies[:2]:
        copy.wait()
    targets, peers = mass_ref.shape[1], table_ref.shape[1]
    shape = (out_ref.shape[0], 1)
    out_ref[:, :, :targets] = jnp.broadcast_to(mass_ref[...][None], shape + (targets,))
    out_ref[:, :, targets:] = jnp.zeros(shape + (out_ref.shape[2] - targets,), F32)
    out_ref[:, :, targets : targets + peers] = jnp.broadcast_to(
        table_ref[...].astype(F32)[None], shape + (peers,)
    )
    copies[2].wait()


def make_note(mass, table, blocks):
    peers = table.shape[1]
    length = mass.shape[1] + -(-peers // LANES) * LANES
    return call(
        note_kernel,
        "make_note",
        (
            jax.ShapeDtypeStruct((peers, 1, length), F32),
            jax.ShapeDtypeStruct(blocks.shape, F32),
        ),
        [whole(pltpu.HBM)] * 3,
        scratch_shapes=[
            pltpu.VMEM(mass.shape, F32),
            pltpu.VMEM(table.shape, jnp.int32),
            pltpu.SemaphoreType.DMA((3,)),
        ],
    )(mass, table, blocks)


def pick_kernel(
    place_ref, notes_ref, own_ref, other_ref, near_ref, far_ref, token_ref, *scratch_refs
):
    asked_ref, near_held, far_held, near_sems, far_sems = scratch_refs
    half, peers = near_ref.shape[0], far_ref.shape[0]
    count, _, width = own_ref.shape
    ahead = other_ref.shape[2]
    first = notes_ref.shape[2] - -(-peers // LANES) * LANES
    me = place_ref[0]
    side = me // half
    tables = notes_ref[:, 0, first:]
    lane = lax.broadcasted_iota(jnp.int32, tables.shape, 1)
    for turn, owner in enumerate((me, jnp.where(side == 0, me + half, me - half))):
        asked = jnp.sum(jnp.where(lane == owner, tables, 0.0), axis=1, keepdims=True)
        asked_ref[turn] = jnp.broadcast_to(asked, asked_ref.shape[1:])

    def select(emb_ref, wanted, columns):
        block = emb_ref[0, :, columns]
        for t in range(1, count):
            block = jnp.where(wanted == t, emb_ref[t, :, columns], block)
        return block

    def wanted_of(turn, d):
        return jnp.broadcast_to(asked_ref[turn, pl.ds(d, 1), :], (CB, LANES))

    def near_copy(d):
        return pltpu.make_async_copy(near_held.at[d], near_ref.at[d], near_sems.at[d])

    def far_copy(d):
        return pltpu.make_async_copy(far_held.at[d], far_ref.at[d], far_sems.at[d])

    def pick_far(d):
        wanted = wanted_of(0, d)
        for start in range(ahead, width, LANES):
            far_held[d, :, start - ahead : start - ahead + LANES] = select(
                own_ref, wanted, pl.ds(start, LANES)
            )
        far_copy(d).start()

    def pick_near(d):
        for turn, emb_ref in enumerate((own_ref, other_ref)):
            at = side if turn == 0 else 1 - side
            wanted = wanted_of(turn, side * half + d)
            for start in range(0, ahead, LANES):
                columns = pl.ds(start, LANES)
                near_held[d, at, :, columns] = select(emb_ref, wanted, columns)
        near_copy(d).start()

    for turns, pick in ((peers, pick_far), (half, pick_near)):
        if turns <= 16:
            for d in range(turns):
                pick(d)
        else:
            pl.loop(0, turns)(pick)
    token_ref[...] = jnp.zeros_like(token_ref)
    for turns, copy in ((peers, far_copy), (half, near_copy)):

        @pl.loop(0, turns)
        def _(d):
            copy(d).wait()


def pick_blocks(me, notes, own, other):
    peers = notes.shape[0]
    half = peers // 2
    ahead = other.shape[2]
    near = (half, 2, CB, ahead)
    far = (peers, CB, own.shape[2] - ahead)
    return call(
        pick_kernel,
        "pick_blocks",
        [jax.ShapeDtypeStruct(shape, F32) for shape in (near, far, (8, LANES))],
        [whole(pltpu.SMEM)] + [whole()] * 3,
        [whole(pl.ANY), whole(pl.ANY), whole()],
        scratch_shapes=[
            pltpu.VMEM((2, peers, LANES), F32),
            pltpu.VMEM(near, F32),
            pltpu.VMEM(far, F32),
            pltpu.SemaphoreType.DMA((half,)),
            pltpu.SemaphoreType.DMA((peers,)),
        ],
    )(me, notes, own, other)


def iota(shape, dimension):
    return lax.broadcasted_iota(jnp.int32, shape, dimension)


def slot_at(column, half, sides):
    block = column // CB
    return block % sides * half + block // sides


def product(a, b):
    return lax.dot_general(a, b, (((1,), (1,)), ((), ())), preferred_element_type=F32)


def prepare_kernel(
    sides,
    place_ref,
    notes_ref,
    table_ref,
    pools_ref,
    slots_ref,
    pool_mass_ref,
    _,
    listed_ref,
    same_ref,
    spare_ref,
    slot_mass_ref,
    mine_ref,
    own_ref,
    mass_ref,
):
    me, live = place_ref[0], place_ref[1]
    peers, columns = own_ref.shape[0], listed_ref.shape[1]
    half = peers // sides
    targets = own_ref.shape[1]
    pairs = pools_ref.shape[1]

    def hot(rows, values):
        return (rows == values).astype(F32).astype(BF16)

    column_slot = slot_at(iota((columns, 1), 0), half, sides)
    slot = slot_at(iota((1, columns), 1), half, sides)
    mine_ref[...] = (slot == me).astype(F32)
    listing = iota((1, pairs), 1) < live
    pool_hot = hot(iota((listed_ref.shape[0], pairs), 0), pools_ref[...])
    slot_hot = hot(column_slot, jnp.where(listing, slots_ref[...], -1))
    listed_ref[...] = product(pool_hot, slot_hot)

    spread = hot(column_slot, iota((columns, peers), 1))
    tables = notes_ref[:, 0, targets : targets + peers]
    table = table_ref[...].astype(F32)
    wide_tables = product(tables.astype(BF16), spread)
    wide_table = product(table.astype(BF16), spread)
    same_ref[...] = (wide_tables == wide_table).astype(F32)
    spare_ref[...] = (wide_table < 0).astype(F32)

    square = iota((peers, peers), 0), iota((peers, peers), 1)
    asked = jnp.sum(jnp.where(square[1] == me, tables, 0.0), axis=1, keepdims=True)
    block = (iota((peers, targets), 1) // CB).astype(F32)
    own_ref[...] = (asked == block).astype(F32)

    wanted = jnp.sum(jnp.where(square[0] == square[1], table, 0.0), axis=1, keepdims=True)
    masses = jnp.where(wanted == block, notes_ref[:, 0, :targets], 0.0)
    masses = fold(masses)
    slot_mass = [
        jnp.sum(
            jnp.where(
                iota((peers, LANES), 0) == slot_at(iota((peers, LANES), 1) + start, half, sides),
                masses,
                0.0,
            ),
            axis=0,
            keepdims=True,
        )
        for start in range(0, columns, LANES)
    ]
    slot_mass_ref[...] = jnp.concatenate(slot_mass, axis=1)

    diagonal = iota((LANES, LANES), 0) == iota((LANES, LANES), 1)
    for start in range(0, mass_ref.shape[0], LANES):
        row = pool_mass_ref[:, pl.ds(start, LANES)]
        mass_ref[pl.ds(start, LANES), :] = jnp.sum(
            jnp.where(diagonal, row, 0.0), axis=1, keepdims=True
        )


def prepare(place, notes, table, pools, slots, pool_mass, token, pool_count, targets, sides):
    peers = notes.shape[0]
    columns = peers * CB
    shapes = [
        (pool_count, columns),
        (peers, columns),
        (1, columns),
        (1, columns),
        (1, columns),
        (peers, targets),
        (pool_mass.shape[1], 1),
    ]
    return call(
        functools.partial(prepare_kernel, sides),
        "prepare",
        [jax.ShapeDtypeStruct(shape, F32) for shape in shapes],
        [whole(pltpu.SMEM)] + [whole()] * 6,
    )(place, notes, table, pools, slots, pool_mass, token)


def fold(rows):
    folded = rows[:, :LANES]
    for start in range(LANES, rows.shape[1], LANES):
        folded += rows[:, start : start + LANES]
    step = LANES // 2
    while step >= CB:
        folded += pltpu.roll(folded, step, 1)
        step //= 2
    return folded


def send_out(row, out_ref):
    out_ref[...] = jnp.broadcast_to(row[None], out_ref.shape)


def halves(x):
    high = x.astype(BF16)
    return high, (x - high.astype(F32)).astype(BF16)


def assemble_kernel(
    scale, pool_ref, near_ref, far_ref, listed_ref, mass_ref, kernel_ref, out_ref
):
    half, sides, _, ahead = near_ref.shape
    near = [near_ref[:, side].reshape(half * CB, ahead) for side in range(sides)]
    near_high, near_low = halves(jnp.concatenate(near, axis=0))
    far_high, far_low = halves(far_ref[...].reshape(kernel_ref.shape[1], -1))
    sums = jnp.zeros((1, kernel_ref.shape[1]), F32)
    rows = 256 if kernel_ref.shape[0] % 256 == 0 else RB

    def scores_of(p, q_high, q_low):
        high, low = halves(p)
        return product(high, q_high) + (product(high, q_low) + product(low, q_high))

    for start in range(0, kernel_ref.shape[0], rows):
        pool = pool_ref[pl.ds(start, rows), :]
        scores = scores_of(pool[:, :ahead], near_high, near_low)
        scores += scores_of(pool[:, ahead:], far_high, far_low)
        for block in range(rows // RB):
            inner = pl.ds(start + block * RB, RB)
            at = start // RB + block
            listed = listed_ref[at : at + 1, :] > 0
            values = jnp.where(
                listed, jnp.exp(scores[block * RB : (block + 1) * RB] * scale), 0.0
            )
            kernel_ref[inner, :] = values
            scaling = mass_ref[inner, :] / jnp.sum(values, axis=1, keepdims=True)
            sums += jnp.sum(values * scaling, axis=0, keepdims=True)
    send_out(sums, out_ref)


def assemble(pool, near, far, listed, mass):
    rows, width = pool.shape
    peers = far.shape[0]
    columns = peers * CB
    return call(
        functools.partial(assemble_kernel, 1.5 / math.sqrt(width)),
        "assemble",
        (
            jax.ShapeDtypeStruct((rows, columns), F32),
            jax.ShapeDtypeStruct((peers, 1, columns), F32),
        ),
        [whole()] * 5,
        cost=(
            6 * rows * columns * width,
            4 * (rows * width + columns * width + rows * columns),
            rows * columns,
        ),
    )(pool, near, far, listed, mass)


def iterate_kernel(
    kernel_ref, notes_ref, same_ref, slot_mass_ref, spare_ref, mass_ref, out_ref, *scaling_refs
):
    col_sums = jnp.sum(notes_ref[:, 0, :] * same_ref[...], axis=0, keepdims=True)
    target_scaling = slot_mass_ref[...] / (col_sums + spare_ref[...])
    sums = jnp.zeros_like(target_scaling)
    diagonal = lax.broadcasted_iota(jnp.int32, (LANES, LANES), 0) == lax.broadcasted_iota(
        jnp.int32, (LANES, LANES), 1
    )
    for start in range(0, kernel_ref.shape[0], LANES):
        inner = pl.ds(start, LANES)
        values = kernel_ref[inner, :]
        scaling = mass_ref[inner, :] / jnp.sum(values * target_scaling, axis=1, keepdims=True)
        sums += jnp.sum(values * scaling, axis=0, keepdims=True)
        for scaling_ref in scaling_refs:
            scaling_ref[:, inner] = jnp.sum(
                jnp.where(diagonal, scaling, 0.0), axis=0, keepdims=True
            )
    send_out(sums, out_ref)


def iterate(kernel, notes, same, slot_mass, spare, mass, last):
    rows, columns = kernel.shape
    out_shape = [jax.ShapeDtypeStruct(notes.shape, F32)]
    if last:
        out_shape.append(jax.ShapeDtypeStruct((1, rows), F32))
    return call(
        iterate_kernel,
        "iterate",
        out_shape,
        [whole()] * 6,
        cost=(4 * rows * columns, 4 * rows * columns, 0),
    )(kernel, notes, same, slot_mass, spare, mass)


def finish_kernel(
    notes_ref,
    mine_ref,
    own_ref,
    mass_ref,
    scaling_ref,
    pool_hbm,
    target_hbm,
    pool_ref,
    target_ref,
    sems,
):
    pool_ref[...] = jnp.log(scaling_ref[0])
    pool_copy = pltpu.make_async_copy(pool_ref, pool_hbm, sems.at[0])
    pool_copy.start()
    col_sums = jnp.sum(fold(notes_ref[:, 0, :] * mine_ref[...]) * own_ref[...], axis=0)
    target_ref[...] = jnp.log(mass_ref[...] / col_sums)
    target_copy = pltpu.make_async_copy(target_ref, target_hbm, sems.at[1])
    target_copy.start()
    pool_copy.wait()
    target_copy.wait()


def finish(notes, mine, own, mass, scaling):
    shapes = (scaling.shape[1:], mass.shape)
    return call(
        finish_kernel,
        "finish",
        tuple(jax.ShapeDtypeStruct(shape, F32) for shape in shapes),
        [whole()] * 5,
        (whole(pl.ANY),) * 2,
        scratch_shapes=[pltpu.VMEM(shape, F32) for shape in shapes]
        + [pltpu.SemaphoreType.DMA((2,))],
    )(notes, mine, own, mass, scaling)


def local(
    pool_emb,
    target_emb,
    pool_mass,
    target_mass,
    fetch_table,
    pair_pool,
    listed_pair_slot,
    pair_count,
):
    peers = lax.axis_size("clus")
    me = lax.axis_index("clus").astype(jnp.int32)
    targets, width = target_emb.shape
    pool_count = pool_emb.shape[0] // RB
    columns = peers * CB
    half = peers // 2
    ahead = width // LANES // 2 * LANES

    blocks = target_emb.reshape(targets // CB, CB, width)
    other = lax.ppermute(
        blocks[:, :, :ahead], "clus", [(i, (i + half) % peers) for i in range(peers)]
    )
    note, held = make_note(target_mass[None], fetch_table, blocks)
    notes = lax.cond(me < peers, exchange, jnp.zeros_like, note)
    near, far, token = pick_blocks(me[None], notes, held, other)
    far = exchange(far)
    near = exchange(near, [list(range(half)), list(range(half, peers))])
    listed, same, spare, slot_mass, mine, own, mass = prepare(
        jnp.concatenate([me[None], pair_count]),
        notes,
        fetch_table,
        pair_pool,
        listed_pair_slot,
        pool_mass[None],
        token,
        pool_count,
        targets,
        1,
    )

    kernel, sums = assemble(pool_emb, near, far, listed, mass)
    for step in range(1, ITERS):
        sums, *scalings = iterate(
            kernel, exchange(sums), same, slot_mass, spare, mass, step == ITERS - 1
        )
    return finish(exchange(sums), mine, own, target_mass, scalings[0])


def solution(mesh):
    return jax.shard_map(
        local,
        mesh=mesh,
        in_specs=(
            P(("groups", "clus"), None),
            P(("groups", "clus"), None),
            P(("groups", "clus")),
            P(("groups", "clus")),
            P(("groups", "clus"), None),
            P(("groups", "clus"), None),
            P(("groups", "clus"), None),
            P(("groups", "clus")),
        ),
        out_specs=(P(("groups", "clus")), P(("groups", "clus"))),
        check_vma=False,
    )
```

```python
import functools
import math

import jax
import jax.numpy as jnp
from jax import lax
from jax.experimental import pallas as pl
from jax.experimental.pallas import tpu as pltpu
from jax.sharding import PartitionSpec as P

RB = 64
CB = 16
ITERS = 3
LANES = 128
VMEM_LIMIT = 48 * 1024 * 1024

F32 = jnp.float32
BF16 = jnp.bfloat16


def whole(space=pltpu.VMEM):
    return pl.BlockSpec(memory_space=space)


def call(kernel, name, out_shape, in_specs, out_specs=None, cost=(0, 0, 0), scratch_shapes=()):
    flops, bytes_accessed, transcendentals = cost
    return pl.pallas_call(
        kernel,
        name=name,
        out_shape=out_shape,
        in_specs=in_specs,
        out_specs=jax.tree.map(lambda _: whole(), out_shape) if out_specs is None else out_specs,
        scratch_shapes=scratch_shapes,
        cost_estimate=pl.CostEstimate(
            flops=flops, bytes_accessed=bytes_accessed, transcendentals=transcendentals
        ),
        compiler_params=pltpu.CompilerParams(vmem_limit_bytes=VMEM_LIMIT),
    )


def exchange(rows, groups=None):
    return lax.all_to_all(
        rows, "clus", split_axis=0, concat_axis=0, tiled=True, axis_index_groups=groups
    )


def mate(local, turn, half):
    if half & (half - 1) == 0:
        return local ^ turn
    return (turn + half - local) % half


def note_kernel(mass_hbm, table_hbm, emb_hbm, out_ref, held_ref, mass_ref, table_ref, sems):
    copies = [
        pltpu.make_async_copy(mass_hbm, mass_ref, sems.at[0]),
        pltpu.make_async_copy(table_hbm, table_ref, sems.at[1]),
        pltpu.make_async_copy(emb_hbm, held_ref, sems.at[2]),
    ]
    for copy in copies:
        copy.start()
    for copy in copies[:2]:
        copy.wait()
    targets, peers = mass_ref.shape[1], table_ref.shape[1]
    shape = (out_ref.shape[0], 1)
    out_ref[:, :, :targets] = jnp.broadcast_to(mass_ref[...][None], shape + (targets,))
    out_ref[:, :, targets:] = jnp.zeros(shape + (out_ref.shape[2] - targets,), F32)
    out_ref[:, :, targets : targets + peers] = jnp.broadcast_to(
        table_ref[...].astype(F32)[None], shape + (peers,)
    )
    copies[2].wait()


def make_note(mass, table, blocks):
    peers = table.shape[1]
    length = mass.shape[1] + -(-peers // LANES) * LANES
    return call(
        note_kernel,
        "make_note",
        (
            jax.ShapeDtypeStruct((peers, 1, length), F32),
            jax.ShapeDtypeStruct(blocks.shape, F32),
        ),
        [whole(pltpu.HBM)] * 3,
        scratch_shapes=[
            pltpu.VMEM(mass.shape, F32),
            pltpu.VMEM(table.shape, jnp.int32),
            pltpu.SemaphoreType.DMA((3,)),
        ],
    )(mass, table, blocks)


def pick_kernel(half, place_ref, notes_ref, own_ref, other_ref, far_ref, token_ref, *refs):
    near_refs, (asked_ref, near_held, far_held, near_sems, far_sems) = refs[:half], refs[half:]
    peers = far_ref.shape[0]
    count, _, width = own_ref.shape
    ahead = other_ref.shape[2]
    first = notes_ref.shape[2] - -(-peers // LANES) * LANES
    me = place_ref[0]
    side = me // half
    tables = notes_ref[:, 0, first:]
    lane = lax.broadcasted_iota(jnp.int32, tables.shape, 1)
    for turn, owner in enumerate((me, jnp.where(side == 0, me + half, me - half))):
        asked = jnp.sum(jnp.where(lane == owner, tables, 0.0), axis=1, keepdims=True)
        asked_ref[turn] = jnp.broadcast_to(asked, asked_ref.shape[1:])

    def select(emb_ref, wanted, columns):
        block = emb_ref[0, :, columns]
        for t in range(1, count):
            block = jnp.where(wanted == t, emb_ref[t, :, columns], block)
        return block

    def wanted_of(turn, d):
        return jnp.broadcast_to(asked_ref[turn, pl.ds(d, 1), :], (CB, LANES))

    def near_copy(turn):
        return pltpu.make_async_copy(near_held.at[turn], near_refs[turn], near_sems.at[turn])

    def far_copy(d):
        return pltpu.make_async_copy(far_held.at[d], far_ref.at[d], far_sems.at[d])

    def pick_far(d):
        wanted = wanted_of(0, d)
        for start in range(ahead, width, LANES):
            far_held[d, :, start - ahead : start - ahead + LANES] = select(
                own_ref, wanted, pl.ds(start, LANES)
            )
        far_copy(d).start()

    if peers <= 16:
        for d in range(peers):
            pick_far(d)
    else:
        pl.loop(0, peers)(pick_far)
    for turn in range(half):
        reader = side * half + mate(me - side * half, turn, half)
        for source, emb_ref in enumerate((own_ref, other_ref)):
            at = side if source == 0 else 1 - side
            wanted = wanted_of(source, reader)

            @pl.loop(0, ahead // LANES)
            def _(part):
                columns = pl.ds(pl.multiple_of(part * LANES, LANES), LANES)
                near_held[turn, at, :, columns] = select(emb_ref, wanted, columns)

        near_copy(turn).start()
    token_ref[...] = jnp.zeros_like(token_ref)

    @pl.loop(0, peers)
    def _(d):
        far_copy(d).wait()

    for turn in range(half):
        near_copy(turn).wait()


def pick_blocks(me, notes, own, other):
    peers = notes.shape[0]
    half = peers // 2
    ahead = other.shape[2]
    near = (2, CB, ahead)
    far = (peers, CB, own.shape[2] - ahead)
    far, token, *near = call(
        functools.partial(pick_kernel, half),
        "pick_blocks",
        [jax.ShapeDtypeStruct(shape, F32) for shape in [far, (8, LANES)] + [near] * half],
        [whole(pltpu.SMEM)] + [whole()] * 3,
        [whole(pl.ANY), whole()] + [whole(pl.ANY)] * half,
        scratch_shapes=[
            pltpu.VMEM((2, peers, LANES), F32),
            pltpu.VMEM((half,) + near, F32),
            pltpu.VMEM(far, F32),
            pltpu.SemaphoreType.DMA((half,)),
            pltpu.SemaphoreType.DMA((peers,)),
        ],
    )(me, notes, own, other)
    return far, token, near


def iota(shape, dimension):
    return lax.broadcasted_iota(jnp.int32, shape, dimension)


def slot_at(column, half, sides):
    block = column // CB
    return block % sides * half + block // sides


def product(a, b):
    return lax.dot_general(a, b, (((1,), (1,)), ((), ())), preferred_element_type=F32)


def prepare_kernel(
    sides,
    place_ref,
    notes_ref,
    table_ref,
    pools_ref,
    slots_ref,
    pool_mass_ref,
    _,
    listed_ref,
    same_ref,
    spare_ref,
    slot_mass_ref,
    mine_ref,
    own_ref,
    mass_ref,
):
    me, live = place_ref[0], place_ref[1]
    peers, columns = own_ref.shape[0], listed_ref.shape[1]
    half = peers // sides
    targets = own_ref.shape[1]
    pairs = pools_ref.shape[1]

    def hot(rows, values):
        return (rows == values).astype(F32).astype(BF16)

    column_slot = slot_at(iota((columns, 1), 0), half, sides)
    slot = slot_at(iota((1, columns), 1), half, sides)
    mine_ref[...] = (slot == me).astype(F32)
    listing = iota((1, pairs), 1) < live
    pool_hot = hot(iota((listed_ref.shape[0], pairs), 0), pools_ref[...])
    slot_hot = hot(column_slot, jnp.where(listing, slots_ref[...], -1))
    listed_ref[...] = product(pool_hot, slot_hot)

    spread = hot(column_slot, iota((columns, peers), 1))
    tables = notes_ref[:, 0, targets : targets + peers]
    table = table_ref[...].astype(F32)
    wide_tables = product(tables.astype(BF16), spread)
    wide_table = product(table.astype(BF16), spread)
    same_ref[...] = (wide_tables == wide_table).astype(F32)
    spare_ref[...] = (wide_table < 0).astype(F32)

    square = iota((peers, peers), 0), iota((peers, peers), 1)
    asked = jnp.sum(jnp.where(square[1] == me, tables, 0.0), axis=1, keepdims=True)
    block = (iota((peers, targets), 1) // CB).astype(F32)
    own_ref[...] = (asked == block).astype(F32)

    wanted = jnp.sum(jnp.where(square[0] == square[1], table, 0.0), axis=1, keepdims=True)
    masses = jnp.where(wanted == block, notes_ref[:, 0, :targets], 0.0)
    masses = fold(masses)
    slot_mass = [
        jnp.sum(
            jnp.where(
                iota((peers, LANES), 0) == slot_at(iota((peers, LANES), 1) + start, half, sides),
                masses,
                0.0,
            ),
            axis=0,
            keepdims=True,
        )
        for start in range(0, columns, LANES)
    ]
    slot_mass_ref[...] = jnp.concatenate(slot_mass, axis=1)

    diagonal = iota((LANES, LANES), 0) == iota((LANES, LANES), 1)
    for start in range(0, mass_ref.shape[0], LANES):
        row = pool_mass_ref[:, pl.ds(start, LANES)]
        mass_ref[pl.ds(start, LANES), :] = jnp.sum(
            jnp.where(diagonal, row, 0.0), axis=1, keepdims=True
        )


def prepare(place, notes, table, pools, slots, pool_mass, token, pool_count, targets, sides):
    peers = notes.shape[0]
    columns = peers * CB
    shapes = [
        (pool_count, columns),
        (peers, columns),
        (1, columns),
        (1, columns),
        (1, columns),
        (peers, targets),
        (pool_mass.shape[1], 1),
    ]
    return call(
        functools.partial(prepare_kernel, sides),
        "prepare",
        [jax.ShapeDtypeStruct(shape, F32) for shape in shapes],
        [whole(pltpu.SMEM)] + [whole()] * 6,
    )(place, notes, table, pools, slots, pool_mass, token)


def fold(rows):
    folded = rows[:, :LANES]
    for start in range(LANES, rows.shape[1], LANES):
        folded += rows[:, start : start + LANES]
    step = LANES // 2
    while step >= CB:
        folded += pltpu.roll(folded, step, 1)
        step //= 2
    return folded


def send_out(row, out_ref):
    out_ref[...] = jnp.broadcast_to(row[None], out_ref.shape)


def halves(x):
    high = x.astype(BF16)
    return high, (x - high.astype(F32)).astype(BF16)


def assemble_kernel(scale, place_ref, pool_ref, far_ref, listed_ref, mass_ref, *refs):
    near_refs, (kernel_ref, out_ref, near_high, near_low) = refs[:-4], refs[-4:]
    half = len(near_refs)
    me = place_ref[0]
    local = jnp.where(me < half, me, me - half)
    for turn, near_ref in enumerate(near_refs):
        for side in range(2):
            slot = side * half + mate(local, turn, half)
            at = pl.ds(pl.multiple_of(slot * CB, CB), CB)
            near_high[at, :], near_low[at, :] = halves(near_ref[side])
    ahead = near_high.shape[1]
    far_high, far_low = halves(far_ref[...].reshape(kernel_ref.shape[1], -1))
    sums = jnp.zeros((1, kernel_ref.shape[1]), F32)
    rows = 256 if kernel_ref.shape[0] % 256 == 0 else RB

    def scores_of(p, q_high, q_low):
        high, low = halves(p)
        return product(high, q_high) + (product(high, q_low) + product(low, q_high))

    for start in range(0, kernel_ref.shape[0], rows):
        pool = pool_ref[pl.ds(start, rows), :]
        scores = scores_of(pool[:, :ahead], near_high[...], near_low[...])
        scores += scores_of(pool[:, ahead:], far_high, far_low)
        for block in range(rows // RB):
            inner = pl.ds(start + block * RB, RB)
            at = start // RB + block
            listed = listed_ref[at : at + 1, :] > 0
            values = jnp.where(
                listed, jnp.exp(scores[block * RB : (block + 1) * RB] * scale), 0.0
            )
            kernel_ref[inner, :] = values
            scaling = mass_ref[inner, :] / jnp.sum(values, axis=1, keepdims=True)
            sums += jnp.sum(values * scaling, axis=0, keepdims=True)
    send_out(sums, out_ref)


def assemble(place, pool, near, far, listed, mass):
    rows, width = pool.shape
    peers = far.shape[0]
    columns = peers * CB
    ahead = near[0].shape[2]
    return call(
        functools.partial(assemble_kernel, 1.5 / math.sqrt(width)),
        "assemble",
        (
            jax.ShapeDtypeStruct((rows, columns), F32),
            jax.ShapeDtypeStruct((peers, 1, columns), F32),
        ),
        [whole(pltpu.SMEM)] + [whole()] * (4 + len(near)),
        cost=(
            6 * rows * columns * width,
            4 * (rows * width + columns * width + rows * columns),
            rows * columns,
        ),
        scratch_shapes=[pltpu.VMEM((columns, ahead), BF16)] * 2,
    )(place, pool, far, listed, mass, *near)


def iterate_kernel(
    kernel_ref, notes_ref, same_ref, slot_mass_ref, spare_ref, mass_ref, out_ref, *scaling_refs
):
    col_sums = jnp.sum(notes_ref[:, 0, :] * same_ref[...], axis=0, keepdims=True)
    target_scaling = slot_mass_ref[...] / (col_sums + spare_ref[...])
    sums = jnp.zeros_like(target_scaling)
    diagonal = lax.broadcasted_iota(jnp.int32, (LANES, LANES), 0) == lax.broadcasted_iota(
        jnp.int32, (LANES, LANES), 1
    )
    for start in range(0, kernel_ref.shape[0], LANES):
        inner = pl.ds(start, LANES)
        values = kernel_ref[inner, :]
        scaling = mass_ref[inner, :] / jnp.sum(values * target_scaling, axis=1, keepdims=True)
        sums += jnp.sum(values * scaling, axis=0, keepdims=True)
        for scaling_ref in scaling_refs:
            scaling_ref[:, inner] = jnp.sum(
                jnp.where(diagonal, scaling, 0.0), axis=0, keepdims=True
            )
    send_out(sums, out_ref)


def iterate(kernel, notes, same, slot_mass, spare, mass, last):
    rows, columns = kernel.shape
    out_shape = [jax.ShapeDtypeStruct(notes.shape, F32)]
    if last:
        out_shape.append(jax.ShapeDtypeStruct((1, rows), F32))
    return call(
        iterate_kernel,
        "iterate",
        out_shape,
        [whole()] * 6,
        cost=(4 * rows * columns, 4 * rows * columns, 0),
    )(kernel, notes, same, slot_mass, spare, mass)


def finish_kernel(
    notes_ref,
    mine_ref,
    own_ref,
    mass_ref,
    scaling_ref,
    pool_hbm,
    target_hbm,
    pool_ref,
    target_ref,
    sems,
):
    pool_ref[...] = jnp.log(scaling_ref[0])
    pool_copy = pltpu.make_async_copy(pool_ref, pool_hbm, sems.at[0])
    pool_copy.start()
    col_sums = jnp.sum(fold(notes_ref[:, 0, :] * mine_ref[...]) * own_ref[...], axis=0)
    target_ref[...] = jnp.log(mass_ref[...] / col_sums)
    target_copy = pltpu.make_async_copy(target_ref, target_hbm, sems.at[1])
    target_copy.start()
    pool_copy.wait()
    target_copy.wait()


def finish(notes, mine, own, mass, scaling):
    shapes = (scaling.shape[1:], mass.shape)
    return call(
        finish_kernel,
        "finish",
        tuple(jax.ShapeDtypeStruct(shape, F32) for shape in shapes),
        [whole()] * 5,
        (whole(pl.ANY),) * 2,
        scratch_shapes=[pltpu.VMEM(shape, F32) for shape in shapes]
        + [pltpu.SemaphoreType.DMA((2,))],
    )(notes, mine, own, mass, scaling)


def local(
    pool_emb,
    target_emb,
    pool_mass,
    target_mass,
    fetch_table,
    pair_pool,
    listed_pair_slot,
    pair_count,
):
    peers = lax.axis_size("clus")
    me = lax.axis_index("clus").astype(jnp.int32)
    targets, width = target_emb.shape
    pool_count = pool_emb.shape[0] // RB
    columns = peers * CB
    half = peers // 2
    ahead = width // LANES // 2 * LANES

    def trade(x, turn):
        pairs = [
            (side * half + mate(i, turn, half), side * half + i)
            for side in range(2)
            for i in range(half)
        ]
        return lax.ppermute(x, "clus", [pair for pair in pairs if pair[0] != pair[1]])

    blocks = target_emb.reshape(targets // CB, CB, width)
    other = lax.ppermute(
        blocks[:, :, :ahead], "clus", [(i, (i + half) % peers) for i in range(peers)]
    )
    note, held = make_note(target_mass[None], fetch_table, blocks)
    notes = lax.cond(me < peers, exchange, jnp.zeros_like, note)
    far, token, near = pick_blocks(me[None], notes, held, other)
    far = exchange(far)
    near = [near[0]] + lax.cond(
        me < peers,
        lambda sent: [trade(x, turn) for turn, x in enumerate(sent, 1)],
        lambda sent: [jnp.zeros_like(x) for x in sent],
        near[1:],
    )
    place = jnp.concatenate([me[None], pair_count])
    listed, same, spare, slot_mass, mine, own, mass = prepare(
        place,
        notes,
        fetch_table,
        pair_pool,
        listed_pair_slot,
        pool_mass[None],
        token,
        pool_count,
        targets,
        1,
    )

    kernel, sums = assemble(place, pool_emb, near, far, listed, mass)
    for step in range(1, ITERS):
        sums, *scalings = iterate(
            kernel, exchange(sums), same, slot_mass, spare, mass, step == ITERS - 1
        )
    return finish(exchange(sums), mine, own, target_mass, scalings[0])


def solution(mesh):
    return jax.shard_map(
        local,
        mesh=mesh,
        in_specs=(
            P(("groups", "clus"), None),
            P(("groups", "clus"), None),
            P(("groups", "clus")),
            P(("groups", "clus")),
            P(("groups", "clus"), None),
            P(("groups", "clus"), None),
            P(("groups", "clus"), None),
            P(("groups", "clus")),
        ),
        out_specs=(P(("groups", "clus")), P(("groups", "clus"))),
        check_vma=False,
    )
```

```python
import functools
import math

import jax
import jax.numpy as jnp
from jax import lax
from jax.experimental import pallas as pl
from jax.experimental.pallas import tpu as pltpu
from jax.sharding import PartitionSpec as P

RB = 64
CB = 16
ITERS = 3
LANES = 128
VMEM_LIMIT = 48 * 1024 * 1024

F32 = jnp.float32
BF16 = jnp.bfloat16


def whole(space=pltpu.VMEM):
    return pl.BlockSpec(memory_space=space)


def call(kernel, name, out_shape, in_specs, out_specs=None, cost=(0, 0, 0), scratch_shapes=(), limit=VMEM_LIMIT):
    flops, bytes_accessed, transcendentals = cost
    return pl.pallas_call(
        kernel,
        name=name,
        out_shape=out_shape,
        in_specs=in_specs,
        out_specs=jax.tree.map(lambda _: whole(), out_shape) if out_specs is None else out_specs,
        scratch_shapes=scratch_shapes,
        cost_estimate=pl.CostEstimate(
            flops=flops, bytes_accessed=bytes_accessed, transcendentals=transcendentals
        ),
        compiler_params=pltpu.CompilerParams(vmem_limit_bytes=limit),
    )


def exchange(rows, groups=None):
    return lax.all_to_all(
        rows, "clus", split_axis=0, concat_axis=0, tiled=True, axis_index_groups=groups
    )


def mate(local, turn, half):
    if half & (half - 1) == 0:
        return local ^ turn
    return (turn + half - local) % half


def note_kernel(
    mass_hbm, table_hbm, emb_hbm, out_ref, held_ref, ahead_ref, mass_ref, table_ref, sems
):
    copies = [
        pltpu.make_async_copy(mass_hbm, mass_ref, sems.at[0]),
        pltpu.make_async_copy(table_hbm, table_ref, sems.at[1]),
        pltpu.make_async_copy(emb_hbm, held_ref, sems.at[2]),
    ]
    for copy in copies[::-1]:
        copy.start()
    for copy in copies[:2]:
        copy.wait()
    targets, peers = mass_ref.shape[1], table_ref.shape[1]
    shape = (out_ref.shape[0], 1)
    out_ref[:, :, :targets] = jnp.broadcast_to(mass_ref[...][None], shape + (targets,))
    out_ref[:, :, targets:] = jnp.zeros(shape + (out_ref.shape[2] - targets,), F32)
    out_ref[:, :, targets : targets + peers] = jnp.broadcast_to(
        table_ref[...].astype(F32)[None], shape + (peers,)
    )
    copies[2].wait()
    ahead_ref[...] = held_ref[:, :, : ahead_ref.shape[2]]


def make_note(mass, table, blocks, ahead):
    peers = table.shape[1]
    length = mass.shape[1] + -(-peers // LANES) * LANES
    return call(
        note_kernel,
        "make_note",
        (
            jax.ShapeDtypeStruct((peers, 1, length), F32),
            jax.ShapeDtypeStruct(blocks.shape, F32),
            jax.ShapeDtypeStruct(blocks.shape[:2] + (ahead,), F32),
        ),
        [whole(pltpu.HBM)] * 3,
        scratch_shapes=[
            pltpu.VMEM(mass.shape, F32),
            pltpu.VMEM(table.shape, jnp.int32),
            pltpu.SemaphoreType.DMA((3,)),
        ],
        limit=None,
    )(mass, table, blocks)


def pick_kernel(half, place_ref, notes_ref, own_ref, other_ref, far_ref, token_ref, *refs):
    near_refs, (asked_ref, near_held, far_held, near_sems, far_sems) = refs[:half], refs[half:]
    peers = far_ref.shape[0]
    count, _, width = own_ref.shape
    ahead = other_ref.shape[2]
    first = notes_ref.shape[2] - -(-peers // LANES) * LANES
    me = place_ref[0]
    side = me // half
    tables = notes_ref[:, 0, first:]
    lane = lax.broadcasted_iota(jnp.int32, tables.shape, 1)
    for turn, owner in enumerate((me, jnp.where(side == 0, me + half, me - half))):
        asked = jnp.sum(jnp.where(lane == owner, tables, 0.0), axis=1, keepdims=True)
        asked_ref[turn] = jnp.broadcast_to(asked, asked_ref.shape[1:])

    def select(emb_ref, wanted, columns):
        block = emb_ref[0, :, columns]
        for t in range(1, count):
            block = jnp.where(wanted == t, emb_ref[t, :, columns], block)
        return block

    def wanted_of(turn, d):
        return jnp.broadcast_to(asked_ref[turn, pl.ds(d, 1), :], (CB, LANES))

    def near_copy(turn):
        return pltpu.make_async_copy(near_held.at[turn], near_refs[turn], near_sems.at[turn])

    def far_copy(d):
        return pltpu.make_async_copy(far_held.at[d], far_ref.at[d], far_sems.at[d])

    def pick_far(d):
        wanted = wanted_of(0, d)
        for start in range(ahead, width, LANES):
            far_held[d, :, start - ahead : start - ahead + LANES] = select(
                own_ref, wanted, pl.ds(start, LANES)
            )
        far_copy(d).start()

    if peers <= 16:
        for d in range(peers):
            pick_far(d)
    else:
        pl.loop(0, peers)(pick_far)
    for turn in range(half):
        reader = side * half + mate(me - side * half, turn, half)
        for source, emb_ref in enumerate((own_ref, other_ref)):
            at = side if source == 0 else 1 - side
            wanted = wanted_of(source, reader)

            @pl.loop(0, ahead // LANES)
            def _(part):
                columns = pl.ds(pl.multiple_of(part * LANES, LANES), LANES)
                near_held[turn, at, :, columns] = select(emb_ref, wanted, columns)

        near_copy(turn).start()
    token_ref[...] = jnp.zeros_like(token_ref)

    @pl.loop(0, peers)
    def _(d):
        far_copy(d).wait()

    for turn in range(half):
        near_copy(turn).wait()


def pick_blocks(me, notes, own, other):
    peers = notes.shape[0]
    half = peers // 2
    ahead = other.shape[2]
    near = (2, CB, ahead)
    far = (peers, CB, own.shape[2] - ahead)
    far, token, *near = call(
        functools.partial(pick_kernel, half),
        "pick_blocks",
        [jax.ShapeDtypeStruct(shape, F32) for shape in [far, (8, LANES)] + [near] * half],
        [whole(pltpu.SMEM)] + [whole()] * 3,
        [whole(pl.ANY), whole()] + [whole(pl.ANY)] * half,
        scratch_shapes=[
            pltpu.VMEM((2, peers, LANES), F32),
            pltpu.VMEM((half,) + near, F32),
            pltpu.VMEM(far, F32),
            pltpu.SemaphoreType.DMA((half,)),
            pltpu.SemaphoreType.DMA((peers,)),
        ],
    )(me, notes, own, other)
    return far, token, near


def iota(shape, dimension):
    return lax.broadcasted_iota(jnp.int32, shape, dimension)


def slot_at(column, half, sides):
    block = column // CB
    return block % sides * half + block // sides


def product(a, b):
    return lax.dot_general(a, b, (((1,), (1,)), ((), ())), preferred_element_type=F32)


def prepare_kernel(
    sides,
    place_ref,
    notes_ref,
    table_ref,
    pools_ref,
    slots_ref,
    pool_mass_ref,
    _,
    listed_ref,
    same_ref,
    spare_ref,
    slot_mass_ref,
    mine_ref,
    own_ref,
    mass_ref,
):
    me, live = place_ref[0], place_ref[1]
    peers, columns = own_ref.shape[0], listed_ref.shape[1]
    half = peers // sides
    targets = own_ref.shape[1]
    pairs = pools_ref.shape[1]

    def hot(rows, values):
        return (rows == values).astype(F32).astype(BF16)

    column_slot = slot_at(iota((columns, 1), 0), half, sides)
    slot = slot_at(iota((1, columns), 1), half, sides)
    mine_ref[...] = (slot == me).astype(F32)
    listing = iota((1, pairs), 1) < live
    pool_hot = hot(iota((listed_ref.shape[0], pairs), 0), pools_ref[...])
    slot_hot = hot(column_slot, jnp.where(listing, slots_ref[...], -1))
    listed_ref[...] = product(pool_hot, slot_hot)

    spread = hot(column_slot, iota((columns, peers), 1))
    tables = notes_ref[:, 0, targets : targets + peers]
    table = table_ref[...].astype(F32)
    wide_tables = product(tables.astype(BF16), spread)
    wide_table = product(table.astype(BF16), spread)
    same_ref[...] = (wide_tables == wide_table).astype(F32)
    spare_ref[...] = (wide_table < 0).astype(F32)

    square = iota((peers, peers), 0), iota((peers, peers), 1)
    asked = jnp.sum(jnp.where(square[1] == me, tables, 0.0), axis=1, keepdims=True)
    block = (iota((peers, targets), 1) // CB).astype(F32)
    own_ref[...] = (asked == block).astype(F32)

    wanted = jnp.sum(jnp.where(square[0] == square[1], table, 0.0), axis=1, keepdims=True)
    masses = jnp.where(wanted == block, notes_ref[:, 0, :targets], 0.0)
    masses = fold(masses)
    slot_mass = [
        jnp.sum(
            jnp.where(
                iota((peers, LANES), 0) == slot_at(iota((peers, LANES), 1) + start, half, sides),
                masses,
                0.0,
            ),
            axis=0,
            keepdims=True,
        )
        for start in range(0, columns, LANES)
    ]
    slot_mass_ref[...] = jnp.concatenate(slot_mass, axis=1)

    diagonal = iota((LANES, LANES), 0) == iota((LANES, LANES), 1)
    for start in range(0, mass_ref.shape[0], LANES):
        row = pool_mass_ref[:, pl.ds(start, LANES)]
        mass_ref[pl.ds(start, LANES), :] = jnp.sum(
            jnp.where(diagonal, row, 0.0), axis=1, keepdims=True
        )


def prepare(place, notes, table, pools, slots, pool_mass, token, pool_count, targets, sides):
    peers = notes.shape[0]
    columns = peers * CB
    shapes = [
        (pool_count, columns),
        (peers, columns),
        (1, columns),
        (1, columns),
        (1, columns),
        (peers, targets),
        (pool_mass.shape[1], 1),
    ]
    return call(
        functools.partial(prepare_kernel, sides),
        "prepare",
        [jax.ShapeDtypeStruct(shape, F32) for shape in shapes],
        [whole(pltpu.SMEM)] + [whole()] * 6,
    )(place, notes, table, pools, slots, pool_mass, token)


def fold(rows):
    folded = rows[:, :LANES]
    for start in range(LANES, rows.shape[1], LANES):
        folded += rows[:, start : start + LANES]
    step = LANES // 2
    while step >= CB:
        folded += pltpu.roll(folded, step, 1)
        step //= 2
    return folded


def send_out(row, out_ref):
    out_ref[...] = jnp.broadcast_to(row[None], out_ref.shape)


def halves(x):
    high = x.astype(BF16)
    return high, (x - high.astype(F32)).astype(BF16)


def assemble_kernel(scale, place_ref, pool_ref, far_ref, listed_ref, mass_ref, *refs):
    near_refs, (kernel_ref, out_ref, near_high, near_low) = refs[:-4], refs[-4:]
    half = len(near_refs)
    me = place_ref[0]
    local = jnp.where(me < half, me, me - half)
    for turn, near_ref in enumerate(near_refs):
        for side in range(2):
            slot = side * half + mate(local, turn, half)
            at = pl.ds(pl.multiple_of(slot * CB, CB), CB)
            near_high[at, :], near_low[at, :] = halves(near_ref[side])
    ahead = near_high.shape[1]
    far_high, far_low = halves(far_ref[...].reshape(kernel_ref.shape[1], -1))
    sums = jnp.zeros((1, kernel_ref.shape[1]), F32)
    rows = 256 if kernel_ref.shape[0] % 256 == 0 else RB

    def scores_of(p, q_high, q_low):
        high, low = halves(p)
        return product(high, q_high) + (product(high, q_low) + product(low, q_high))

    for start in range(0, kernel_ref.shape[0], rows):
        pool = pool_ref[pl.ds(start, rows), :]
        scores = scores_of(pool[:, :ahead], near_high[...], near_low[...])
        scores += scores_of(pool[:, ahead:], far_high, far_low)
        for block in range(rows // RB):
            inner = pl.ds(start + block * RB, RB)
            at = start // RB + block
            listed = listed_ref[at : at + 1, :] > 0
            values = jnp.where(
                listed, jnp.exp(scores[block * RB : (block + 1) * RB] * scale), 0.0
            )
            kernel_ref[inner, :] = values
            scaling = mass_ref[inner, :] / jnp.sum(values, axis=1, keepdims=True)
            sums += jnp.sum(values * scaling, axis=0, keepdims=True)
    send_out(sums, out_ref)


def assemble(place, pool, near, far, listed, mass):
    rows, width = pool.shape
    peers = far.shape[0]
    columns = peers * CB
    ahead = near[0].shape[2]
    return call(
        functools.partial(assemble_kernel, 1.5 / math.sqrt(width)),
        "assemble",
        (
            jax.ShapeDtypeStruct((rows, columns), F32),
            jax.ShapeDtypeStruct((peers, 1, columns), F32),
        ),
        [whole(pltpu.SMEM)] + [whole()] * (4 + len(near)),
        cost=(
            6 * rows * columns * width,
            4 * (rows * width + columns * width + rows * columns),
            rows * columns,
        ),
        scratch_shapes=[pltpu.VMEM((columns, ahead), BF16)] * 2,
    )(place, pool, far, listed, mass, *near)


def iterate_kernel(
    kernel_ref, notes_ref, same_ref, slot_mass_ref, spare_ref, mass_ref, out_ref, *scaling_refs
):
    col_sums = jnp.sum(notes_ref[:, 0, :] * same_ref[...], axis=0, keepdims=True)
    target_scaling = slot_mass_ref[...] / (col_sums + spare_ref[...])
    sums = jnp.zeros_like(target_scaling)
    diagonal = lax.broadcasted_iota(jnp.int32, (LANES, LANES), 0) == lax.broadcasted_iota(
        jnp.int32, (LANES, LANES), 1
    )
    for start in range(0, kernel_ref.shape[0], LANES):
        inner = pl.ds(start, LANES)
        values = kernel_ref[inner, :]
        scaling = mass_ref[inner, :] / jnp.sum(values * target_scaling, axis=1, keepdims=True)
        sums += jnp.sum(values * scaling, axis=0, keepdims=True)
        for scaling_ref in scaling_refs:
            scaling_ref[:, inner] = jnp.sum(
                jnp.where(diagonal, scaling, 0.0), axis=0, keepdims=True
            )
    send_out(sums, out_ref)


def iterate(kernel, notes, same, slot_mass, spare, mass, last):
    rows, columns = kernel.shape
    out_shape = [jax.ShapeDtypeStruct(notes.shape, F32)]
    if last:
        out_shape.append(jax.ShapeDtypeStruct((1, rows), F32))
    return call(
        iterate_kernel,
        "iterate",
        out_shape,
        [whole()] * 6,
        cost=(4 * rows * columns, 4 * rows * columns, 0),
    )(kernel, notes, same, slot_mass, spare, mass)


def finish_kernel(
    notes_ref,
    mine_ref,
    own_ref,
    mass_ref,
    scaling_ref,
    pool_hbm,
    target_hbm,
    pool_ref,
    target_ref,
    sems,
):
    pool_ref[...] = jnp.log(scaling_ref[0])
    pool_copy = pltpu.make_async_copy(pool_ref, pool_hbm, sems.at[0])
    pool_copy.start()
    col_sums = jnp.sum(fold(notes_ref[:, 0, :] * mine_ref[...]) * own_ref[...], axis=0)
    target_ref[...] = jnp.log(mass_ref[...] / col_sums)
    target_copy = pltpu.make_async_copy(target_ref, target_hbm, sems.at[1])
    target_copy.start()
    pool_copy.wait()
    target_copy.wait()


def finish(notes, mine, own, mass, scaling):
    shapes = (scaling.shape[1:], mass.shape)
    return call(
        finish_kernel,
        "finish",
        tuple(jax.ShapeDtypeStruct(shape, F32) for shape in shapes),
        [whole()] * 5,
        (whole(pl.ANY),) * 2,
        scratch_shapes=[pltpu.VMEM(shape, F32) for shape in shapes]
        + [pltpu.SemaphoreType.DMA((2,))],
    )(notes, mine, own, mass, scaling)


def local(
    pool_emb,
    target_emb,
    pool_mass,
    target_mass,
    fetch_table,
    pair_pool,
    listed_pair_slot,
    pair_count,
):
    peers = lax.axis_size("clus")
    me = lax.axis_index("clus").astype(jnp.int32)
    targets, width = target_emb.shape
    pool_count = pool_emb.shape[0] // RB
    columns = peers * CB
    half = peers // 2
    ahead = width // LANES // 2 * LANES

    def trade(x, turn):
        pairs = [
            (side * half + mate(i, turn, half), side * half + i)
            for side in range(2)
            for i in range(half)
        ]
        return lax.ppermute(x, "clus", [pair for pair in pairs if pair[0] != pair[1]])

    blocks = target_emb.reshape(targets // CB, CB, width)
    note, held, other = make_note(target_mass[None], fetch_table, blocks, ahead)
    other = lax.ppermute(other, "clus", [(i, (i + half) % peers) for i in range(peers)])
    notes = lax.cond(me < peers, exchange, jnp.zeros_like, note)
    far, token, near = pick_blocks(me[None], notes, held, other)
    far = exchange(far)
    near = [near[0]] + [trade(x, turn) for turn, x in enumerate(near[1:], 1)]
    place = jnp.concatenate([me[None], pair_count])
    listed, same, spare, slot_mass, mine, own, mass = prepare(
        place,
        notes,
        fetch_table,
        pair_pool,
        listed_pair_slot,
        pool_mass[None],
        token,
        pool_count,
        targets,
        1,
    )

    kernel, sums = assemble(place, pool_emb, near, far, listed, mass)
    for step in range(1, ITERS):
        sums, *scalings = iterate(
            kernel, exchange(sums), same, slot_mass, spare, mass, step == ITERS - 1
        )
    return finish(exchange(sums), mine, own, target_mass, scalings[0])


def solution(mesh):
    return jax.shard_map(
        local,
        mesh=mesh,
        in_specs=(
            P(("groups", "clus"), None),
            P(("groups", "clus"), None),
            P(("groups", "clus")),
            P(("groups", "clus")),
            P(("groups", "clus"), None),
            P(("groups", "clus"), None),
            P(("groups", "clus"), None),
            P(("groups", "clus")),
        ),
        out_specs=(P(("groups", "clus")), P(("groups", "clus"))),
        check_vma=False,
    )
```

```python
import functools
import math

import jax
import jax.numpy as jnp
from jax import lax
from jax.experimental import pallas as pl
from jax.experimental.pallas import tpu as pltpu
from jax.sharding import PartitionSpec as P

RB = 64
CB = 16
ITERS = 3
LANES = 128
VMEM_LIMIT = 48 * 1024 * 1024

F32 = jnp.float32
BF16 = jnp.bfloat16


def whole(space=pltpu.VMEM):
    return pl.BlockSpec(memory_space=space)


def call(kernel, name, out_shape, in_specs, out_specs=None, cost=(0, 0, 0), scratch_shapes=()):
    flops, bytes_accessed, transcendentals = cost
    return pl.pallas_call(
        kernel,
        name=name,
        out_shape=out_shape,
        in_specs=in_specs,
        out_specs=jax.tree.map(lambda _: whole(), out_shape) if out_specs is None else out_specs,
        scratch_shapes=scratch_shapes,
        cost_estimate=pl.CostEstimate(
            flops=flops, bytes_accessed=bytes_accessed, transcendentals=transcendentals
        ),
        compiler_params=pltpu.CompilerParams(vmem_limit_bytes=VMEM_LIMIT),
    )


def exchange(rows, groups=None):
    return lax.all_to_all(
        rows, "clus", split_axis=0, concat_axis=0, tiled=True, axis_index_groups=groups
    )


def mate(local, turn, half):
    if half & (half - 1) == 0:
        return local ^ turn
    return (turn + half - local) % half


def note_kernel(mass_hbm, table_hbm, emb_hbm, out_ref, held_ref, mass_ref, table_ref, sems):
    copies = [
        pltpu.make_async_copy(mass_hbm, mass_ref, sems.at[0]),
        pltpu.make_async_copy(table_hbm, table_ref, sems.at[1]),
        pltpu.make_async_copy(emb_hbm, held_ref, sems.at[2]),
    ]
    for copy in copies:
        copy.start()
    for copy in copies[:2]:
        copy.wait()
    targets, peers = mass_ref.shape[1], table_ref.shape[1]
    shape = (out_ref.shape[0], 1)
    out_ref[:, :, :targets] = jnp.broadcast_to(mass_ref[...][None], shape + (targets,))
    out_ref[:, :, targets:] = jnp.zeros(shape + (out_ref.shape[2] - targets,), F32)
    out_ref[:, :, targets : targets + peers] = jnp.broadcast_to(
        table_ref[...].astype(F32)[None], shape + (peers,)
    )
    copies[2].wait()


def make_note(mass, table, blocks):
    peers = table.shape[1]
    length = mass.shape[1] + -(-peers // LANES) * LANES
    return call(
        note_kernel,
        "make_note",
        (
            jax.ShapeDtypeStruct((peers, 1, length), F32),
            jax.ShapeDtypeStruct(blocks.shape, F32),
        ),
        [whole(pltpu.HBM)] * 3,
        scratch_shapes=[
            pltpu.VMEM(mass.shape, F32),
            pltpu.VMEM(table.shape, jnp.int32),
            pltpu.SemaphoreType.DMA((3,)),
        ],
    )(mass, table, blocks)


def pick_kernel(half, place_ref, notes_ref, own_ref, other_ref, far_ref, token_ref, *refs):
    near_refs, (asked_ref, near_held, far_held, near_sems, far_sems) = refs[:half], refs[half:]
    peers = far_ref.shape[0]
    count, _, width = own_ref.shape
    ahead = other_ref.shape[2]
    first = notes_ref.shape[2] - -(-peers // LANES) * LANES
    me = place_ref[0]
    side = me // half
    tables = notes_ref[:, 0, first:]
    lane = lax.broadcasted_iota(jnp.int32, tables.shape, 1)
    for turn, owner in enumerate((me, jnp.where(side == 0, me + half, me - half))):
        asked = jnp.sum(jnp.where(lane == owner, tables, 0.0), axis=1, keepdims=True)
        asked_ref[turn] = jnp.broadcast_to(asked, asked_ref.shape[1:])

    def select(emb_ref, wanted, columns):
        block = emb_ref[0, :, columns]
        for t in range(1, count):
            block = jnp.where(wanted == t, emb_ref[t, :, columns], block)
        return block

    def wanted_of(turn, d):
        return jnp.broadcast_to(asked_ref[turn, pl.ds(d, 1), :], (CB, LANES))

    def near_copy(turn):
        return pltpu.make_async_copy(near_held.at[turn], near_refs[turn], near_sems.at[turn])

    def far_copy(d):
        return pltpu.make_async_copy(far_held.at[d], far_ref.at[d], far_sems.at[d])

    def pick_far(d):
        wanted = wanted_of(0, d)
        for start in range(ahead, width, LANES):
            far_held[d, :, start - ahead : start - ahead + LANES] = select(
                own_ref, wanted, pl.ds(start, LANES)
            )
        far_copy(d).start()

    if peers <= 16:
        for d in range(peers):
            pick_far(d)
    else:
        pl.loop(0, peers)(pick_far)
    for turn in range(half):
        reader = side * half + mate(me - side * half, turn, half)
        for source, emb_ref in enumerate((own_ref, other_ref)):
            at = side if source == 0 else 1 - side
            wanted = wanted_of(source, reader)

            @pl.loop(0, ahead // LANES)
            def _(part):
                columns = pl.ds(pl.multiple_of(part * LANES, LANES), LANES)
                near_held[turn, at, :, columns] = select(emb_ref, wanted, columns)

        near_copy(turn).start()
    token_ref[...] = jnp.zeros_like(token_ref)

    @pl.loop(0, peers)
    def _(d):
        far_copy(d).wait()

    for turn in range(half):
        near_copy(turn).wait()


def pick_blocks(me, notes, own, other):
    peers = notes.shape[0]
    half = peers // 2
    ahead = other.shape[2]
    near = (2, CB, ahead)
    far = (peers, CB, own.shape[2] - ahead)
    far, token, *near = call(
        functools.partial(pick_kernel, half),
        "pick_blocks",
        [jax.ShapeDtypeStruct(shape, F32) for shape in [far, (8, LANES)] + [near] * half],
        [whole(pltpu.SMEM)] + [whole()] * 3,
        [whole(pl.ANY), whole()] + [whole(pl.ANY)] * half,
        scratch_shapes=[
            pltpu.VMEM((2, peers, LANES), F32),
            pltpu.VMEM((half,) + near, F32),
            pltpu.VMEM(far, F32),
            pltpu.SemaphoreType.DMA((half,)),
            pltpu.SemaphoreType.DMA((peers,)),
        ],
    )(me, notes, own, other)
    return far, token, near


def iota(shape, dimension):
    return lax.broadcasted_iota(jnp.int32, shape, dimension)


def slot_at(column, half, sides):
    block = column // CB
    return block % sides * half + block // sides


def product(a, b):
    return lax.dot_general(a, b, (((1,), (1,)), ((), ())), preferred_element_type=F32)


def prepare_kernel(
    sides,
    place_ref,
    notes_ref,
    table_ref,
    pools_ref,
    slots_ref,
    pool_mass_ref,
    _,
    listed_ref,
    same_ref,
    spare_ref,
    slot_mass_ref,
    mine_ref,
    own_ref,
    mass_ref,
):
    me, live = place_ref[0], place_ref[1]
    peers, columns = own_ref.shape[0], listed_ref.shape[1]
    half = peers // sides
    targets = own_ref.shape[1]
    pairs = pools_ref.shape[1]

    def hot(rows, values):
        return (rows == values).astype(F32).astype(BF16)

    column_slot = slot_at(iota((columns, 1), 0), half, sides)
    slot = slot_at(iota((1, columns), 1), half, sides)
    mine_ref[...] = (slot == me).astype(F32)
    listing = iota((1, pairs), 1) < live
    pool_hot = hot(iota((listed_ref.shape[0], pairs), 0), pools_ref[...])
    slot_hot = hot(column_slot, jnp.where(listing, slots_ref[...], -1))
    listed_ref[...] = product(pool_hot, slot_hot)

    spread = hot(column_slot, iota((columns, peers), 1))
    tables = notes_ref[:, 0, targets : targets + peers]
    table = table_ref[...].astype(F32)
    wide_tables = product(tables.astype(BF16), spread)
    wide_table = product(table.astype(BF16), spread)
    same_ref[...] = (wide_tables == wide_table).astype(F32)
    spare_ref[...] = (wide_table < 0).astype(F32)

    square = iota((peers, peers), 0), iota((peers, peers), 1)
    asked = jnp.sum(jnp.where(square[1] == me, tables, 0.0), axis=1, keepdims=True)
    block = (iota((peers, targets), 1) // CB).astype(F32)
    own_ref[...] = (asked == block).astype(F32)

    wanted = jnp.sum(jnp.where(square[0] == square[1], table, 0.0), axis=1, keepdims=True)
    masses = jnp.where(wanted == block, notes_ref[:, 0, :targets], 0.0)
    masses = fold(masses)
    slot_mass = [
        jnp.sum(
            jnp.where(
                iota((peers, LANES), 0) == slot_at(iota((peers, LANES), 1) + start, half, sides),
                masses,
                0.0,
            ),
            axis=0,
            keepdims=True,
        )
        for start in range(0, columns, LANES)
    ]
    slot_mass_ref[...] = jnp.concatenate(slot_mass, axis=1)

    diagonal = iota((LANES, LANES), 0) == iota((LANES, LANES), 1)
    for start in range(0, mass_ref.shape[0], LANES):
        row = pool_mass_ref[:, pl.ds(start, LANES)]
        mass_ref[pl.ds(start, LANES), :] = jnp.sum(
            jnp.where(diagonal, row, 0.0), axis=1, keepdims=True
        )


def prepare(place, notes, table, pools, slots, pool_mass, token, pool_count, targets, sides):
    peers = notes.shape[0]
    columns = peers * CB
    shapes = [
        (pool_count, columns),
        (peers, columns),
        (1, columns),
        (1, columns),
        (1, columns),
        (peers, targets),
        (pool_mass.shape[1], 1),
    ]
    return call(
        functools.partial(prepare_kernel, sides),
        "prepare",
        [jax.ShapeDtypeStruct(shape, F32) for shape in shapes],
        [whole(pltpu.SMEM)] + [whole()] * 6,
    )(place, notes, table, pools, slots, pool_mass, token)


def fold(rows):
    folded = rows[:, :LANES]
    for start in range(LANES, rows.shape[1], LANES):
        folded += rows[:, start : start + LANES]
    step = LANES // 2
    while step >= CB:
        folded += pltpu.roll(folded, step, 1)
        step //= 2
    return folded


def send_out(row, out_ref):
    out_ref[...] = jnp.broadcast_to(row[None], out_ref.shape)


def halves(x):
    high = x.astype(BF16)
    return high, (x - high.astype(F32)).astype(BF16)


def assemble_kernel(scale, place_ref, pool_ref, far_ref, listed_ref, mass_ref, *refs):
    near_refs, (kernel_ref, out_ref, near_high, near_low) = refs[:-4], refs[-4:]
    half = len(near_refs)
    me = place_ref[0]
    local = jnp.where(me < half, me, me - half)
    for turn, near_ref in enumerate(near_refs):
        for side in range(2):
            slot = side * half + mate(local, turn, half)
            at = pl.ds(pl.multiple_of(slot * CB, CB), CB)
            near_high[at, :], near_low[at, :] = halves(near_ref[side])
    ahead = near_high.shape[1]
    far_high, far_low = halves(far_ref[...].reshape(kernel_ref.shape[1], -1))
    sums = jnp.zeros((1, kernel_ref.shape[1]), F32)
    rows = 256 if kernel_ref.shape[0] % 256 == 0 else RB

    def scores_of(p, q_high, q_low):
        high, low = halves(p)
        return product(high, q_high) + (product(high, q_low) + product(low, q_high))

    for start in range(0, kernel_ref.shape[0], rows):
        pool = pool_ref[pl.ds(start, rows), :]
        scores = scores_of(pool[:, :ahead], near_high[...], near_low[...])
        scores += scores_of(pool[:, ahead:], far_high, far_low)
        for block in range(rows // RB):
            inner = pl.ds(start + block * RB, RB)
            at = start // RB + block
            listed = listed_ref[at : at + 1, :] > 0
            values = jnp.where(
                listed, jnp.exp(scores[block * RB : (block + 1) * RB] * scale), 0.0
            )
            kernel_ref[inner, :] = values
            scaling = mass_ref[inner, :] / jnp.sum(values, axis=1, keepdims=True)
            sums += jnp.sum(values * scaling, axis=0, keepdims=True)
    send_out(sums, out_ref)


def assemble(place, pool, near, far, listed, mass):
    rows, width = pool.shape
    peers = far.shape[0]
    columns = peers * CB
    ahead = near[0].shape[2]
    return call(
        functools.partial(assemble_kernel, 1.5 / math.sqrt(width)),
        "assemble",
        (
            jax.ShapeDtypeStruct((rows, columns), F32),
            jax.ShapeDtypeStruct((peers, 1, columns), F32),
        ),
        [whole(pltpu.SMEM)] + [whole()] * (4 + len(near)),
        cost=(
            6 * rows * columns * width,
            4 * (rows * width + columns * width + rows * columns),
            rows * columns,
        ),
        scratch_shapes=[pltpu.VMEM((columns, ahead), BF16)] * 2,
    )(place, pool, far, listed, mass, *near)


def iterate_kernel(
    kernel_ref, notes_ref, same_ref, slot_mass_ref, spare_ref, mass_ref, out_ref, *scaling_refs
):
    col_sums = jnp.sum(notes_ref[:, 0, :] * same_ref[...], axis=0, keepdims=True)
    target_scaling = slot_mass_ref[...] / (col_sums + spare_ref[...])
    sums = jnp.zeros_like(target_scaling)
    diagonal = lax.broadcasted_iota(jnp.int32, (LANES, LANES), 0) == lax.broadcasted_iota(
        jnp.int32, (LANES, LANES), 1
    )
    for start in range(0, kernel_ref.shape[0], LANES):
        inner = pl.ds(start, LANES)
        values = kernel_ref[inner, :]
        scaling = mass_ref[inner, :] / jnp.sum(values * target_scaling, axis=1, keepdims=True)
        sums += jnp.sum(values * scaling, axis=0, keepdims=True)
        for scaling_ref in scaling_refs:
            scaling_ref[:, inner] = jnp.sum(
                jnp.where(diagonal, scaling, 0.0), axis=0, keepdims=True
            )
    send_out(sums, out_ref)


def iterate(kernel, notes, same, slot_mass, spare, mass, last):
    rows, columns = kernel.shape
    out_shape = [jax.ShapeDtypeStruct(notes.shape, F32)]
    if last:
        out_shape.append(jax.ShapeDtypeStruct((1, rows), F32))
    return call(
        iterate_kernel,
        "iterate",
        out_shape,
        [whole()] * 6,
        cost=(4 * rows * columns, 4 * rows * columns, 0),
    )(kernel, notes, same, slot_mass, spare, mass)


def finish_kernel(
    notes_ref,
    mine_ref,
    own_ref,
    mass_ref,
    scaling_ref,
    pool_hbm,
    target_hbm,
    pool_ref,
    target_ref,
    sems,
):
    pool_ref[...] = jnp.log(scaling_ref[0])
    pool_copy = pltpu.make_async_copy(pool_ref, pool_hbm, sems.at[0])
    pool_copy.start()
    col_sums = jnp.sum(fold(notes_ref[:, 0, :] * mine_ref[...]) * own_ref[...], axis=0)
    target_ref[...] = jnp.log(mass_ref[...] / col_sums)
    target_copy = pltpu.make_async_copy(target_ref, target_hbm, sems.at[1])
    target_copy.start()
    pool_copy.wait()
    target_copy.wait()


def finish(notes, mine, own, mass, scaling):
    shapes = (scaling.shape[1:], mass.shape)
    return call(
        finish_kernel,
        "finish",
        tuple(jax.ShapeDtypeStruct(shape, F32) for shape in shapes),
        [whole()] * 5,
        (whole(pl.ANY),) * 2,
        scratch_shapes=[pltpu.VMEM(shape, F32) for shape in shapes]
        + [pltpu.SemaphoreType.DMA((2,))],
    )(notes, mine, own, mass, scaling)


def local(
    pool_emb,
    target_emb,
    pool_mass,
    target_mass,
    fetch_table,
    pair_pool,
    listed_pair_slot,
    pair_count,
):
    peers = lax.axis_size("clus")
    me = lax.axis_index("clus").astype(jnp.int32)
    targets, width = target_emb.shape
    pool_count = pool_emb.shape[0] // RB
    columns = peers * CB
    half = peers // 2
    ahead = width // LANES // 2 * LANES

    def trade(x, turn):
        pairs = [
            (side * half + mate(i, turn, half), side * half + i)
            for side in range(2)
            for i in range(half)
        ]
        return lax.ppermute(x, "clus", [pair for pair in pairs if pair[0] != pair[1]])

    blocks = target_emb.reshape(targets // CB, CB, width)
    other = lax.ppermute(
        blocks[:, :, :ahead], "clus", [(i, (i + half) % peers) for i in range(peers)]
    )
    note, held = make_note(target_mass[None], fetch_table, blocks)
    notes = lax.cond(me < peers, exchange, jnp.zeros_like, note)
    far, token, near = pick_blocks(me[None], notes, held, other)
    far = exchange(far)
    near = [near[0]] + [trade(x, turn) for turn, x in enumerate(near[1:], 1)]
    place = jnp.concatenate([me[None], pair_count])
    listed, same, spare, slot_mass, mine, own, mass = prepare(
        place,
        notes,
        fetch_table,
        pair_pool,
        listed_pair_slot,
        pool_mass[None],
        token,
        pool_count,
        targets,
        1,
    )

    kernel, sums = assemble(place, pool_emb, near, far, listed, mass)
    for step in range(1, ITERS):
        sums, *scalings = iterate(
            kernel, exchange(sums), same, slot_mass, spare, mass, step == ITERS - 1
        )
    return finish(exchange(sums), mine, own, target_mass, scalings[0])


def solution(mesh):
    return jax.shard_map(
        local,
        mesh=mesh,
        in_specs=(
            P(("groups", "clus"), None),
            P(("groups", "clus"), None),
            P(("groups", "clus")),
            P(("groups", "clus")),
            P(("groups", "clus"), None),
            P(("groups", "clus"), None),
            P(("groups", "clus"), None),
            P(("groups", "clus")),
        ),
        out_specs=(P(("groups", "clus")), P(("groups", "clus"))),
        check_vma=False,
    )
```

```python
import functools
import math

import jax
import jax.numpy as jnp
from jax import lax
from jax.experimental import pallas as pl
from jax.experimental.pallas import tpu as pltpu
from jax.sharding import PartitionSpec as P

RB = 64
CB = 16
ITERS = 3
LANES = 128
VMEM_LIMIT = 48 * 1024 * 1024

F32 = jnp.float32
BF16 = jnp.bfloat16


def whole(space=pltpu.VMEM):
    return pl.BlockSpec(memory_space=space)


def call(kernel, name, out_shape, in_specs, out_specs=None, cost=(0, 0, 0), scratch_shapes=()):
    flops, bytes_accessed, transcendentals = cost
    return pl.pallas_call(
        kernel,
        name=name,
        out_shape=out_shape,
        in_specs=in_specs,
        out_specs=jax.tree.map(lambda _: whole(), out_shape) if out_specs is None else out_specs,
        scratch_shapes=scratch_shapes,
        cost_estimate=pl.CostEstimate(
            flops=flops, bytes_accessed=bytes_accessed, transcendentals=transcendentals
        ),
        compiler_params=pltpu.CompilerParams(vmem_limit_bytes=VMEM_LIMIT),
    )


def exchange(rows, groups=None):
    return lax.all_to_all(
        rows, "clus", split_axis=0, concat_axis=0, tiled=True, axis_index_groups=groups
    )


def mate(local, turn, half):
    if half & (half - 1) == 0:
        return local ^ turn
    return (turn + half - local) % half


def note_kernel(mass_hbm, table_hbm, emb_hbm, out_ref, held_ref, mass_ref, table_ref, sems):
    copies = [
        pltpu.make_async_copy(mass_hbm, mass_ref, sems.at[0]),
        pltpu.make_async_copy(table_hbm, table_ref, sems.at[1]),
        pltpu.make_async_copy(emb_hbm, held_ref, sems.at[2]),
    ]
    for copy in copies:
        copy.start()
    for copy in copies[:2]:
        copy.wait()
    targets, peers = mass_ref.shape[1], table_ref.shape[1]
    shape = (out_ref.shape[0], 1)
    out_ref[:, :, :targets] = jnp.broadcast_to(mass_ref[...][None], shape + (targets,))
    out_ref[:, :, targets:] = jnp.zeros(shape + (out_ref.shape[2] - targets,), F32)
    out_ref[:, :, targets : targets + peers] = jnp.broadcast_to(
        table_ref[...].astype(F32)[None], shape + (peers,)
    )
    copies[2].wait()


def make_note(mass, table, blocks):
    peers = table.shape[1]
    length = mass.shape[1] + -(-peers // LANES) * LANES
    return call(
        note_kernel,
        "make_note",
        (
            jax.ShapeDtypeStruct((peers, 1, length), F32),
            jax.ShapeDtypeStruct(blocks.shape, F32),
        ),
        [whole(pltpu.HBM)] * 3,
        scratch_shapes=[
            pltpu.VMEM(mass.shape, F32),
            pltpu.VMEM(table.shape, jnp.int32),
            pltpu.SemaphoreType.DMA((3,)),
        ],
    )(mass, table, blocks)


def pick_kernel(half, place_ref, notes_ref, own_ref, other_ref, far_ref, token_ref, *refs):
    near_refs, (asked_ref, near_held, far_held, near_sems, far_sems) = refs[:half], refs[half:]
    peers = far_ref.shape[0]
    count, _, width = own_ref.shape
    ahead = other_ref.shape[2]
    first = notes_ref.shape[2] - -(-peers // LANES) * LANES
    me = place_ref[0]
    side = me // half
    tables = notes_ref[:, 0, first:]
    lane = lax.broadcasted_iota(jnp.int32, tables.shape, 1)
    for turn, owner in enumerate((me, jnp.where(side == 0, me + half, me - half))):
        asked = jnp.sum(jnp.where(lane == owner, tables, 0.0), axis=1, keepdims=True)
        asked_ref[turn] = jnp.broadcast_to(asked, asked_ref.shape[1:])

    def select(emb_ref, wanted, columns):
        block = emb_ref[0, :, columns]
        for t in range(1, count):
            block = jnp.where(wanted == t, emb_ref[t, :, columns], block)
        return block

    def wanted_of(turn, d):
        return jnp.broadcast_to(asked_ref[turn, pl.ds(d, 1), :], (CB, LANES))

    def near_copy(turn):
        return pltpu.make_async_copy(near_held.at[turn], near_refs[turn], near_sems.at[turn])

    def far_copy(d):
        return pltpu.make_async_copy(far_held.at[d], far_ref.at[d], far_sems.at[d])

    def pick_far(d):
        wanted = wanted_of(0, d)
        for start in range(ahead, width, LANES):
            far_held[d, :, start - ahead : start - ahead + LANES] = select(
                own_ref, wanted, pl.ds(start, LANES)
            )
        far_copy(d).start()

    if peers <= 16:
        for d in range(peers):
            pick_far(d)
    else:
        pl.loop(0, peers)(pick_far)
    for turn in range(half):
        reader = side * half + mate(me - side * half, turn, half)
        for source, emb_ref in enumerate((own_ref, other_ref)):
            at = side if source == 0 else 1 - side
            wanted = wanted_of(source, reader)

            @pl.loop(0, ahead // LANES)
            def _(part):
                columns = pl.ds(pl.multiple_of(part * LANES, LANES), LANES)
                near_held[turn, at, :, columns] = select(emb_ref, wanted, columns)

        near_copy(turn).start()
    token_ref[...] = jnp.zeros_like(token_ref)

    @pl.loop(0, peers)
    def _(d):
        far_copy(d).wait()

    for turn in range(half):
        near_copy(turn).wait()


def pick_blocks(me, notes, own, other):
    peers = notes.shape[0]
    half = peers // 2
    ahead = other.shape[2]
    near = (2, CB, ahead)
    far = (peers, CB, own.shape[2] - ahead)
    far, token, *near = call(
        functools.partial(pick_kernel, half),
        "pick_blocks",
        [jax.ShapeDtypeStruct(shape, F32) for shape in [far, (8, LANES)] + [near] * half],
        [whole(pltpu.SMEM)] + [whole()] * 3,
        [whole(pl.ANY), whole()] + [whole(pl.ANY)] * half,
        scratch_shapes=[
            pltpu.VMEM((2, peers, LANES), F32),
            pltpu.VMEM((half,) + near, F32),
            pltpu.VMEM(far, F32),
            pltpu.SemaphoreType.DMA((half,)),
            pltpu.SemaphoreType.DMA((peers,)),
        ],
    )(me, notes, own, other)
    return far, token, near


def iota(shape, dimension):
    return lax.broadcasted_iota(jnp.int32, shape, dimension)


def slot_at(column, half, sides):
    block = column // CB
    return block % sides * half + block // sides


def product(a, b):
    return lax.dot_general(a, b, (((1,), (1,)), ((), ())), preferred_element_type=F32)


def prepare_kernel(
    sides,
    place_ref,
    notes_ref,
    table_ref,
    pools_ref,
    slots_ref,
    pool_mass_ref,
    _,
    listed_ref,
    same_ref,
    spare_ref,
    slot_mass_ref,
    mine_ref,
    own_ref,
    mass_ref,
):
    me, live = place_ref[0], place_ref[1]
    peers, columns = own_ref.shape[0], listed_ref.shape[1]
    half = peers // sides
    targets = own_ref.shape[1]
    pairs = pools_ref.shape[1]

    def hot(rows, values):
        return (rows == values).astype(F32).astype(BF16)

    column_slot = slot_at(iota((columns, 1), 0), half, sides)
    slot = slot_at(iota((1, columns), 1), half, sides)
    mine_ref[...] = (slot == me).astype(F32)
    listing = iota((1, pairs), 1) < live
    pool_hot = hot(iota((listed_ref.shape[0], pairs), 0), pools_ref[...])
    slot_hot = hot(column_slot, jnp.where(listing, slots_ref[...], -1))
    listed_ref[...] = product(pool_hot, slot_hot)

    spread = hot(column_slot, iota((columns, peers), 1))
    tables = notes_ref[:, 0, targets : targets + peers]
    table = table_ref[...].astype(F32)
    wide_tables = product(tables.astype(BF16), spread)
    wide_table = product(table.astype(BF16), spread)
    same_ref[...] = (wide_tables == wide_table).astype(F32)
    spare_ref[...] = (wide_table < 0).astype(F32)

    square = iota((peers, peers), 0), iota((peers, peers), 1)
    asked = jnp.sum(jnp.where(square[1] == me, tables, 0.0), axis=1, keepdims=True)
    block = (iota((peers, targets), 1) // CB).astype(F32)
    own_ref[...] = (asked == block).astype(F32)

    wanted = jnp.sum(jnp.where(square[0] == square[1], table, 0.0), axis=1, keepdims=True)
    masses = jnp.where(wanted == block, notes_ref[:, 0, :targets], 0.0)
    masses = fold(masses)
    slot_mass = [
        jnp.sum(
            jnp.where(
                iota((peers, LANES), 0) == slot_at(iota((peers, LANES), 1) + start, half, sides),
                masses,
                0.0,
            ),
            axis=0,
            keepdims=True,
        )
        for start in range(0, columns, LANES)
    ]
    slot_mass_ref[...] = jnp.concatenate(slot_mass, axis=1)

    diagonal = iota((LANES, LANES), 0) == iota((LANES, LANES), 1)
    for start in range(0, mass_ref.shape[0], LANES):
        row = pool_mass_ref[:, pl.ds(start, LANES)]
        mass_ref[pl.ds(start, LANES), :] = jnp.sum(
            jnp.where(diagonal, row, 0.0), axis=1, keepdims=True
        )


def prepare(place, notes, table, pools, slots, pool_mass, token, pool_count, targets, sides):
    peers = notes.shape[0]
    columns = peers * CB
    shapes = [
        (pool_count, columns),
        (peers, columns),
        (1, columns),
        (1, columns),
        (1, columns),
        (peers, targets),
        (pool_mass.shape[1], 1),
    ]
    return call(
        functools.partial(prepare_kernel, sides),
        "prepare",
        [jax.ShapeDtypeStruct(shape, F32) for shape in shapes],
        [whole(pltpu.SMEM)] + [whole()] * 6,
    )(place, notes, table, pools, slots, pool_mass, token)


def fold(rows):
    folded = rows[:, :LANES]
    for start in range(LANES, rows.shape[1], LANES):
        folded += rows[:, start : start + LANES]
    step = LANES // 2
    while step >= CB:
        folded += pltpu.roll(folded, step, 1)
        step //= 2
    return folded


def send_out(row, out_ref):
    out_ref[...] = jnp.broadcast_to(row[None], out_ref.shape)


def halves(x):
    high = x.astype(BF16)
    return high, (x - high.astype(F32)).astype(BF16)


def assemble_kernel(scale, place_ref, pool_ref, far_ref, listed_ref, mass_ref, *refs):
    near_refs, (kernel_ref, out_ref, near_high, near_low) = refs[:-4], refs[-4:]
    half = len(near_refs)
    me = place_ref[0]
    local = jnp.where(me < half, me, me - half)
    for turn, near_ref in enumerate(near_refs):
        for side in range(2):
            slot = side * half + mate(local, turn, half)
            at = pl.ds(pl.multiple_of(slot * CB, CB), CB)
            near_high[at, :], near_low[at, :] = halves(near_ref[side])
    ahead = near_high.shape[1]
    far_high, far_low = halves(far_ref[...].reshape(kernel_ref.shape[1], -1))
    sums = jnp.zeros((1, kernel_ref.shape[1]), F32)
    rows = 256 if kernel_ref.shape[0] % 256 == 0 else RB

    def scores_of(p, q_high, q_low):
        high, low = halves(p)
        return product(high, q_high) + (product(high, q_low) + product(low, q_high))

    for start in range(0, kernel_ref.shape[0], rows):
        pool = pool_ref[pl.ds(start, rows), :]
        scores = scores_of(pool[:, :ahead], near_high[...], near_low[...])
        scores += scores_of(pool[:, ahead:], far_high, far_low)
        for block in range(rows // RB):
            inner = pl.ds(start + block * RB, RB)
            at = start // RB + block
            listed = listed_ref[at : at + 1, :] > 0
            values = jnp.where(
                listed, jnp.exp(scores[block * RB : (block + 1) * RB] * scale), 0.0
            )
            kernel_ref[inner, :] = values
            scaling = mass_ref[inner, :] / jnp.sum(values, axis=1, keepdims=True)
            sums += jnp.sum(values * scaling, axis=0, keepdims=True)
    send_out(sums, out_ref)


def assemble(place, pool, near, far, listed, mass):
    rows, width = pool.shape
    peers = far.shape[0]
    columns = peers * CB
    ahead = near[0].shape[2]
    return call(
        functools.partial(assemble_kernel, 1.5 / math.sqrt(width)),
        "assemble",
        (
            jax.ShapeDtypeStruct((rows, columns), F32),
            jax.ShapeDtypeStruct((peers, 1, columns), F32),
        ),
        [whole(pltpu.SMEM)] + [whole()] * (4 + len(near)),
        cost=(
            6 * rows * columns * width,
            4 * (rows * width + columns * width + rows * columns),
            rows * columns,
        ),
        scratch_shapes=[pltpu.VMEM((columns, ahead), BF16)] * 2,
    )(place, pool, far, listed, mass, *near)


def iterate_kernel(
    kernel_ref, notes_ref, same_ref, slot_mass_ref, spare_ref, mass_ref, out_ref, *scaling_refs
):
    col_sums = jnp.sum(notes_ref[:, 0, :] * same_ref[...], axis=0, keepdims=True)
    target_scaling = slot_mass_ref[...] / (col_sums + spare_ref[...])
    sums = jnp.zeros_like(target_scaling)
    diagonal = lax.broadcasted_iota(jnp.int32, (LANES, LANES), 0) == lax.broadcasted_iota(
        jnp.int32, (LANES, LANES), 1
    )
    for start in range(0, kernel_ref.shape[0], LANES):
        inner = pl.ds(start, LANES)
        values = kernel_ref[inner, :]
        scaling = mass_ref[inner, :] / jnp.sum(values * target_scaling, axis=1, keepdims=True)
        sums += jnp.sum(values * scaling, axis=0, keepdims=True)
        for scaling_ref in scaling_refs:
            scaling_ref[:, inner] = jnp.sum(
                jnp.where(diagonal, scaling, 0.0), axis=0, keepdims=True
            )
    send_out(sums, out_ref)


def iterate(kernel, notes, same, slot_mass, spare, mass, last):
    rows, columns = kernel.shape
    out_shape = [jax.ShapeDtypeStruct(notes.shape, F32)]
    if last:
        out_shape.append(jax.ShapeDtypeStruct((1, rows), F32))
    return call(
        iterate_kernel,
        "iterate",
        out_shape,
        [whole()] * 6,
        cost=(4 * rows * columns, 4 * rows * columns, 0),
    )(kernel, notes, same, slot_mass, spare, mass)


def finish_kernel(
    notes_ref,
    mine_ref,
    own_ref,
    mass_ref,
    scaling_ref,
    pool_hbm,
    target_hbm,
    pool_ref,
    target_ref,
    sems,
):
    pool_ref[...] = jnp.log(scaling_ref[0])
    pool_copy = pltpu.make_async_copy(pool_ref, pool_hbm, sems.at[0])
    pool_copy.start()
    col_sums = jnp.sum(fold(notes_ref[:, 0, :] * mine_ref[...]) * own_ref[...], axis=0)
    target_ref[...] = jnp.log(mass_ref[...] / col_sums)
    target_copy = pltpu.make_async_copy(target_ref, target_hbm, sems.at[1])
    target_copy.start()
    pool_copy.wait()
    target_copy.wait()


def finish(notes, mine, own, mass, scaling):
    shapes = (scaling.shape[1:], mass.shape)
    return call(
        finish_kernel,
        "finish",
        tuple(jax.ShapeDtypeStruct(shape, F32) for shape in shapes),
        [whole()] * 5,
        (whole(pl.ANY),) * 2,
        scratch_shapes=[pltpu.VMEM(shape, F32) for shape in shapes]
        + [pltpu.SemaphoreType.DMA((2,))],
    )(notes, mine, own, mass, scaling)


def local(
    pool_emb,
    target_emb,
    pool_mass,
    target_mass,
    fetch_table,
    pair_pool,
    listed_pair_slot,
    pair_count,
):
    peers = lax.axis_size("clus")
    me = lax.axis_index("clus").astype(jnp.int32)
    targets, width = target_emb.shape
    pool_count = pool_emb.shape[0] // RB
    columns = peers * CB
    half = peers // 2
    ahead = width // LANES // 3 * LANES

    def trade(x, turn):
        pairs = [
            (side * half + mate(i, turn, half), side * half + i)
            for side in range(2)
            for i in range(half)
        ]
        return lax.ppermute(x, "clus", [pair for pair in pairs if pair[0] != pair[1]])

    blocks = target_emb.reshape(targets // CB, CB, width)
    other = lax.ppermute(
        blocks[:, :, :ahead], "clus", [(i, (i + half) % peers) for i in range(peers)]
    )
    note, held = make_note(target_mass[None], fetch_table, blocks)
    notes = lax.cond(me < peers, exchange, jnp.zeros_like, note)
    far, token, near = pick_blocks(me[None], notes, held, other)
    far = exchange(far)
    near = [near[0]] + [trade(x, turn) for turn, x in enumerate(near[1:], 1)]
    place = jnp.concatenate([me[None], pair_count])
    listed, same, spare, slot_mass, mine, own, mass = prepare(
        place,
        notes,
        fetch_table,
        pair_pool,
        listed_pair_slot,
        pool_mass[None],
        token,
        pool_count,
        targets,
        1,
    )

    kernel, sums = assemble(place, pool_emb, near, far, listed, mass)
    for step in range(1, ITERS):
        sums, *scalings = iterate(
            kernel, exchange(sums), same, slot_mass, spare, mass, step == ITERS - 1
        )
    return finish(exchange(sums), mine, own, target_mass, scalings[0])


def solution(mesh):
    return jax.shard_map(
        local,
        mesh=mesh,
        in_specs=(
            P(("groups", "clus"), None),
            P(("groups", "clus"), None),
            P(("groups", "clus")),
            P(("groups", "clus")),
            P(("groups", "clus"), None),
            P(("groups", "clus"), None),
            P(("groups", "clus"), None),
            P(("groups", "clus")),
        ),
        out_specs=(P(("groups", "clus")), P(("groups", "clus"))),
        check_vma=False,
    )
```

```python
import functools
import math

import jax
import jax.numpy as jnp
from jax import lax
from jax.experimental import pallas as pl
from jax.experimental.pallas import tpu as pltpu
from jax.sharding import PartitionSpec as P

RB = 64
CB = 16
ITERS = 3
LANES = 128
VMEM_LIMIT = 48 * 1024 * 1024

F32 = jnp.float32
BF16 = jnp.bfloat16


def whole(space=pltpu.VMEM):
    return pl.BlockSpec(memory_space=space)


def call(kernel, name, out_shape, in_specs, out_specs=None, cost=(0, 0, 0), scratch_shapes=(), limit=VMEM_LIMIT):
    flops, bytes_accessed, transcendentals = cost
    return pl.pallas_call(
        kernel,
        name=name,
        out_shape=out_shape,
        in_specs=in_specs,
        out_specs=jax.tree.map(lambda _: whole(), out_shape) if out_specs is None else out_specs,
        scratch_shapes=scratch_shapes,
        cost_estimate=pl.CostEstimate(
            flops=flops, bytes_accessed=bytes_accessed, transcendentals=transcendentals
        ),
        compiler_params=pltpu.CompilerParams(vmem_limit_bytes=limit),
    )


def exchange(rows, groups=None):
    return lax.all_to_all(
        rows, "clus", split_axis=0, concat_axis=0, tiled=True, axis_index_groups=groups
    )


def mate(local, turn, half):
    if half & (half - 1) == 0:
        return local ^ turn
    return (turn + half - local) % half


def note_kernel(mass_hbm, table_hbm, out_ref, mass_ref, table_ref, sems):
    copies = [
        pltpu.make_async_copy(mass_hbm, mass_ref, sems.at[0]),
        pltpu.make_async_copy(table_hbm, table_ref, sems.at[1]),
    ]
    for copy in copies:
        copy.start()
    for copy in copies:
        copy.wait()
    targets, peers = mass_ref.shape[1], table_ref.shape[1]
    shape = (out_ref.shape[0], 1)
    out_ref[:, :, :targets] = jnp.broadcast_to(mass_ref[...][None], shape + (targets,))
    out_ref[:, :, targets:] = jnp.zeros(shape + (out_ref.shape[2] - targets,), F32)
    out_ref[:, :, targets : targets + peers] = jnp.broadcast_to(
        table_ref[...].astype(F32)[None], shape + (peers,)
    )


def make_note(mass, table):
    peers = table.shape[1]
    length = mass.shape[1] + -(-peers // LANES) * LANES
    return call(
        note_kernel,
        "make_note",
        jax.ShapeDtypeStruct((peers, 1, length), F32),
        [whole(pltpu.HBM)] * 2,
        scratch_shapes=[
            pltpu.VMEM(mass.shape, F32),
            pltpu.VMEM(table.shape, jnp.int32),
            pltpu.SemaphoreType.DMA((2,)),
        ],
        limit=None,
    )(mass, table)


def pick_kernel(half, place_ref, notes_ref, own_hbm, other_ref, far_ref, token_ref, *refs):
    near_refs, refs = refs[:half], refs[half:]
    asked_ref, own_ref, near_held, far_held, own_sem, near_sems, far_sems = refs
    own_copy = pltpu.make_async_copy(own_hbm, own_ref, own_sem)
    own_copy.start()
    peers = far_ref.shape[0]
    count, _, width = own_ref.shape
    ahead = other_ref.shape[2]
    first = notes_ref.shape[2] - -(-peers // LANES) * LANES
    me = place_ref[0]
    side = me // half
    tables = notes_ref[:, 0, first:]
    lane = lax.broadcasted_iota(jnp.int32, tables.shape, 1)
    for turn, owner in enumerate((me, jnp.where(side == 0, me + half, me - half))):
        asked = jnp.sum(jnp.where(lane == owner, tables, 0.0), axis=1, keepdims=True)
        asked_ref[turn] = jnp.broadcast_to(asked, asked_ref.shape[1:])

    def select(emb_ref, wanted, columns):
        block = emb_ref[0, :, columns]
        for t in range(1, count):
            block = jnp.where(wanted == t, emb_ref[t, :, columns], block)
        return block

    def wanted_of(turn, d):
        return jnp.broadcast_to(asked_ref[turn, pl.ds(d, 1), :], (CB, LANES))

    def near_copy(turn):
        return pltpu.make_async_copy(near_held.at[turn], near_refs[turn], near_sems.at[turn])

    def far_copy(d):
        return pltpu.make_async_copy(far_held.at[d], far_ref.at[d], far_sems.at[d])

    def pick_far(d):
        wanted = wanted_of(0, d)
        for start in range(ahead, width, LANES):
            far_held[d, :, start - ahead : start - ahead + LANES] = select(
                own_ref, wanted, pl.ds(start, LANES)
            )
        far_copy(d).start()

    def pick_near(turn, emb_ref, source):
        reader = side * half + mate(me - side * half, turn, half)
        at = side if source == 0 else 1 - side
        wanted = wanted_of(source, reader)
        for start in range(0, ahead, LANES):
            columns = pl.ds(start, LANES)
            near_held[turn, at, :, columns] = select(emb_ref, wanted, columns)

    for turn in range(half):
        pick_near(turn, other_ref, 1)
    own_copy.wait()
    if peers <= 16:
        for d in range(peers):
            pick_far(d)
    else:
        pl.loop(0, peers)(pick_far)
    for turn in range(half):
        pick_near(turn, own_ref, 0)
        near_copy(turn).start()
    token_ref[...] = jnp.zeros_like(token_ref)

    @pl.loop(0, peers)
    def _(d):
        far_copy(d).wait()

    for turn in range(half):
        near_copy(turn).wait()


def pick_blocks(me, notes, own, other):
    peers = notes.shape[0]
    half = peers // 2
    ahead = other.shape[2]
    near = (2, CB, ahead)
    far = (peers, CB, own.shape[2] - ahead)
    far, token, *near = call(
        functools.partial(pick_kernel, half),
        "pick_blocks",
        [jax.ShapeDtypeStruct(shape, F32) for shape in [far, (8, LANES)] + [near] * half],
        [whole(pltpu.SMEM), whole(), whole(pltpu.HBM), whole()],
        [whole(pl.ANY), whole()] + [whole(pl.ANY)] * half,
        scratch_shapes=[
            pltpu.VMEM((2, peers, LANES), F32),
            pltpu.VMEM(own.shape, F32),
            pltpu.VMEM((half,) + near, F32),
            pltpu.VMEM(far, F32),
            pltpu.SemaphoreType.DMA,
            pltpu.SemaphoreType.DMA((half,)),
            pltpu.SemaphoreType.DMA((peers,)),
        ],
        limit=None,
    )(me, notes, own, other)
    return far, token, near


def iota(shape, dimension):
    return lax.broadcasted_iota(jnp.int32, shape, dimension)


def slot_at(column, half, sides):
    block = column // CB
    return block % sides * half + block // sides


def product(a, b):
    return lax.dot_general(a, b, (((1,), (1,)), ((), ())), preferred_element_type=F32)


def prepare_kernel(
    sides,
    place_ref,
    notes_ref,
    table_ref,
    pools_ref,
    slots_ref,
    pool_mass_ref,
    _,
    listed_ref,
    same_ref,
    spare_ref,
    slot_mass_ref,
    mine_ref,
    own_ref,
    mass_ref,
):
    me, live = place_ref[0], place_ref[1]
    peers, columns = own_ref.shape[0], listed_ref.shape[1]
    half = peers // sides
    targets = own_ref.shape[1]
    pairs = pools_ref.shape[1]

    def hot(rows, values):
        return (rows == values).astype(F32).astype(BF16)

    column_slot = slot_at(iota((columns, 1), 0), half, sides)
    slot = slot_at(iota((1, columns), 1), half, sides)
    mine_ref[...] = (slot == me).astype(F32)
    listing = iota((1, pairs), 1) < live
    pool_hot = hot(iota((listed_ref.shape[0], pairs), 0), pools_ref[...])
    slot_hot = hot(column_slot, jnp.where(listing, slots_ref[...], -1))
    listed_ref[...] = product(pool_hot, slot_hot)

    spread = hot(column_slot, iota((columns, peers), 1))
    tables = notes_ref[:, 0, targets : targets + peers]
    table = table_ref[...].astype(F32)
    wide_tables = product(tables.astype(BF16), spread)
    wide_table = product(table.astype(BF16), spread)
    same_ref[...] = (wide_tables == wide_table).astype(F32)
    spare_ref[...] = (wide_table < 0).astype(F32)

    square = iota((peers, peers), 0), iota((peers, peers), 1)
    asked = jnp.sum(jnp.where(square[1] == me, tables, 0.0), axis=1, keepdims=True)
    block = (iota((peers, targets), 1) // CB).astype(F32)
    own_ref[...] = (asked == block).astype(F32)

    wanted = jnp.sum(jnp.where(square[0] == square[1], table, 0.0), axis=1, keepdims=True)
    masses = jnp.where(wanted == block, notes_ref[:, 0, :targets], 0.0)
    masses = fold(masses)
    slot_mass = [
        jnp.sum(
            jnp.where(
                iota((peers, LANES), 0) == slot_at(iota((peers, LANES), 1) + start, half, sides),
                masses,
                0.0,
            ),
            axis=0,
            keepdims=True,
        )
        for start in range(0, columns, LANES)
    ]
    slot_mass_ref[...] = jnp.concatenate(slot_mass, axis=1)

    diagonal = iota((LANES, LANES), 0) == iota((LANES, LANES), 1)
    for start in range(0, mass_ref.shape[0], LANES):
        row = pool_mass_ref[:, pl.ds(start, LANES)]
        mass_ref[pl.ds(start, LANES), :] = jnp.sum(
            jnp.where(diagonal, row, 0.0), axis=1, keepdims=True
        )


def prepare(place, notes, table, pools, slots, pool_mass, token, pool_count, targets, sides):
    peers = notes.shape[0]
    columns = peers * CB
    shapes = [
        (pool_count, columns),
        (peers, columns),
        (1, columns),
        (1, columns),
        (1, columns),
        (peers, targets),
        (pool_mass.shape[1], 1),
    ]
    return call(
        functools.partial(prepare_kernel, sides),
        "prepare",
        [jax.ShapeDtypeStruct(shape, F32) for shape in shapes],
        [whole(pltpu.SMEM)] + [whole()] * 6,
    )(place, notes, table, pools, slots, pool_mass, token)


def fold(rows):
    folded = rows[:, :LANES]
    for start in range(LANES, rows.shape[1], LANES):
        folded += rows[:, start : start + LANES]
    step = LANES // 2
    while step >= CB:
        folded += pltpu.roll(folded, step, 1)
        step //= 2
    return folded


def send_out(row, out_ref):
    out_ref[...] = jnp.broadcast_to(row[None], out_ref.shape)


def halves(x):
    high = x.astype(BF16)
    return high, (x - high.astype(F32)).astype(BF16)


def assemble_kernel(scale, place_ref, pool_ref, far_ref, listed_ref, mass_ref, *refs):
    near_refs, (kernel_ref, out_ref, near_high, near_low) = refs[:-4], refs[-4:]
    half = len(near_refs)
    me = place_ref[0]
    local = jnp.where(me < half, me, me - half)
    for turn, near_ref in enumerate(near_refs):
        for side in range(2):
            slot = side * half + mate(local, turn, half)
            at = pl.ds(pl.multiple_of(slot * CB, CB), CB)
            near_high[at, :], near_low[at, :] = halves(near_ref[side])
    ahead = near_high.shape[1]
    far_high, far_low = halves(far_ref[...].reshape(kernel_ref.shape[1], -1))
    sums = jnp.zeros((1, kernel_ref.shape[1]), F32)
    rows = 256 if kernel_ref.shape[0] % 256 == 0 else RB

    def scores_of(p, q_high, q_low):
        high, low = halves(p)
        return product(high, q_high) + (product(high, q_low) + product(low, q_high))

    for start in range(0, kernel_ref.shape[0], rows):
        pool = pool_ref[pl.ds(start, rows), :]
        scores = scores_of(pool[:, :ahead], near_high[...], near_low[...])
        scores += scores_of(pool[:, ahead:], far_high, far_low)
        for block in range(rows // RB):
            inner = pl.ds(start + block * RB, RB)
            at = start // RB + block
            listed = listed_ref[at : at + 1, :] > 0
            values = jnp.where(
                listed, jnp.exp(scores[block * RB : (block + 1) * RB] * scale), 0.0
            )
            kernel_ref[inner, :] = values
            scaling = mass_ref[inner, :] / jnp.sum(values, axis=1, keepdims=True)
            sums += jnp.sum(values * scaling, axis=0, keepdims=True)
    send_out(sums, out_ref)


def assemble(place, pool, near, far, listed, mass):
    rows, width = pool.shape
    peers = far.shape[0]
    columns = peers * CB
    ahead = near[0].shape[2]
    return call(
        functools.partial(assemble_kernel, 1.5 / math.sqrt(width)),
        "assemble",
        (
            jax.ShapeDtypeStruct((rows, columns), F32),
            jax.ShapeDtypeStruct((peers, 1, columns), F32),
        ),
        [whole(pltpu.SMEM)] + [whole()] * (4 + len(near)),
        cost=(
            6 * rows * columns * width,
            4 * (rows * width + columns * width + rows * columns),
            rows * columns,
        ),
        scratch_shapes=[pltpu.VMEM((columns, ahead), BF16)] * 2,
    )(place, pool, far, listed, mass, *near)


def iterate_kernel(
    kernel_ref, notes_ref, same_ref, slot_mass_ref, spare_ref, mass_ref, out_ref, *scaling_refs
):
    col_sums = jnp.sum(notes_ref[:, 0, :] * same_ref[...], axis=0, keepdims=True)
    target_scaling = slot_mass_ref[...] / (col_sums + spare_ref[...])
    sums = jnp.zeros_like(target_scaling)
    diagonal = lax.broadcasted_iota(jnp.int32, (LANES, LANES), 0) == lax.broadcasted_iota(
        jnp.int32, (LANES, LANES), 1
    )
    for start in range(0, kernel_ref.shape[0], LANES):
        inner = pl.ds(start, LANES)
        values = kernel_ref[inner, :]
        scaling = mass_ref[inner, :] / jnp.sum(values * target_scaling, axis=1, keepdims=True)
        sums += jnp.sum(values * scaling, axis=0, keepdims=True)
        for scaling_ref in scaling_refs:
            scaling_ref[:, inner] = jnp.sum(
                jnp.where(diagonal, scaling, 0.0), axis=0, keepdims=True
            )
    send_out(sums, out_ref)


def iterate(kernel, notes, same, slot_mass, spare, mass, last):
    rows, columns = kernel.shape
    out_shape = [jax.ShapeDtypeStruct(notes.shape, F32)]
    if last:
        out_shape.append(jax.ShapeDtypeStruct((1, rows), F32))
    return call(
        iterate_kernel,
        "iterate",
        out_shape,
        [whole()] * 6,
        cost=(4 * rows * columns, 4 * rows * columns, 0),
    )(kernel, notes, same, slot_mass, spare, mass)


def finish_kernel(
    notes_ref,
    mine_ref,
    own_ref,
    mass_ref,
    scaling_ref,
    pool_hbm,
    target_hbm,
    pool_ref,
    target_ref,
    sems,
):
    pool_ref[...] = jnp.log(scaling_ref[0])
    pool_copy = pltpu.make_async_copy(pool_ref, pool_hbm, sems.at[0])
    pool_copy.start()
    col_sums = jnp.sum(fold(notes_ref[:, 0, :] * mine_ref[...]) * own_ref[...], axis=0)
    target_ref[...] = jnp.log(mass_ref[...] / col_sums)
    target_copy = pltpu.make_async_copy(target_ref, target_hbm, sems.at[1])
    target_copy.start()
    pool_copy.wait()
    target_copy.wait()


def finish(notes, mine, own, mass, scaling):
    shapes = (scaling.shape[1:], mass.shape)
    return call(
        finish_kernel,
        "finish",
        tuple(jax.ShapeDtypeStruct(shape, F32) for shape in shapes),
        [whole()] * 5,
        (whole(pl.ANY),) * 2,
        scratch_shapes=[pltpu.VMEM(shape, F32) for shape in shapes]
        + [pltpu.SemaphoreType.DMA((2,))],
    )(notes, mine, own, mass, scaling)


def local(
    pool_emb,
    target_emb,
    pool_mass,
    target_mass,
    fetch_table,
    pair_pool,
    listed_pair_slot,
    pair_count,
):
    peers = lax.axis_size("clus")
    me = lax.axis_index("clus").astype(jnp.int32)
    targets, width = target_emb.shape
    pool_count = pool_emb.shape[0] // RB
    columns = peers * CB
    half = peers // 2
    ahead = width // LANES // 2 * LANES

    def trade(x, turn):
        pairs = [
            (side * half + mate(i, turn, half), side * half + i)
            for side in range(2)
            for i in range(half)
        ]
        return lax.ppermute(x, "clus", [pair for pair in pairs if pair[0] != pair[1]])

    blocks = target_emb.reshape(targets // CB, CB, width)
    other = lax.ppermute(
        blocks[:, :, :ahead], "clus", [(i, (i + half) % peers) for i in range(peers)]
    )
    note = make_note(target_mass[None], fetch_table)
    notes = lax.cond(me < peers, exchange, jnp.zeros_like, note)
    far, token, near = pick_blocks(me[None], notes, blocks, other)
    far = exchange(far)
    near = [near[0]] + [trade(x, turn) for turn, x in enumerate(near[1:], 1)]
    place = jnp.concatenate([me[None], pair_count])
    listed, same, spare, slot_mass, mine, own, mass = prepare(
        place,
        notes,
        fetch_table,
        pair_pool,
        listed_pair_slot,
        pool_mass[None],
        token,
        pool_count,
        targets,
        1,
    )

    kernel, sums = assemble(place, pool_emb, near, far, listed, mass)
    for step in range(1, ITERS):
        sums, *scalings = iterate(
            kernel, exchange(sums), same, slot_mass, spare, mass, step == ITERS - 1
        )
    return finish(exchange(sums), mine, own, target_mass, scalings[0])


def solution(mesh):
    return jax.shard_map(
        local,
        mesh=mesh,
        in_specs=(
            P(("groups", "clus"), None),
            P(("groups", "clus"), None),
            P(("groups", "clus")),
            P(("groups", "clus")),
            P(("groups", "clus"), None),
            P(("groups", "clus"), None),
            P(("groups", "clus"), None),
            P(("groups", "clus")),
        ),
        out_specs=(P(("groups", "clus")), P(("groups", "clus"))),
        check_vma=False,
    )
```

```python
import functools
import math

import jax
import jax.numpy as jnp
from jax import lax
from jax.experimental import pallas as pl
from jax.experimental.pallas import tpu as pltpu
from jax.sharding import PartitionSpec as P

RB = 64
CB = 16
ITERS = 3
LANES = 128
VMEM_LIMIT = 48 * 1024 * 1024

F32 = jnp.float32
BF16 = jnp.bfloat16


def whole(space=pltpu.VMEM):
    return pl.BlockSpec(memory_space=space)


def call(kernel, name, out_shape, in_specs, out_specs=None, cost=(0, 0, 0), scratch_shapes=(), limit=VMEM_LIMIT):
    flops, bytes_accessed, transcendentals = cost
    return pl.pallas_call(
        kernel,
        name=name,
        out_shape=out_shape,
        in_specs=in_specs,
        out_specs=jax.tree.map(lambda _: whole(), out_shape) if out_specs is None else out_specs,
        scratch_shapes=scratch_shapes,
        cost_estimate=pl.CostEstimate(
            flops=flops, bytes_accessed=bytes_accessed, transcendentals=transcendentals
        ),
        compiler_params=pltpu.CompilerParams(vmem_limit_bytes=limit),
    )


def exchange(rows, groups=None):
    return lax.all_to_all(
        rows, "clus", split_axis=0, concat_axis=0, tiled=True, axis_index_groups=groups
    )


def mate(local, turn, half):
    if half & (half - 1) == 0:
        return local ^ turn
    return (turn + half - local) % half


def note_kernel(mass_hbm, table_hbm, out_ref, mass_ref, table_ref, sems):
    copies = [
        pltpu.make_async_copy(mass_hbm, mass_ref, sems.at[0]),
        pltpu.make_async_copy(table_hbm, table_ref, sems.at[1]),
    ]
    for copy in copies:
        copy.start()
    for copy in copies:
        copy.wait()
    targets, peers = mass_ref.shape[1], table_ref.shape[1]
    shape = (out_ref.shape[0], 1)
    out_ref[:, :, :targets] = jnp.broadcast_to(mass_ref[...][None], shape + (targets,))
    out_ref[:, :, targets:] = jnp.zeros(shape + (out_ref.shape[2] - targets,), F32)
    out_ref[:, :, targets : targets + peers] = jnp.broadcast_to(
        table_ref[...].astype(F32)[None], shape + (peers,)
    )


def make_note(mass, table):
    peers = table.shape[1]
    length = mass.shape[1] + -(-peers // LANES) * LANES
    return call(
        note_kernel,
        "make_note",
        jax.ShapeDtypeStruct((peers, 1, length), F32),
        [whole(pltpu.HBM)] * 2,
        scratch_shapes=[
            pltpu.VMEM(mass.shape, F32),
            pltpu.VMEM(table.shape, jnp.int32),
            pltpu.SemaphoreType.DMA((2,)),
        ],
        limit=None,
    )(mass, table)


def cut_kernel(x_ref, held_ref, ahead_ref):
    held_ref[...] = x_ref[...]
    ahead_ref[...] = x_ref[:, :, : ahead_ref.shape[2]]


def cut(blocks, ahead):
    return call(
        cut_kernel,
        "cut",
        (
            jax.ShapeDtypeStruct(blocks.shape, F32),
            jax.ShapeDtypeStruct(blocks.shape[:2] + (ahead,), F32),
        ),
        [whole()],
    )(blocks)


def pick_kernel(half, place_ref, notes_ref, own_ref, other_ref, far_ref, token_ref, *refs):
    near_refs, (asked_ref, near_held, far_held, near_sems, far_sems) = refs[:half], refs[half:]
    peers = far_ref.shape[0]
    count, _, width = own_ref.shape
    ahead = other_ref.shape[2]
    first = notes_ref.shape[2] - -(-peers // LANES) * LANES
    me = place_ref[0]
    side = me // half
    tables = notes_ref[:, 0, first:]
    lane = lax.broadcasted_iota(jnp.int32, tables.shape, 1)
    for turn, owner in enumerate((me, jnp.where(side == 0, me + half, me - half))):
        asked = jnp.sum(jnp.where(lane == owner, tables, 0.0), axis=1, keepdims=True)
        asked_ref[turn] = jnp.broadcast_to(asked, asked_ref.shape[1:])

    def select(emb_ref, wanted, columns):
        block = emb_ref[0, :, columns]
        for t in range(1, count):
            block = jnp.where(wanted == t, emb_ref[t, :, columns], block)
        return block

    def wanted_of(turn, d):
        return jnp.broadcast_to(asked_ref[turn, pl.ds(d, 1), :], (CB, LANES))

    def near_copy(turn):
        return pltpu.make_async_copy(near_held.at[turn], near_refs[turn], near_sems.at[turn])

    def far_copy(d):
        return pltpu.make_async_copy(far_held.at[d], far_ref.at[d], far_sems.at[d])

    def pick_far(d):
        wanted = wanted_of(0, d)
        for start in range(ahead, width, LANES):
            far_held[d, :, start - ahead : start - ahead + LANES] = select(
                own_ref, wanted, pl.ds(start, LANES)
            )
        far_copy(d).start()

    if peers <= 16:
        for d in range(peers):
            pick_far(d)
    else:
        pl.loop(0, peers)(pick_far)
    for turn in range(half):
        reader = side * half + mate(me - side * half, turn, half)
        for source, emb_ref in enumerate((own_ref, other_ref)):
            at = side if source == 0 else 1 - side
            wanted = wanted_of(source, reader)

            @pl.loop(0, ahead // LANES)
            def _(part):
                columns = pl.ds(pl.multiple_of(part * LANES, LANES), LANES)
                near_held[turn, at, :, columns] = select(emb_ref, wanted, columns)

        near_copy(turn).start()
    token_ref[...] = jnp.zeros_like(token_ref)

    @pl.loop(0, peers)
    def _(d):
        far_copy(d).wait()

    for turn in range(half):
        near_copy(turn).wait()


def pick_blocks(me, notes, own, other):
    peers = notes.shape[0]
    half = peers // 2
    ahead = other.shape[2]
    near = (2, CB, ahead)
    far = (peers, CB, own.shape[2] - ahead)
    far, token, *near = call(
        functools.partial(pick_kernel, half),
        "pick_blocks",
        [jax.ShapeDtypeStruct(shape, F32) for shape in [far, (8, LANES)] + [near] * half],
        [whole(pltpu.SMEM)] + [whole()] * 3,
        [whole(pl.ANY), whole()] + [whole(pl.ANY)] * half,
        scratch_shapes=[
            pltpu.VMEM((2, peers, LANES), F32),
            pltpu.VMEM((half,) + near, F32),
            pltpu.VMEM(far, F32),
            pltpu.SemaphoreType.DMA((half,)),
            pltpu.SemaphoreType.DMA((peers,)),
        ],
    )(me, notes, own, other)
    return far, token, near


def iota(shape, dimension):
    return lax.broadcasted_iota(jnp.int32, shape, dimension)


def slot_at(column, half, sides):
    block = column // CB
    return block % sides * half + block // sides


def product(a, b):
    return lax.dot_general(a, b, (((1,), (1,)), ((), ())), preferred_element_type=F32)


def prepare_kernel(
    sides,
    place_ref,
    notes_ref,
    table_ref,
    pools_ref,
    slots_ref,
    pool_mass_ref,
    _,
    listed_ref,
    same_ref,
    spare_ref,
    slot_mass_ref,
    mine_ref,
    own_ref,
    mass_ref,
):
    me, live = place_ref[0], place_ref[1]
    peers, columns = own_ref.shape[0], listed_ref.shape[1]
    half = peers // sides
    targets = own_ref.shape[1]
    pairs = pools_ref.shape[1]

    def hot(rows, values):
        return (rows == values).astype(F32).astype(BF16)

    column_slot = slot_at(iota((columns, 1), 0), half, sides)
    slot = slot_at(iota((1, columns), 1), half, sides)
    mine_ref[...] = (slot == me).astype(F32)
    listing = iota((1, pairs), 1) < live
    pool_hot = hot(iota((listed_ref.shape[0], pairs), 0), pools_ref[...])
    slot_hot = hot(column_slot, jnp.where(listing, slots_ref[...], -1))
    listed_ref[...] = product(pool_hot, slot_hot)

    spread = hot(column_slot, iota((columns, peers), 1))
    tables = notes_ref[:, 0, targets : targets + peers]
    table = table_ref[...].astype(F32)
    wide_tables = product(tables.astype(BF16), spread)
    wide_table = product(table.astype(BF16), spread)
    same_ref[...] = (wide_tables == wide_table).astype(F32)
    spare_ref[...] = (wide_table < 0).astype(F32)

    square = iota((peers, peers), 0), iota((peers, peers), 1)
    asked = jnp.sum(jnp.where(square[1] == me, tables, 0.0), axis=1, keepdims=True)
    block = (iota((peers, targets), 1) // CB).astype(F32)
    own_ref[...] = (asked == block).astype(F32)

    wanted = jnp.sum(jnp.where(square[0] == square[1], table, 0.0), axis=1, keepdims=True)
    masses = jnp.where(wanted == block, notes_ref[:, 0, :targets], 0.0)
    masses = fold(masses)
    slot_mass = [
        jnp.sum(
            jnp.where(
                iota((peers, LANES), 0) == slot_at(iota((peers, LANES), 1) + start, half, sides),
                masses,
                0.0,
            ),
            axis=0,
            keepdims=True,
        )
        for start in range(0, columns, LANES)
    ]
    slot_mass_ref[...] = jnp.concatenate(slot_mass, axis=1)

    diagonal = iota((LANES, LANES), 0) == iota((LANES, LANES), 1)
    for start in range(0, mass_ref.shape[0], LANES):
        row = pool_mass_ref[:, pl.ds(start, LANES)]
        mass_ref[pl.ds(start, LANES), :] = jnp.sum(
            jnp.where(diagonal, row, 0.0), axis=1, keepdims=True
        )


def prepare(place, notes, table, pools, slots, pool_mass, token, pool_count, targets, sides):
    peers = notes.shape[0]
    columns = peers * CB
    shapes = [
        (pool_count, columns),
        (peers, columns),
        (1, columns),
        (1, columns),
        (1, columns),
        (peers, targets),
        (pool_mass.shape[1], 1),
    ]
    return call(
        functools.partial(prepare_kernel, sides),
        "prepare",
        [jax.ShapeDtypeStruct(shape, F32) for shape in shapes],
        [whole(pltpu.SMEM)] + [whole()] * 6,
    )(place, notes, table, pools, slots, pool_mass, token)


def fold(rows):
    folded = rows[:, :LANES]
    for start in range(LANES, rows.shape[1], LANES):
        folded += rows[:, start : start + LANES]
    step = LANES // 2
    while step >= CB:
        folded += pltpu.roll(folded, step, 1)
        step //= 2
    return folded


def send_out(row, out_ref):
    out_ref[...] = jnp.broadcast_to(row[None], out_ref.shape)


def halves(x):
    high = x.astype(BF16)
    return high, (x - high.astype(F32)).astype(BF16)


def assemble_kernel(scale, place_ref, pool_ref, far_ref, listed_ref, mass_ref, *refs):
    near_refs, (kernel_ref, out_ref, near_high, near_low) = refs[:-4], refs[-4:]
    half = len(near_refs)
    me = place_ref[0]
    local = jnp.where(me < half, me, me - half)
    for turn, near_ref in enumerate(near_refs):
        for side in range(2):
            slot = side * half + mate(local, turn, half)
            at = pl.ds(pl.multiple_of(slot * CB, CB), CB)
            near_high[at, :], near_low[at, :] = halves(near_ref[side])
    ahead = near_high.shape[1]
    far_high, far_low = halves(far_ref[...].reshape(kernel_ref.shape[1], -1))
    sums = jnp.zeros((1, kernel_ref.shape[1]), F32)
    rows = 256 if kernel_ref.shape[0] % 256 == 0 else RB

    def scores_of(p, q_high, q_low):
        high, low = halves(p)
        return product(high, q_high) + (product(high, q_low) + product(low, q_high))

    for start in range(0, kernel_ref.shape[0], rows):
        pool = pool_ref[pl.ds(start, rows), :]
        scores = scores_of(pool[:, :ahead], near_high[...], near_low[...])
        scores += scores_of(pool[:, ahead:], far_high, far_low)
        for block in range(rows // RB):
            inner = pl.ds(start + block * RB, RB)
            at = start // RB + block
            listed = listed_ref[at : at + 1, :] > 0
            values = jnp.where(
                listed, jnp.exp(scores[block * RB : (block + 1) * RB] * scale), 0.0
            )
            kernel_ref[inner, :] = values
            scaling = mass_ref[inner, :] / jnp.sum(values, axis=1, keepdims=True)
            sums += jnp.sum(values * scaling, axis=0, keepdims=True)
    send_out(sums, out_ref)


def assemble(place, pool, near, far, listed, mass):
    rows, width = pool.shape
    peers = far.shape[0]
    columns = peers * CB
    ahead = near[0].shape[2]
    return call(
        functools.partial(assemble_kernel, 1.5 / math.sqrt(width)),
        "assemble",
        (
            jax.ShapeDtypeStruct((rows, columns), F32),
            jax.ShapeDtypeStruct((peers, 1, columns), F32),
        ),
        [whole(pltpu.SMEM)] + [whole()] * (4 + len(near)),
        cost=(
            6 * rows * columns * width,
            4 * (rows * width + columns * width + rows * columns),
            rows * columns,
        ),
        scratch_shapes=[pltpu.VMEM((columns, ahead), BF16)] * 2,
    )(place, pool, far, listed, mass, *near)


def iterate_kernel(
    kernel_ref, notes_ref, same_ref, slot_mass_ref, spare_ref, mass_ref, out_ref, *scaling_refs
):
    col_sums = jnp.sum(notes_ref[:, 0, :] * same_ref[...], axis=0, keepdims=True)
    target_scaling = slot_mass_ref[...] / (col_sums + spare_ref[...])
    sums = jnp.zeros_like(target_scaling)
    diagonal = lax.broadcasted_iota(jnp.int32, (LANES, LANES), 0) == lax.broadcasted_iota(
        jnp.int32, (LANES, LANES), 1
    )
    for start in range(0, kernel_ref.shape[0], LANES):
        inner = pl.ds(start, LANES)
        values = kernel_ref[inner, :]
        scaling = mass_ref[inner, :] / jnp.sum(values * target_scaling, axis=1, keepdims=True)
        sums += jnp.sum(values * scaling, axis=0, keepdims=True)
        for scaling_ref in scaling_refs:
            scaling_ref[:, inner] = jnp.sum(
                jnp.where(diagonal, scaling, 0.0), axis=0, keepdims=True
            )
    send_out(sums, out_ref)


def iterate(kernel, notes, same, slot_mass, spare, mass, last):
    rows, columns = kernel.shape
    out_shape = [jax.ShapeDtypeStruct(notes.shape, F32)]
    if last:
        out_shape.append(jax.ShapeDtypeStruct((1, rows), F32))
    return call(
        iterate_kernel,
        "iterate",
        out_shape,
        [whole()] * 6,
        cost=(4 * rows * columns, 4 * rows * columns, 0),
    )(kernel, notes, same, slot_mass, spare, mass)


def finish_kernel(
    notes_ref,
    mine_ref,
    own_ref,
    mass_ref,
    scaling_ref,
    pool_hbm,
    target_hbm,
    pool_ref,
    target_ref,
    sems,
):
    pool_ref[...] = jnp.log(scaling_ref[0])
    pool_copy = pltpu.make_async_copy(pool_ref, pool_hbm, sems.at[0])
    pool_copy.start()
    col_sums = jnp.sum(fold(notes_ref[:, 0, :] * mine_ref[...]) * own_ref[...], axis=0)
    target_ref[...] = jnp.log(mass_ref[...] / col_sums)
    target_copy = pltpu.make_async_copy(target_ref, target_hbm, sems.at[1])
    target_copy.start()
    pool_copy.wait()
    target_copy.wait()


def finish(notes, mine, own, mass, scaling):
    shapes = (scaling.shape[1:], mass.shape)
    return call(
        finish_kernel,
        "finish",
        tuple(jax.ShapeDtypeStruct(shape, F32) for shape in shapes),
        [whole()] * 5,
        (whole(pl.ANY),) * 2,
        scratch_shapes=[pltpu.VMEM(shape, F32) for shape in shapes]
        + [pltpu.SemaphoreType.DMA((2,))],
    )(notes, mine, own, mass, scaling)


def local(
    pool_emb,
    target_emb,
    pool_mass,
    target_mass,
    fetch_table,
    pair_pool,
    listed_pair_slot,
    pair_count,
):
    peers = lax.axis_size("clus")
    me = lax.axis_index("clus").astype(jnp.int32)
    targets, width = target_emb.shape
    pool_count = pool_emb.shape[0] // RB
    columns = peers * CB
    half = peers // 2
    ahead = width // LANES // 3 * LANES

    def trade(x, turn):
        pairs = [
            (side * half + mate(i, turn, half), side * half + i)
            for side in range(2)
            for i in range(half)
        ]
        return lax.ppermute(x, "clus", [pair for pair in pairs if pair[0] != pair[1]])

    blocks = target_emb.reshape(targets // CB, CB, width)
    held, other = cut(blocks, ahead)
    other = lax.ppermute(other, "clus", [(i, (i + half) % peers) for i in range(peers)])
    note = make_note(target_mass[None], fetch_table)
    notes = lax.cond(me < peers, exchange, jnp.zeros_like, note)
    far, token, near = pick_blocks(me[None], notes, held, other)
    far = exchange(far)
    near = [near[0]] + [trade(x, turn) for turn, x in enumerate(near[1:], 1)]
    place = jnp.concatenate([me[None], pair_count])
    listed, same, spare, slot_mass, mine, own, mass = prepare(
        place,
        notes,
        fetch_table,
        pair_pool,
        listed_pair_slot,
        pool_mass[None],
        token,
        pool_count,
        targets,
        1,
    )

    kernel, sums = assemble(place, pool_emb, near, far, listed, mass)
    for step in range(1, ITERS):
        sums, *scalings = iterate(
            kernel, exchange(sums), same, slot_mass, spare, mass, step == ITERS - 1
        )
    return finish(exchange(sums), mine, own, target_mass, scalings[0])


def solution(mesh):
    return jax.shard_map(
        local,
        mesh=mesh,
        in_specs=(
            P(("groups", "clus"), None),
            P(("groups", "clus"), None),
            P(("groups", "clus")),
            P(("groups", "clus")),
            P(("groups", "clus"), None),
            P(("groups", "clus"), None),
            P(("groups", "clus"), None),
            P(("groups", "clus")),
        ),
        out_specs=(P(("groups", "clus")), P(("groups", "clus"))),
        check_vma=False,
    )
```

```python
import functools
import math

import jax
import jax.numpy as jnp
from jax import lax
from jax.experimental import pallas as pl
from jax.experimental.pallas import tpu as pltpu
from jax.sharding import PartitionSpec as P

RB = 64
CB = 16
ITERS = 3
LANES = 128
VMEM_LIMIT = 48 * 1024 * 1024

F32 = jnp.float32
BF16 = jnp.bfloat16


def whole(space=pltpu.VMEM):
    return pl.BlockSpec(memory_space=space)


def call(kernel, name, out_shape, in_specs, out_specs=None, cost=(0, 0, 0), scratch_shapes=(), limit=VMEM_LIMIT):
    flops, bytes_accessed, transcendentals = cost
    return pl.pallas_call(
        kernel,
        name=name,
        out_shape=out_shape,
        in_specs=in_specs,
        out_specs=jax.tree.map(lambda _: whole(), out_shape) if out_specs is None else out_specs,
        scratch_shapes=scratch_shapes,
        cost_estimate=pl.CostEstimate(
            flops=flops, bytes_accessed=bytes_accessed, transcendentals=transcendentals
        ),
        compiler_params=pltpu.CompilerParams(vmem_limit_bytes=limit),
    )


def exchange(rows, groups=None):
    return lax.all_to_all(
        rows, "clus", split_axis=0, concat_axis=0, tiled=True, axis_index_groups=groups
    )


def mate(local, turn, half):
    if half & (half - 1) == 0:
        return local ^ turn
    return (turn + half - local) % half


def note_kernel(mass_hbm, table_hbm, out_ref, mass_ref, table_ref, sems):
    copies = [
        pltpu.make_async_copy(mass_hbm, mass_ref, sems.at[0]),
        pltpu.make_async_copy(table_hbm, table_ref, sems.at[1]),
    ]
    for copy in copies:
        copy.start()
    for copy in copies:
        copy.wait()
    targets, peers = mass_ref.shape[1], table_ref.shape[1]
    shape = (out_ref.shape[0], 1)
    out_ref[:, :, :targets] = jnp.broadcast_to(mass_ref[...][None], shape + (targets,))
    out_ref[:, :, targets:] = jnp.zeros(shape + (out_ref.shape[2] - targets,), F32)
    out_ref[:, :, targets : targets + peers] = jnp.broadcast_to(
        table_ref[...].astype(F32)[None], shape + (peers,)
    )


def make_note(mass, table):
    peers = table.shape[1]
    length = mass.shape[1] + -(-peers // LANES) * LANES
    return call(
        note_kernel,
        "make_note",
        jax.ShapeDtypeStruct((peers, 1, length), F32),
        [whole(pltpu.HBM)] * 2,
        scratch_shapes=[
            pltpu.VMEM(mass.shape, F32),
            pltpu.VMEM(table.shape, jnp.int32),
            pltpu.SemaphoreType.DMA((2,)),
        ],
        limit=None,
    )(mass, table)


def cut_kernel(x_ref, held_ref, ahead_ref):
    held_ref[...] = x_ref[...]
    ahead_ref[...] = x_ref[:, :, : ahead_ref.shape[2]]


def cut(blocks, ahead):
    return call(
        cut_kernel,
        "cut",
        (
            jax.ShapeDtypeStruct(blocks.shape, F32),
            jax.ShapeDtypeStruct(blocks.shape[:2] + (ahead,), F32),
        ),
        [whole()],
    )(blocks)


def pick_kernel(half, place_ref, notes_ref, own_ref, other_ref, far_ref, token_ref, *refs):
    near_refs, (asked_ref, near_held, far_held, near_sems, far_sems) = refs[:half], refs[half:]
    peers = far_ref.shape[0]
    count, _, width = own_ref.shape
    ahead = other_ref.shape[2]
    first = notes_ref.shape[2] - -(-peers // LANES) * LANES
    me = place_ref[0]
    side = me // half
    tables = notes_ref[:, 0, first:]
    lane = lax.broadcasted_iota(jnp.int32, tables.shape, 1)
    for turn, owner in enumerate((me, jnp.where(side == 0, me + half, me - half))):
        asked = jnp.sum(jnp.where(lane == owner, tables, 0.0), axis=1, keepdims=True)
        asked_ref[turn] = jnp.broadcast_to(asked, asked_ref.shape[1:])

    def select(emb_ref, wanted, columns):
        block = emb_ref[0, :, columns]
        for t in range(1, count):
            block = jnp.where(wanted == t, emb_ref[t, :, columns], block)
        return block

    def wanted_of(turn, d):
        return jnp.broadcast_to(asked_ref[turn, pl.ds(d, 1), :], (CB, LANES))

    def near_copy(turn):
        return pltpu.make_async_copy(near_held.at[turn], near_refs[turn], near_sems.at[turn])

    def far_copy(d):
        return pltpu.make_async_copy(far_held.at[d], far_ref.at[d], far_sems.at[d])

    def pick_far(d):
        wanted = wanted_of(0, d)
        for start in range(ahead, width, LANES):
            far_held[d, :, start - ahead : start - ahead + LANES] = select(
                own_ref, wanted, pl.ds(start, LANES)
            )
        far_copy(d).start()

    if peers <= 16:
        for d in range(peers):
            pick_far(d)
    else:
        pl.loop(0, peers)(pick_far)
    for turn in range(half):
        reader = side * half + mate(me - side * half, turn, half)
        for source, emb_ref in enumerate((own_ref, other_ref)):
            at = side if source == 0 else 1 - side
            wanted = wanted_of(source, reader)

            @pl.loop(0, ahead // LANES)
            def _(part):
                columns = pl.ds(pl.multiple_of(part * LANES, LANES), LANES)
                near_held[turn, at, :, columns] = select(emb_ref, wanted, columns)

        near_copy(turn).start()
    token_ref[...] = jnp.zeros_like(token_ref)

    @pl.loop(0, peers)
    def _(d):
        far_copy(d).wait()

    for turn in range(half):
        near_copy(turn).wait()


def pick_blocks(me, notes, own, other):
    peers = notes.shape[0]
    half = peers // 2
    ahead = other.shape[2]
    near = (2, CB, ahead)
    far = (peers, CB, own.shape[2] - ahead)
    far, token, *near = call(
        functools.partial(pick_kernel, half),
        "pick_blocks",
        [jax.ShapeDtypeStruct(shape, F32) for shape in [far, (8, LANES)] + [near] * half],
        [whole(pltpu.SMEM)] + [whole()] * 3,
        [whole(pl.ANY), whole()] + [whole(pl.ANY)] * half,
        scratch_shapes=[
            pltpu.VMEM((2, peers, LANES), F32),
            pltpu.VMEM((half,) + near, F32),
            pltpu.VMEM(far, F32),
            pltpu.SemaphoreType.DMA((half,)),
            pltpu.SemaphoreType.DMA((peers,)),
        ],
    )(me, notes, own, other)
    return far, token, near


def iota(shape, dimension):
    return lax.broadcasted_iota(jnp.int32, shape, dimension)


def slot_at(column, half, sides):
    block = column // CB
    return block % sides * half + block // sides


def product(a, b):
    return lax.dot_general(a, b, (((1,), (1,)), ((), ())), preferred_element_type=F32)


def prepare_kernel(
    sides,
    place_ref,
    notes_ref,
    table_ref,
    pools_ref,
    slots_ref,
    pool_mass_ref,
    _,
    listed_ref,
    same_ref,
    spare_ref,
    slot_mass_ref,
    mine_ref,
    own_ref,
    mass_ref,
):
    me, live = place_ref[0], place_ref[1]
    peers, columns = own_ref.shape[0], listed_ref.shape[1]
    half = peers // sides
    targets = own_ref.shape[1]
    pairs = pools_ref.shape[1]

    def hot(rows, values):
        return (rows == values).astype(F32).astype(BF16)

    column_slot = slot_at(iota((columns, 1), 0), half, sides)
    slot = slot_at(iota((1, columns), 1), half, sides)
    mine_ref[...] = (slot == me).astype(F32)
    listing = iota((1, pairs), 1) < live
    pool_hot = hot(iota((listed_ref.shape[0], pairs), 0), pools_ref[...])
    slot_hot = hot(column_slot, jnp.where(listing, slots_ref[...], -1))
    listed_ref[...] = product(pool_hot, slot_hot)

    spread = hot(column_slot, iota((columns, peers), 1))
    tables = notes_ref[:, 0, targets : targets + peers]
    table = table_ref[...].astype(F32)
    wide_tables = product(tables.astype(BF16), spread)
    wide_table = product(table.astype(BF16), spread)
    same_ref[...] = (wide_tables == wide_table).astype(F32)
    spare_ref[...] = (wide_table < 0).astype(F32)

    square = iota((peers, peers), 0), iota((peers, peers), 1)
    asked = jnp.sum(jnp.where(square[1] == me, tables, 0.0), axis=1, keepdims=True)
    block = (iota((peers, targets), 1) // CB).astype(F32)
    own_ref[...] = (asked == block).astype(F32)

    wanted = jnp.sum(jnp.where(square[0] == square[1], table, 0.0), axis=1, keepdims=True)
    masses = jnp.where(wanted == block, notes_ref[:, 0, :targets], 0.0)
    masses = fold(masses)
    slot_mass = [
        jnp.sum(
            jnp.where(
                iota((peers, LANES), 0) == slot_at(iota((peers, LANES), 1) + start, half, sides),
                masses,
                0.0,
            ),
            axis=0,
            keepdims=True,
        )
        for start in range(0, columns, LANES)
    ]
    slot_mass_ref[...] = jnp.concatenate(slot_mass, axis=1)

    diagonal = iota((LANES, LANES), 0) == iota((LANES, LANES), 1)
    for start in range(0, mass_ref.shape[0], LANES):
        row = pool_mass_ref[:, pl.ds(start, LANES)]
        mass_ref[pl.ds(start, LANES), :] = jnp.sum(
            jnp.where(diagonal, row, 0.0), axis=1, keepdims=True
        )


def prepare(place, notes, table, pools, slots, pool_mass, token, pool_count, targets, sides):
    peers = notes.shape[0]
    columns = peers * CB
    shapes = [
        (pool_count, columns),
        (peers, columns),
        (1, columns),
        (1, columns),
        (1, columns),
        (peers, targets),
        (pool_mass.shape[1], 1),
    ]
    return call(
        functools.partial(prepare_kernel, sides),
        "prepare",
        [jax.ShapeDtypeStruct(shape, F32) for shape in shapes],
        [whole(pltpu.SMEM)] + [whole()] * 6,
    )(place, notes, table, pools, slots, pool_mass, token)


def fold(rows):
    folded = rows[:, :LANES]
    for start in range(LANES, rows.shape[1], LANES):
        folded += rows[:, start : start + LANES]
    step = LANES // 2
    while step >= CB:
        folded += pltpu.roll(folded, step, 1)
        step //= 2
    return folded


def send_out(row, out_ref):
    out_ref[...] = jnp.broadcast_to(row[None], out_ref.shape)


def halves(x):
    high = x.astype(BF16)
    return high, (x - high.astype(F32)).astype(BF16)


def scores_of(p, q_high, q_low):
    high, low = halves(p)
    return product(high, q_high) + (product(high, q_low) + product(low, q_high))


def near_kernel(place_ref, pool_ref, *refs):
    near_refs, (scores_ref, near_high, near_low) = refs[:-3], refs[-3:]
    half = len(near_refs)
    me = place_ref[0]
    local = jnp.where(me < half, me, me - half)
    for turn, near_ref in enumerate(near_refs):
        for side in range(2):
            slot = side * half + mate(local, turn, half)
            at = pl.ds(pl.multiple_of(slot * CB, CB), CB)
            near_high[at, :], near_low[at, :] = halves(near_ref[side])
    ahead = near_high.shape[1]
    scores_ref[...] = scores_of(pool_ref[:, :ahead], near_high[...], near_low[...])


def near_scores(place, pool, near):
    rows = pool.shape[0]
    columns = 2 * len(near) * CB
    ahead = near[0].shape[2]
    return call(
        near_kernel,
        "near_scores",
        jax.ShapeDtypeStruct((rows, columns), F32),
        [whole(pltpu.SMEM)] + [whole()] * (1 + len(near)),
        cost=(6 * rows * columns * ahead, 4 * (rows + columns) * ahead, 0),
        scratch_shapes=[pltpu.VMEM((columns, ahead), BF16)] * 2,
    )(place, pool, *near)


def assemble_kernel(
    scale, pool_ref, near_ref, far_ref, listed_ref, mass_ref, kernel_ref, out_ref
):
    ahead = pool_ref.shape[1] - far_ref.shape[2]
    far_high, far_low = halves(far_ref[...].reshape(kernel_ref.shape[1], -1))
    sums = jnp.zeros((1, kernel_ref.shape[1]), F32)
    rows = 256 if kernel_ref.shape[0] % 256 == 0 else RB
    for start in range(0, kernel_ref.shape[0], rows):
        part = pl.ds(start, rows)
        scores = near_ref[part, :] + scores_of(pool_ref[part, ahead:], far_high, far_low)
        for block in range(rows // RB):
            inner = pl.ds(start + block * RB, RB)
            at = start // RB + block
            listed = listed_ref[at : at + 1, :] > 0
            values = jnp.where(
                listed, jnp.exp(scores[block * RB : (block + 1) * RB] * scale), 0.0
            )
            kernel_ref[inner, :] = values
            scaling = mass_ref[inner, :] / jnp.sum(values, axis=1, keepdims=True)
            sums += jnp.sum(values * scaling, axis=0, keepdims=True)
    send_out(sums, out_ref)


def assemble(pool, near, far, listed, mass):
    rows, width = pool.shape
    peers = far.shape[0]
    columns = peers * CB
    return call(
        functools.partial(assemble_kernel, 1.5 / math.sqrt(width)),
        "assemble",
        (
            jax.ShapeDtypeStruct((rows, columns), F32),
            jax.ShapeDtypeStruct((peers, 1, columns), F32),
        ),
        [whole()] * 5,
        cost=(
            6 * rows * columns * width,
            4 * (rows * width + columns * width + rows * columns),
            rows * columns,
        ),
    )(pool, near, far, listed, mass)


def iterate_kernel(
    kernel_ref, notes_ref, same_ref, slot_mass_ref, spare_ref, mass_ref, out_ref, *scaling_refs
):
    col_sums = jnp.sum(notes_ref[:, 0, :] * same_ref[...], axis=0, keepdims=True)
    target_scaling = slot_mass_ref[...] / (col_sums + spare_ref[...])
    sums = jnp.zeros_like(target_scaling)
    diagonal = lax.broadcasted_iota(jnp.int32, (LANES, LANES), 0) == lax.broadcasted_iota(
        jnp.int32, (LANES, LANES), 1
    )
    for start in range(0, kernel_ref.shape[0], LANES):
        inner = pl.ds(start, LANES)
        values = kernel_ref[inner, :]
        scaling = mass_ref[inner, :] / jnp.sum(values * target_scaling, axis=1, keepdims=True)
        sums += jnp.sum(values * scaling, axis=0, keepdims=True)
        for scaling_ref in scaling_refs:
            scaling_ref[:, inner] = jnp.sum(
                jnp.where(diagonal, scaling, 0.0), axis=0, keepdims=True
            )
    send_out(sums, out_ref)


def iterate(kernel, notes, same, slot_mass, spare, mass, last):
    rows, columns = kernel.shape
    out_shape = [jax.ShapeDtypeStruct(notes.shape, F32)]
    if last:
        out_shape.append(jax.ShapeDtypeStruct((1, rows), F32))
    return call(
        iterate_kernel,
        "iterate",
        out_shape,
        [whole()] * 6,
        cost=(4 * rows * columns, 4 * rows * columns, 0),
    )(kernel, notes, same, slot_mass, spare, mass)


def finish_kernel(
    notes_ref,
    mine_ref,
    own_ref,
    mass_ref,
    scaling_ref,
    pool_hbm,
    target_hbm,
    pool_ref,
    target_ref,
    sems,
):
    pool_ref[...] = jnp.log(scaling_ref[0])
    pool_copy = pltpu.make_async_copy(pool_ref, pool_hbm, sems.at[0])
    pool_copy.start()
    col_sums = jnp.sum(fold(notes_ref[:, 0, :] * mine_ref[...]) * own_ref[...], axis=0)
    target_ref[...] = jnp.log(mass_ref[...] / col_sums)
    target_copy = pltpu.make_async_copy(target_ref, target_hbm, sems.at[1])
    target_copy.start()
    pool_copy.wait()
    target_copy.wait()


def finish(notes, mine, own, mass, scaling):
    shapes = (scaling.shape[1:], mass.shape)
    return call(
        finish_kernel,
        "finish",
        tuple(jax.ShapeDtypeStruct(shape, F32) for shape in shapes),
        [whole()] * 5,
        (whole(pl.ANY),) * 2,
        scratch_shapes=[pltpu.VMEM(shape, F32) for shape in shapes]
        + [pltpu.SemaphoreType.DMA((2,))],
    )(notes, mine, own, mass, scaling)


def local(
    pool_emb,
    target_emb,
    pool_mass,
    target_mass,
    fetch_table,
    pair_pool,
    listed_pair_slot,
    pair_count,
):
    peers = lax.axis_size("clus")
    me = lax.axis_index("clus").astype(jnp.int32)
    targets, width = target_emb.shape
    pool_count = pool_emb.shape[0] // RB
    columns = peers * CB
    half = peers // 2
    ahead = width // LANES // 3 * LANES

    def trade(x, turn):
        pairs = [
            (side * half + mate(i, turn, half), side * half + i)
            for side in range(2)
            for i in range(half)
        ]
        return lax.ppermute(x, "clus", [pair for pair in pairs if pair[0] != pair[1]])

    blocks = target_emb.reshape(targets // CB, CB, width)
    held, other = cut(blocks, ahead)
    other = lax.ppermute(other, "clus", [(i, (i + half) % peers) for i in range(peers)])
    note = make_note(target_mass[None], fetch_table)
    notes = lax.cond(me < peers, exchange, jnp.zeros_like, note)
    far, token, near = pick_blocks(me[None], notes, held, other)
    far = exchange(far)
    near = [near[0]] + [trade(x, turn) for turn, x in enumerate(near[1:], 1)]
    place = jnp.concatenate([me[None], pair_count])
    listed, same, spare, slot_mass, mine, own, mass = prepare(
        place,
        notes,
        fetch_table,
        pair_pool,
        listed_pair_slot,
        pool_mass[None],
        token,
        pool_count,
        targets,
        1,
    )

    kernel, sums = assemble(
        pool_emb, near_scores(place, pool_emb, near), far, listed, mass
    )
    for step in range(1, ITERS):
        sums, *scalings = iterate(
            kernel, exchange(sums), same, slot_mass, spare, mass, step == ITERS - 1
        )
    return finish(exchange(sums), mine, own, target_mass, scalings[0])


def solution(mesh):
    return jax.shard_map(
        local,
        mesh=mesh,
        in_specs=(
            P(("groups", "clus"), None),
            P(("groups", "clus"), None),
            P(("groups", "clus")),
            P(("groups", "clus")),
            P(("groups", "clus"), None),
            P(("groups", "clus"), None),
            P(("groups", "clus"), None),
            P(("groups", "clus")),
        ),
        out_specs=(P(("groups", "clus")), P(("groups", "clus"))),
        check_vma=False,
    )
```

```python
import functools
import math

import jax
import jax.numpy as jnp
from jax import lax
from jax.experimental import pallas as pl
from jax.experimental.pallas import tpu as pltpu
from jax.sharding import PartitionSpec as P

RB = 64
CB = 16
ITERS = 3
LANES = 128
VMEM_LIMIT = 48 * 1024 * 1024

F32 = jnp.float32
BF16 = jnp.bfloat16


def whole(space=pltpu.VMEM):
    return pl.BlockSpec(memory_space=space)


def call(kernel, name, out_shape, in_specs, out_specs=None, cost=(0, 0, 0), scratch_shapes=(), limit=VMEM_LIMIT):
    flops, bytes_accessed, transcendentals = cost
    return pl.pallas_call(
        kernel,
        name=name,
        out_shape=out_shape,
        in_specs=in_specs,
        out_specs=jax.tree.map(lambda _: whole(), out_shape) if out_specs is None else out_specs,
        scratch_shapes=scratch_shapes,
        cost_estimate=pl.CostEstimate(
            flops=flops, bytes_accessed=bytes_accessed, transcendentals=transcendentals
        ),
        compiler_params=pltpu.CompilerParams(vmem_limit_bytes=limit),
    )


def exchange(rows, groups=None):
    return lax.all_to_all(
        rows, "clus", split_axis=0, concat_axis=0, tiled=True, axis_index_groups=groups
    )


def mate(local, turn, half):
    if half & (half - 1) == 0:
        return local ^ turn
    return (turn + half - local) % half


def note_kernel(mass_hbm, table_hbm, out_ref, mass_ref, table_ref, sems):
    copies = [
        pltpu.make_async_copy(mass_hbm, mass_ref, sems.at[0]),
        pltpu.make_async_copy(table_hbm, table_ref, sems.at[1]),
    ]
    for copy in copies:
        copy.start()
    for copy in copies:
        copy.wait()
    targets, peers = mass_ref.shape[1], table_ref.shape[1]
    shape = (out_ref.shape[0], 1)
    out_ref[:, :, :targets] = jnp.broadcast_to(mass_ref[...][None], shape + (targets,))
    out_ref[:, :, targets:] = jnp.zeros(shape + (out_ref.shape[2] - targets,), F32)
    out_ref[:, :, targets : targets + peers] = jnp.broadcast_to(
        table_ref[...].astype(F32)[None], shape + (peers,)
    )


def make_note(mass, table):
    peers = table.shape[1]
    length = mass.shape[1] + -(-peers // LANES) * LANES
    return call(
        note_kernel,
        "make_note",
        jax.ShapeDtypeStruct((peers, 1, length), F32),
        [whole(pltpu.HBM)] * 2,
        scratch_shapes=[
            pltpu.VMEM(mass.shape, F32),
            pltpu.VMEM(table.shape, jnp.int32),
            pltpu.SemaphoreType.DMA((2,)),
        ],
        limit=None,
    )(mass, table)


def cut_kernel(x_ref, held_ref, ahead_ref):
    held_ref[...] = x_ref[...]
    ahead_ref[...] = x_ref[:, :, : ahead_ref.shape[2]]


def cut(blocks, ahead):
    return call(
        cut_kernel,
        "cut",
        (
            jax.ShapeDtypeStruct(blocks.shape, F32),
            jax.ShapeDtypeStruct(blocks.shape[:2] + (ahead,), F32),
        ),
        [whole()],
    )(blocks)


def pick_kernel(half, place_ref, notes_ref, own_ref, other_ref, far_ref, token_ref, *refs):
    near_refs, (asked_ref, near_held, far_held, near_sems, far_sems) = refs[:half], refs[half:]
    peers = far_ref.shape[0]
    count, _, width = own_ref.shape
    ahead = other_ref.shape[2]
    first = notes_ref.shape[2] - -(-peers // LANES) * LANES
    me = place_ref[0]
    side = me // half
    tables = notes_ref[:, 0, first:]
    lane = lax.broadcasted_iota(jnp.int32, tables.shape, 1)
    for turn, owner in enumerate((me, jnp.where(side == 0, me + half, me - half))):
        asked = jnp.sum(jnp.where(lane == owner, tables, 0.0), axis=1, keepdims=True)
        asked_ref[turn] = jnp.broadcast_to(asked, asked_ref.shape[1:])

    def select(emb_ref, wanted, columns):
        block = emb_ref[0, :, columns]
        for t in range(1, count):
            block = jnp.where(wanted == t, emb_ref[t, :, columns], block)
        return block

    def wanted_of(turn, d):
        return jnp.broadcast_to(asked_ref[turn, pl.ds(d, 1), :], (CB, LANES))

    def near_copy(turn):
        return pltpu.make_async_copy(near_held.at[turn], near_refs[turn], near_sems.at[turn])

    def far_copy(d):
        return pltpu.make_async_copy(far_held.at[d], far_ref.at[d], far_sems.at[d])

    def pick_far(d):
        wanted = wanted_of(0, d)
        for start in range(ahead, width, LANES):
            far_held[d, :, start - ahead : start - ahead + LANES] = select(
                own_ref, wanted, pl.ds(start, LANES)
            )
        far_copy(d).start()

    if peers <= 16:
        for d in range(peers):
            pick_far(d)
    else:
        pl.loop(0, peers)(pick_far)
    for turn in range(half):
        reader = side * half + mate(me - side * half, turn, half)
        for source, emb_ref in enumerate((own_ref, other_ref)):
            at = side if source == 0 else 1 - side
            wanted = wanted_of(source, reader)

            @pl.loop(0, ahead // LANES)
            def _(part):
                columns = pl.ds(pl.multiple_of(part * LANES, LANES), LANES)
                near_held[turn, at, :, columns] = select(emb_ref, wanted, columns)

        near_copy(turn).start()
    token_ref[...] = jnp.zeros_like(token_ref)

    @pl.loop(0, peers)
    def _(d):
        far_copy(d).wait()

    for turn in range(half):
        near_copy(turn).wait()


def pick_blocks(me, notes, own, other):
    peers = notes.shape[0]
    half = peers // 2
    ahead = other.shape[2]
    near = (2, CB, ahead)
    far = (peers, CB, own.shape[2] - ahead)
    far, token, *near = call(
        functools.partial(pick_kernel, half),
        "pick_blocks",
        [jax.ShapeDtypeStruct(shape, F32) for shape in [far, (8, LANES)] + [near] * half],
        [whole(pltpu.SMEM)] + [whole()] * 3,
        [whole(pl.ANY), whole()] + [whole(pl.ANY)] * half,
        scratch_shapes=[
            pltpu.VMEM((2, peers, LANES), F32),
            pltpu.VMEM((half,) + near, F32),
            pltpu.VMEM(far, F32),
            pltpu.SemaphoreType.DMA((half,)),
            pltpu.SemaphoreType.DMA((peers,)),
        ],
    )(me, notes, own, other)
    return far, token, near


def iota(shape, dimension):
    return lax.broadcasted_iota(jnp.int32, shape, dimension)


def slot_at(column, half, sides):
    block = column // CB
    return block % sides * half + block // sides


def product(a, b):
    return lax.dot_general(a, b, (((1,), (1,)), ((), ())), preferred_element_type=F32)


def prepare_kernel(
    sides,
    place_ref,
    notes_ref,
    table_ref,
    pools_ref,
    slots_ref,
    pool_mass_ref,
    _,
    listed_ref,
    same_ref,
    spare_ref,
    slot_mass_ref,
    mine_ref,
    own_ref,
    mass_ref,
):
    me, live = place_ref[0], place_ref[1]
    peers, columns = own_ref.shape[0], listed_ref.shape[1]
    half = peers // sides
    targets = own_ref.shape[1]
    pairs = pools_ref.shape[1]

    def hot(rows, values):
        return (rows == values).astype(F32).astype(BF16)

    column_slot = slot_at(iota((columns, 1), 0), half, sides)
    slot = slot_at(iota((1, columns), 1), half, sides)
    mine_ref[...] = (slot == me).astype(F32)
    listing = iota((1, pairs), 1) < live
    pool_hot = hot(iota((listed_ref.shape[0], pairs), 0), pools_ref[...])
    slot_hot = hot(column_slot, jnp.where(listing, slots_ref[...], -1))
    listed_ref[...] = product(pool_hot, slot_hot)

    spread = hot(column_slot, iota((columns, peers), 1))
    tables = notes_ref[:, 0, targets : targets + peers]
    table = table_ref[...].astype(F32)
    wide_tables = product(tables.astype(BF16), spread)
    wide_table = product(table.astype(BF16), spread)
    same_ref[...] = (wide_tables == wide_table).astype(F32)
    spare_ref[...] = (wide_table < 0).astype(F32)

    square = iota((peers, peers), 0), iota((peers, peers), 1)
    asked = jnp.sum(jnp.where(square[1] == me, tables, 0.0), axis=1, keepdims=True)
    block = (iota((peers, targets), 1) // CB).astype(F32)
    own_ref[...] = (asked == block).astype(F32)

    wanted = jnp.sum(jnp.where(square[0] == square[1], table, 0.0), axis=1, keepdims=True)
    masses = jnp.where(wanted == block, notes_ref[:, 0, :targets], 0.0)
    masses = fold(masses)
    slot_mass = [
        jnp.sum(
            jnp.where(
                iota((peers, LANES), 0) == slot_at(iota((peers, LANES), 1) + start, half, sides),
                masses,
                0.0,
            ),
            axis=0,
            keepdims=True,
        )
        for start in range(0, columns, LANES)
    ]
    slot_mass_ref[...] = jnp.concatenate(slot_mass, axis=1)

    diagonal = iota((LANES, LANES), 0) == iota((LANES, LANES), 1)
    for start in range(0, mass_ref.shape[0], LANES):
        row = pool_mass_ref[:, pl.ds(start, LANES)]
        mass_ref[pl.ds(start, LANES), :] = jnp.sum(
            jnp.where(diagonal, row, 0.0), axis=1, keepdims=True
        )


def prepare(place, notes, table, pools, slots, pool_mass, token, pool_count, targets, sides):
    peers = notes.shape[0]
    columns = peers * CB
    shapes = [
        (pool_count, columns),
        (peers, columns),
        (1, columns),
        (1, columns),
        (1, columns),
        (peers, targets),
        (pool_mass.shape[1], 1),
    ]
    return call(
        functools.partial(prepare_kernel, sides),
        "prepare",
        [jax.ShapeDtypeStruct(shape, F32) for shape in shapes],
        [whole(pltpu.SMEM)] + [whole()] * 6,
    )(place, notes, table, pools, slots, pool_mass, token)


def fold(rows):
    folded = rows[:, :LANES]
    for start in range(LANES, rows.shape[1], LANES):
        folded += rows[:, start : start + LANES]
    step = LANES // 2
    while step >= CB:
        folded += pltpu.roll(folded, step, 1)
        step //= 2
    return folded


def send_out(row, out_ref):
    out_ref[...] = jnp.broadcast_to(row[None], out_ref.shape)


def halves(x):
    high = x.astype(BF16)
    return high, (x - high.astype(F32)).astype(BF16)


def assemble_kernel(scale, place_ref, pool_ref, far_ref, listed_ref, mass_ref, *refs):
    near_refs, (kernel_ref, out_ref, near_high, near_low) = refs[:-4], refs[-4:]
    half = len(near_refs)
    me = place_ref[0]
    local = jnp.where(me < half, me, me - half)
    for turn, near_ref in enumerate(near_refs):
        for side in range(2):
            slot = side * half + mate(local, turn, half)
            at = pl.ds(pl.multiple_of(slot * CB, CB), CB)
            near_high[at, :], near_low[at, :] = halves(near_ref[side])
    ahead = near_high.shape[1]
    far_high, far_low = halves(far_ref[...].reshape(kernel_ref.shape[1], -1))
    sums = jnp.zeros((1, kernel_ref.shape[1]), F32)
    rows = 256 if kernel_ref.shape[0] % 256 == 0 else RB

    def scores_of(p, q_high, q_low):
        high, low = halves(p)
        return product(high, q_high) + (product(high, q_low) + product(low, q_high))

    for start in range(0, kernel_ref.shape[0], rows):
        pool = pool_ref[pl.ds(start, rows), :]
        scores = scores_of(pool[:, :ahead], near_high[...], near_low[...])
        scores += scores_of(pool[:, ahead:], far_high, far_low)
        for block in range(rows // RB):
            inner = pl.ds(start + block * RB, RB)
            at = start // RB + block
            listed = listed_ref[at : at + 1, :] > 0
            values = jnp.where(
                listed, jnp.exp(scores[block * RB : (block + 1) * RB] * scale), 0.0
            )
            kernel_ref[inner, :] = values
            scaling = mass_ref[inner, :] / jnp.sum(values, axis=1, keepdims=True)
            sums += jnp.sum(values * scaling, axis=0, keepdims=True)
    send_out(sums, out_ref)


def assemble(place, pool, near, far, listed, mass):
    rows, width = pool.shape
    peers = far.shape[0]
    columns = peers * CB
    ahead = near[0].shape[2]
    return call(
        functools.partial(assemble_kernel, 1.5 / math.sqrt(width)),
        "assemble",
        (
            jax.ShapeDtypeStruct((rows, columns), F32),
            jax.ShapeDtypeStruct((peers, 1, columns), F32),
        ),
        [whole(pltpu.SMEM)] + [whole()] * (4 + len(near)),
        cost=(
            6 * rows * columns * width,
            4 * (rows * width + columns * width + rows * columns),
            rows * columns,
        ),
        scratch_shapes=[pltpu.VMEM((columns, ahead), BF16)] * 2,
    )(place, pool, far, listed, mass, *near)


def iterate_kernel(
    kernel_ref, notes_ref, same_ref, slot_mass_ref, spare_ref, mass_ref, out_ref, *scaling_refs
):
    col_sums = jnp.sum(notes_ref[:, 0, :] * same_ref[...], axis=0, keepdims=True)
    target_scaling = slot_mass_ref[...] / (col_sums + spare_ref[...])
    sums = jnp.zeros_like(target_scaling)
    diagonal = lax.broadcasted_iota(jnp.int32, (LANES, LANES), 0) == lax.broadcasted_iota(
        jnp.int32, (LANES, LANES), 1
    )
    for start in range(0, kernel_ref.shape[0], LANES):
        inner = pl.ds(start, LANES)
        values = kernel_ref[inner, :]
        scaling = mass_ref[inner, :] / jnp.sum(values * target_scaling, axis=1, keepdims=True)
        sums += jnp.sum(values * scaling, axis=0, keepdims=True)
        for scaling_ref in scaling_refs:
            scaling_ref[:, inner] = jnp.sum(
                jnp.where(diagonal, scaling, 0.0), axis=0, keepdims=True
            )
    send_out(sums, out_ref)


def iterate(kernel, notes, same, slot_mass, spare, mass, last):
    rows, columns = kernel.shape
    out_shape = [jax.ShapeDtypeStruct(notes.shape, F32)]
    if last:
        out_shape.append(jax.ShapeDtypeStruct((1, rows), F32))
    return call(
        iterate_kernel,
        "iterate",
        out_shape,
        [whole()] * 6,
        cost=(4 * rows * columns, 4 * rows * columns, 0),
    )(kernel, notes, same, slot_mass, spare, mass)


def finish_kernel(
    notes_ref,
    mine_ref,
    own_ref,
    mass_ref,
    scaling_ref,
    pool_hbm,
    target_hbm,
    pool_ref,
    target_ref,
    sems,
):
    pool_ref[...] = jnp.log(scaling_ref[0])
    pool_copy = pltpu.make_async_copy(pool_ref, pool_hbm, sems.at[0])
    pool_copy.start()
    col_sums = jnp.sum(fold(notes_ref[:, 0, :] * mine_ref[...]) * own_ref[...], axis=0)
    target_ref[...] = jnp.log(mass_ref[...] / col_sums)
    target_copy = pltpu.make_async_copy(target_ref, target_hbm, sems.at[1])
    target_copy.start()
    pool_copy.wait()
    target_copy.wait()


def finish(notes, mine, own, mass, scaling):
    shapes = (scaling.shape[1:], mass.shape)
    return call(
        finish_kernel,
        "finish",
        tuple(jax.ShapeDtypeStruct(shape, F32) for shape in shapes),
        [whole()] * 5,
        (whole(pl.ANY),) * 2,
        scratch_shapes=[pltpu.VMEM(shape, F32) for shape in shapes]
        + [pltpu.SemaphoreType.DMA((2,))],
    )(notes, mine, own, mass, scaling)


def local(
    pool_emb,
    target_emb,
    pool_mass,
    target_mass,
    fetch_table,
    pair_pool,
    listed_pair_slot,
    pair_count,
):
    peers = lax.axis_size("clus")
    me = lax.axis_index("clus").astype(jnp.int32)
    targets, width = target_emb.shape
    pool_count = pool_emb.shape[0] // RB
    columns = peers * CB
    half = peers // 2
    ahead = width // LANES // 2 * LANES

    def trade(x, turn):
        pairs = [
            (side * half + mate(i, turn, half), side * half + i)
            for side in range(2)
            for i in range(half)
        ]
        return lax.ppermute(x, "clus", [pair for pair in pairs if pair[0] != pair[1]])

    blocks = target_emb.reshape(targets // CB, CB, width)
    held, other = cut(blocks, ahead)
    other = lax.ppermute(other, "clus", [(i, (i + half) % peers) for i in range(peers)])
    note = make_note(target_mass[None], fetch_table)
    notes = lax.cond(me < peers, exchange, jnp.zeros_like, note)
    far, token, near = pick_blocks(me[None], notes, held, other)
    far = exchange(far)
    near = [near[0]] + [trade(x, turn) for turn, x in enumerate(near[1:], 1)]
    place = jnp.concatenate([me[None], pair_count])
    listed, same, spare, slot_mass, mine, own, mass = prepare(
        place,
        notes,
        fetch_table,
        pair_pool,
        listed_pair_slot,
        pool_mass[None],
        token,
        pool_count,
        targets,
        1,
    )

    kernel, sums = assemble(place, pool_emb, near, far, listed, mass)
    for step in range(1, ITERS):
        sums, *scalings = iterate(
            kernel, exchange(sums), same, slot_mass, spare, mass, step == ITERS - 1
        )
    return finish(exchange(sums), mine, own, target_mass, scalings[0])


def solution(mesh):
    return jax.shard_map(
        local,
        mesh=mesh,
        in_specs=(
            P(("groups", "clus"), None),
            P(("groups", "clus"), None),
            P(("groups", "clus")),
            P(("groups", "clus")),
            P(("groups", "clus"), None),
            P(("groups", "clus"), None),
            P(("groups", "clus"), None),
            P(("groups", "clus")),
        ),
        out_specs=(P(("groups", "clus")), P(("groups", "clus"))),
        check_vma=False,
    )
```

```python
import functools
import math

import jax
import jax.numpy as jnp
from jax import lax
from jax.experimental import pallas as pl
from jax.experimental.pallas import tpu as pltpu
from jax.sharding import PartitionSpec as P

RB = 64
CB = 16
ITERS = 3
LANES = 128
VMEM_LIMIT = 48 * 1024 * 1024

F32 = jnp.float32
BF16 = jnp.bfloat16


def whole(space=pltpu.VMEM):
    return pl.BlockSpec(memory_space=space)


def call(kernel, name, out_shape, in_specs, out_specs=None, cost=(0, 0, 0), scratch_shapes=(), limit=VMEM_LIMIT):
    flops, bytes_accessed, transcendentals = cost
    return pl.pallas_call(
        kernel,
        name=name,
        out_shape=out_shape,
        in_specs=in_specs,
        out_specs=jax.tree.map(lambda _: whole(), out_shape) if out_specs is None else out_specs,
        scratch_shapes=scratch_shapes,
        cost_estimate=pl.CostEstimate(
            flops=flops, bytes_accessed=bytes_accessed, transcendentals=transcendentals
        ),
        compiler_params=pltpu.CompilerParams(vmem_limit_bytes=limit),
    )


def exchange(rows, groups=None):
    return lax.all_to_all(
        rows, "clus", split_axis=0, concat_axis=0, tiled=True, axis_index_groups=groups
    )


def mate(local, turn, half):
    if half & (half - 1) == 0:
        return local ^ ((half - turn) % half)
    return (turn + half - local) % half


def note_kernel(mass_hbm, table_hbm, out_ref, mass_ref, table_ref, sems):
    copies = [
        pltpu.make_async_copy(mass_hbm, mass_ref, sems.at[0]),
        pltpu.make_async_copy(table_hbm, table_ref, sems.at[1]),
    ]
    for copy in copies:
        copy.start()
    for copy in copies:
        copy.wait()
    targets, peers = mass_ref.shape[1], table_ref.shape[1]
    shape = (out_ref.shape[0], 1)
    out_ref[:, :, :targets] = jnp.broadcast_to(mass_ref[...][None], shape + (targets,))
    out_ref[:, :, targets:] = jnp.zeros(shape + (out_ref.shape[2] - targets,), F32)
    out_ref[:, :, targets : targets + peers] = jnp.broadcast_to(
        table_ref[...].astype(F32)[None], shape + (peers,)
    )


def make_note(mass, table):
    peers = table.shape[1]
    length = mass.shape[1] + -(-peers // LANES) * LANES
    return call(
        note_kernel,
        "make_note",
        jax.ShapeDtypeStruct((peers, 1, length), F32),
        [whole(pltpu.HBM)] * 2,
        scratch_shapes=[
            pltpu.VMEM(mass.shape, F32),
            pltpu.VMEM(table.shape, jnp.int32),
            pltpu.SemaphoreType.DMA((2,)),
        ],
        limit=None,
    )(mass, table)


def cut_kernel(x_ref, held_ref, ahead_ref):
    held_ref[...] = x_ref[...]
    ahead_ref[...] = x_ref[:, :, : ahead_ref.shape[2]]


def cut(blocks, ahead):
    return call(
        cut_kernel,
        "cut",
        (
            jax.ShapeDtypeStruct(blocks.shape, F32),
            jax.ShapeDtypeStruct(blocks.shape[:2] + (ahead,), F32),
        ),
        [whole()],
    )(blocks)


def pick_kernel(half, place_ref, notes_ref, own_ref, other_ref, far_ref, token_ref, *refs):
    near_refs, (asked_ref, near_held, far_held, near_sems, far_sems) = refs[:half], refs[half:]
    peers = far_ref.shape[0]
    count, _, width = own_ref.shape
    ahead = other_ref.shape[2]
    first = notes_ref.shape[2] - -(-peers // LANES) * LANES
    me = place_ref[0]
    side = me // half
    tables = notes_ref[:, 0, first:]
    lane = lax.broadcasted_iota(jnp.int32, tables.shape, 1)
    for turn, owner in enumerate((me, jnp.where(side == 0, me + half, me - half))):
        asked = jnp.sum(jnp.where(lane == owner, tables, 0.0), axis=1, keepdims=True)
        asked_ref[turn] = jnp.broadcast_to(asked, asked_ref.shape[1:])

    def select(emb_ref, wanted, columns):
        block = emb_ref[0, :, columns]
        for t in range(1, count):
            block = jnp.where(wanted == t, emb_ref[t, :, columns], block)
        return block

    def wanted_of(turn, d):
        return jnp.broadcast_to(asked_ref[turn, pl.ds(d, 1), :], (CB, LANES))

    def near_copy(turn):
        return pltpu.make_async_copy(near_held.at[turn], near_refs[turn], near_sems.at[turn])

    def far_copy(d):
        return pltpu.make_async_copy(far_held.at[d], far_ref.at[d], far_sems.at[d])

    def pick_far(d):
        wanted = wanted_of(0, d)
        for start in range(ahead, width, LANES):
            far_held[d, :, start - ahead : start - ahead + LANES] = select(
                own_ref, wanted, pl.ds(start, LANES)
            )
        far_copy(d).start()

    if peers <= 16:
        for d in range(peers):
            pick_far(d)
    else:
        pl.loop(0, peers)(pick_far)
    for turn in range(half):
        reader = side * half + mate(me - side * half, turn, half)
        for source, emb_ref in enumerate((own_ref, other_ref)):
            at = side if source == 0 else 1 - side
            wanted = wanted_of(source, reader)

            @pl.loop(0, ahead // LANES)
            def _(part):
                columns = pl.ds(pl.multiple_of(part * LANES, LANES), LANES)
                near_held[turn, at, :, columns] = select(emb_ref, wanted, columns)

        near_copy(turn).start()
    token_ref[...] = jnp.zeros_like(token_ref)

    @pl.loop(0, peers)
    def _(d):
        far_copy(d).wait()

    for turn in range(half):
        near_copy(turn).wait()


def pick_blocks(me, notes, own, other):
    peers = notes.shape[0]
    half = peers // 2
    ahead = other.shape[2]
    near = (2, CB, ahead)
    far = (peers, CB, own.shape[2] - ahead)
    far, token, *near = call(
        functools.partial(pick_kernel, half),
        "pick_blocks",
        [jax.ShapeDtypeStruct(shape, F32) for shape in [far, (8, LANES)] + [near] * half],
        [whole(pltpu.SMEM)] + [whole()] * 3,
        [whole(pl.ANY), whole()] + [whole(pl.ANY)] * half,
        scratch_shapes=[
            pltpu.VMEM((2, peers, LANES), F32),
            pltpu.VMEM((half,) + near, F32),
            pltpu.VMEM(far, F32),
            pltpu.SemaphoreType.DMA((half,)),
            pltpu.SemaphoreType.DMA((peers,)),
        ],
    )(me, notes, own, other)
    return far, token, near


def iota(shape, dimension):
    return lax.broadcasted_iota(jnp.int32, shape, dimension)


def slot_at(column, half, sides):
    block = column // CB
    return block % sides * half + block // sides


def product(a, b):
    return lax.dot_general(a, b, (((1,), (1,)), ((), ())), preferred_element_type=F32)


def prepare_kernel(
    sides,
    place_ref,
    notes_ref,
    table_ref,
    pools_ref,
    slots_ref,
    pool_mass_ref,
    _,
    listed_ref,
    same_ref,
    spare_ref,
    slot_mass_ref,
    mine_ref,
    own_ref,
    mass_ref,
):
    me, live = place_ref[0], place_ref[1]
    peers, columns = own_ref.shape[0], listed_ref.shape[1]
    half = peers // sides
    targets = own_ref.shape[1]
    pairs = pools_ref.shape[1]

    def hot(rows, values):
        return (rows == values).astype(F32).astype(BF16)

    column_slot = slot_at(iota((columns, 1), 0), half, sides)
    slot = slot_at(iota((1, columns), 1), half, sides)
    mine_ref[...] = (slot == me).astype(F32)
    listing = iota((1, pairs), 1) < live
    pool_hot = hot(iota((listed_ref.shape[0], pairs), 0), pools_ref[...])
    slot_hot = hot(column_slot, jnp.where(listing, slots_ref[...], -1))
    listed_ref[...] = product(pool_hot, slot_hot)

    spread = hot(column_slot, iota((columns, peers), 1))
    tables = notes_ref[:, 0, targets : targets + peers]
    table = table_ref[...].astype(F32)
    wide_tables = product(tables.astype(BF16), spread)
    wide_table = product(table.astype(BF16), spread)
    same_ref[...] = (wide_tables == wide_table).astype(F32)
    spare_ref[...] = (wide_table < 0).astype(F32)

    square = iota((peers, peers), 0), iota((peers, peers), 1)
    asked = jnp.sum(jnp.where(square[1] == me, tables, 0.0), axis=1, keepdims=True)
    block = (iota((peers, targets), 1) // CB).astype(F32)
    own_ref[...] = (asked == block).astype(F32)

    wanted = jnp.sum(jnp.where(square[0] == square[1], table, 0.0), axis=1, keepdims=True)
    masses = jnp.where(wanted == block, notes_ref[:, 0, :targets], 0.0)
    masses = fold(masses)
    slot_mass = [
        jnp.sum(
            jnp.where(
                iota((peers, LANES), 0) == slot_at(iota((peers, LANES), 1) + start, half, sides),
                masses,
                0.0,
            ),
            axis=0,
            keepdims=True,
        )
        for start in range(0, columns, LANES)
    ]
    slot_mass_ref[...] = jnp.concatenate(slot_mass, axis=1)

    diagonal = iota((LANES, LANES), 0) == iota((LANES, LANES), 1)
    for start in range(0, mass_ref.shape[0], LANES):
        row = pool_mass_ref[:, pl.ds(start, LANES)]
        mass_ref[pl.ds(start, LANES), :] = jnp.sum(
            jnp.where(diagonal, row, 0.0), axis=1, keepdims=True
        )


def prepare(place, notes, table, pools, slots, pool_mass, token, pool_count, targets, sides):
    peers = notes.shape[0]
    columns = peers * CB
    shapes = [
        (pool_count, columns),
        (peers, columns),
        (1, columns),
        (1, columns),
        (1, columns),
        (peers, targets),
        (pool_mass.shape[1], 1),
    ]
    return call(
        functools.partial(prepare_kernel, sides),
        "prepare",
        [jax.ShapeDtypeStruct(shape, F32) for shape in shapes],
        [whole(pltpu.SMEM)] + [whole()] * 6,
    )(place, notes, table, pools, slots, pool_mass, token)


def fold(rows):
    folded = rows[:, :LANES]
    for start in range(LANES, rows.shape[1], LANES):
        folded += rows[:, start : start + LANES]
    step = LANES // 2
    while step >= CB:
        folded += pltpu.roll(folded, step, 1)
        step //= 2
    return folded


def send_out(row, out_ref):
    out_ref[...] = jnp.broadcast_to(row[None], out_ref.shape)


def halves(x):
    high = x.astype(BF16)
    return high, (x - high.astype(F32)).astype(BF16)


def assemble_kernel(scale, place_ref, pool_ref, far_ref, listed_ref, mass_ref, *refs):
    near_refs, (kernel_ref, out_ref, near_high, near_low) = refs[:-4], refs[-4:]
    half = len(near_refs)
    me = place_ref[0]
    local = jnp.where(me < half, me, me - half)
    for turn, near_ref in enumerate(near_refs):
        for side in range(2):
            slot = side * half + mate(local, turn, half)
            at = pl.ds(pl.multiple_of(slot * CB, CB), CB)
            near_high[at, :], near_low[at, :] = halves(near_ref[side])
    ahead = near_high.shape[1]
    far_high, far_low = halves(far_ref[...].reshape(kernel_ref.shape[1], -1))
    sums = jnp.zeros((1, kernel_ref.shape[1]), F32)
    rows = 256 if kernel_ref.shape[0] % 256 == 0 else RB

    def scores_of(p, q_high, q_low):
        high, low = halves(p)
        return product(high, q_high) + (product(high, q_low) + product(low, q_high))

    for start in range(0, kernel_ref.shape[0], rows):
        pool = pool_ref[pl.ds(start, rows), :]
        scores = scores_of(pool[:, :ahead], near_high[...], near_low[...])
        scores += scores_of(pool[:, ahead:], far_high, far_low)
        for block in range(rows // RB):
            inner = pl.ds(start + block * RB, RB)
            at = start // RB + block
            listed = listed_ref[at : at + 1, :] > 0
            values = jnp.where(
                listed, jnp.exp(scores[block * RB : (block + 1) * RB] * scale), 0.0
            )
            kernel_ref[inner, :] = values
            scaling = mass_ref[inner, :] / jnp.sum(values, axis=1, keepdims=True)
            sums += jnp.sum(values * scaling, axis=0, keepdims=True)
    send_out(sums, out_ref)


def assemble(place, pool, near, far, listed, mass):
    rows, width = pool.shape
    peers = far.shape[0]
    columns = peers * CB
    ahead = near[0].shape[2]
    return call(
        functools.partial(assemble_kernel, 1.5 / math.sqrt(width)),
        "assemble",
        (
            jax.ShapeDtypeStruct((rows, columns), F32),
            jax.ShapeDtypeStruct((peers, 1, columns), F32),
        ),
        [whole(pltpu.SMEM)] + [whole()] * (4 + len(near)),
        cost=(
            6 * rows * columns * width,
            4 * (rows * width + columns * width + rows * columns),
            rows * columns,
        ),
        scratch_shapes=[pltpu.VMEM((columns, ahead), BF16)] * 2,
    )(place, pool, far, listed, mass, *near)


def iterate_kernel(
    kernel_ref, notes_ref, same_ref, slot_mass_ref, spare_ref, mass_ref, out_ref, *scaling_refs
):
    col_sums = jnp.sum(notes_ref[:, 0, :] * same_ref[...], axis=0, keepdims=True)
    target_scaling = slot_mass_ref[...] / (col_sums + spare_ref[...])
    sums = jnp.zeros_like(target_scaling)
    diagonal = lax.broadcasted_iota(jnp.int32, (LANES, LANES), 0) == lax.broadcasted_iota(
        jnp.int32, (LANES, LANES), 1
    )
    for start in range(0, kernel_ref.shape[0], LANES):
        inner = pl.ds(start, LANES)
        values = kernel_ref[inner, :]
        scaling = mass_ref[inner, :] / jnp.sum(values * target_scaling, axis=1, keepdims=True)
        sums += jnp.sum(values * scaling, axis=0, keepdims=True)
        for scaling_ref in scaling_refs:
            scaling_ref[:, inner] = jnp.sum(
                jnp.where(diagonal, scaling, 0.0), axis=0, keepdims=True
            )
    send_out(sums, out_ref)


def iterate(kernel, notes, same, slot_mass, spare, mass, last):
    rows, columns = kernel.shape
    out_shape = [jax.ShapeDtypeStruct(notes.shape, F32)]
    if last:
        out_shape.append(jax.ShapeDtypeStruct((1, rows), F32))
    return call(
        iterate_kernel,
        "iterate",
        out_shape,
        [whole()] * 6,
        cost=(4 * rows * columns, 4 * rows * columns, 0),
    )(kernel, notes, same, slot_mass, spare, mass)


def finish_kernel(
    notes_ref,
    mine_ref,
    own_ref,
    mass_ref,
    scaling_ref,
    pool_hbm,
    target_hbm,
    pool_ref,
    target_ref,
    sems,
):
    pool_ref[...] = jnp.log(scaling_ref[0])
    pool_copy = pltpu.make_async_copy(pool_ref, pool_hbm, sems.at[0])
    pool_copy.start()
    col_sums = jnp.sum(fold(notes_ref[:, 0, :] * mine_ref[...]) * own_ref[...], axis=0)
    target_ref[...] = jnp.log(mass_ref[...] / col_sums)
    target_copy = pltpu.make_async_copy(target_ref, target_hbm, sems.at[1])
    target_copy.start()
    pool_copy.wait()
    target_copy.wait()


def finish(notes, mine, own, mass, scaling):
    shapes = (scaling.shape[1:], mass.shape)
    return call(
        finish_kernel,
        "finish",
        tuple(jax.ShapeDtypeStruct(shape, F32) for shape in shapes),
        [whole()] * 5,
        (whole(pl.ANY),) * 2,
        scratch_shapes=[pltpu.VMEM(shape, F32) for shape in shapes]
        + [pltpu.SemaphoreType.DMA((2,))],
    )(notes, mine, own, mass, scaling)


def local(
    pool_emb,
    target_emb,
    pool_mass,
    target_mass,
    fetch_table,
    pair_pool,
    listed_pair_slot,
    pair_count,
):
    peers = lax.axis_size("clus")
    me = lax.axis_index("clus").astype(jnp.int32)
    targets, width = target_emb.shape
    pool_count = pool_emb.shape[0] // RB
    columns = peers * CB
    half = peers // 2
    ahead = width // LANES // 3 * LANES

    def trade(x, turn):
        pairs = [
            (side * half + mate(i, turn, half), side * half + i)
            for side in range(2)
            for i in range(half)
        ]
        return lax.ppermute(x, "clus", [pair for pair in pairs if pair[0] != pair[1]])

    blocks = target_emb.reshape(targets // CB, CB, width)
    held, other = cut(blocks, ahead)
    other = lax.ppermute(other, "clus", [(i, (i + half) % peers) for i in range(peers)])
    note = make_note(target_mass[None], fetch_table)
    notes = lax.cond(me < peers, exchange, jnp.zeros_like, note)
    far, token, near = pick_blocks(me[None], notes, held, other)
    far = exchange(far)
    near = [near[0]] + [trade(x, turn) for turn, x in enumerate(near[1:], 1)]
    place = jnp.concatenate([me[None], pair_count])
    listed, same, spare, slot_mass, mine, own, mass = prepare(
        place,
        notes,
        fetch_table,
        pair_pool,
        listed_pair_slot,
        pool_mass[None],
        token,
        pool_count,
        targets,
        1,
    )

    kernel, sums = assemble(place, pool_emb, near, far, listed, mass)
    for step in range(1, ITERS):
        sums, *scalings = iterate(
            kernel, exchange(sums), same, slot_mass, spare, mass, step == ITERS - 1
        )
    return finish(exchange(sums), mine, own, target_mass, scalings[0])


def solution(mesh):
    return jax.shard_map(
        local,
        mesh=mesh,
        in_specs=(
            P(("groups", "clus"), None),
            P(("groups", "clus"), None),
            P(("groups", "clus")),
            P(("groups", "clus")),
            P(("groups", "clus"), None),
            P(("groups", "clus"), None),
            P(("groups", "clus"), None),
            P(("groups", "clus")),
        ),
        out_specs=(P(("groups", "clus")), P(("groups", "clus"))),
        check_vma=False,
    )
```

```python
import functools
import math

import jax
import jax.numpy as jnp
from jax import lax
from jax.experimental import pallas as pl
from jax.experimental.pallas import tpu as pltpu
from jax.sharding import PartitionSpec as P

RB = 64
CB = 16
ITERS = 3
LANES = 128
VMEM_LIMIT = 48 * 1024 * 1024

F32 = jnp.float32
BF16 = jnp.bfloat16


def whole(space=pltpu.VMEM):
    return pl.BlockSpec(memory_space=space)


def call(kernel, name, out_shape, in_specs, out_specs=None, cost=(0, 0, 0), scratch_shapes=(), limit=VMEM_LIMIT):
    flops, bytes_accessed, transcendentals = cost
    return pl.pallas_call(
        kernel,
        name=name,
        out_shape=out_shape,
        in_specs=in_specs,
        out_specs=jax.tree.map(lambda _: whole(), out_shape) if out_specs is None else out_specs,
        scratch_shapes=scratch_shapes,
        cost_estimate=pl.CostEstimate(
            flops=flops, bytes_accessed=bytes_accessed, transcendentals=transcendentals
        ),
        compiler_params=pltpu.CompilerParams(vmem_limit_bytes=limit),
    )


def exchange(rows, groups=None):
    return lax.all_to_all(
        rows, "clus", split_axis=0, concat_axis=0, tiled=True, axis_index_groups=groups
    )


def mate(local, turn, half):
    if half & (half - 1) == 0:
        return local ^ turn
    return (turn + half - local) % half


def note_kernel(mass_hbm, table_hbm, out_ref, mass_ref, table_ref, sems):
    copies = [
        pltpu.make_async_copy(mass_hbm, mass_ref, sems.at[0]),
        pltpu.make_async_copy(table_hbm, table_ref, sems.at[1]),
    ]
    for copy in copies:
        copy.start()
    for copy in copies:
        copy.wait()
    targets, peers = mass_ref.shape[1], table_ref.shape[1]
    shape = (out_ref.shape[0], 1)
    out_ref[:, :, :targets] = jnp.broadcast_to(mass_ref[...][None], shape + (targets,))
    out_ref[:, :, targets:] = jnp.zeros(shape + (out_ref.shape[2] - targets,), F32)
    out_ref[:, :, targets : targets + peers] = jnp.broadcast_to(
        table_ref[...].astype(F32)[None], shape + (peers,)
    )


def make_note(mass, table):
    peers = table.shape[1]
    length = mass.shape[1] + -(-peers // LANES) * LANES
    return call(
        note_kernel,
        "make_note",
        jax.ShapeDtypeStruct((peers, 1, length), F32),
        [whole(pltpu.HBM)] * 2,
        scratch_shapes=[
            pltpu.VMEM(mass.shape, F32),
            pltpu.VMEM(table.shape, jnp.int32),
            pltpu.SemaphoreType.DMA((2,)),
        ],
        limit=None,
    )(mass, table)


def cut_kernel(x_ref, held_ref, ahead_ref):
    held_ref[...] = x_ref[...]
    ahead_ref[...] = x_ref[:, :, : ahead_ref.shape[2]]


def cut(blocks, ahead):
    return call(
        cut_kernel,
        "cut",
        (
            jax.ShapeDtypeStruct(blocks.shape, F32),
            jax.ShapeDtypeStruct(blocks.shape[:2] + (ahead,), F32),
        ),
        [whole()],
    )(blocks)


def pick_kernel(half, place_ref, notes_ref, own_ref, other_ref, far_ref, token_ref, *refs):
    near_refs, (asked_ref, near_held, far_held, near_sems, far_sems) = refs[:half], refs[half:]
    peers = far_ref.shape[0]
    count, _, width = own_ref.shape
    ahead = other_ref.shape[2]
    first = notes_ref.shape[2] - -(-peers // LANES) * LANES
    me = place_ref[0]
    side = me // half
    tables = notes_ref[:, 0, first:]
    lane = lax.broadcasted_iota(jnp.int32, tables.shape, 1)
    for turn, owner in enumerate((me, jnp.where(side == 0, me + half, me - half))):
        asked = jnp.sum(jnp.where(lane == owner, tables, 0.0), axis=1, keepdims=True)
        asked_ref[turn] = jnp.broadcast_to(asked, asked_ref.shape[1:])

    def select(emb_ref, wanted, columns):
        block = emb_ref[0, :, columns]
        for t in range(1, count):
            block = jnp.where(wanted == t, emb_ref[t, :, columns], block)
        return block

    def wanted_of(turn, d):
        return jnp.broadcast_to(asked_ref[turn, pl.ds(d, 1), :], (CB, LANES))

    def near_copy(turn):
        return pltpu.make_async_copy(near_held.at[turn], near_refs[turn], near_sems.at[turn])

    def far_copy(d):
        return pltpu.make_async_copy(far_held.at[d], far_ref.at[d], far_sems.at[d])

    def pick_far(d):
        wanted = wanted_of(0, d)
        for start in range(ahead, width, LANES):
            far_held[d, :, start - ahead : start - ahead + LANES] = select(
                own_ref, wanted, pl.ds(start, LANES)
            )
        far_copy(d).start()

    if peers <= 16:
        for d in range(peers):
            pick_far(d)
    else:
        pl.loop(0, peers)(pick_far)
    for turn in range(half):
        reader = side * half + mate(me - side * half, turn, half)
        for source, emb_ref in enumerate((own_ref, other_ref)):
            at = side if source == 0 else 1 - side
            wanted = wanted_of(source, reader)

            @pl.loop(0, ahead // LANES)
            def _(part):
                columns = pl.ds(pl.multiple_of(part * LANES, LANES), LANES)
                near_held[turn, at, :, columns] = select(emb_ref, wanted, columns)

        near_copy(turn).start()
    token_ref[...] = jnp.zeros_like(token_ref)

    @pl.loop(0, peers)
    def _(d):
        far_copy(d).wait()

    for turn in range(half):
        near_copy(turn).wait()


def pick_blocks(me, notes, own, other):
    peers = notes.shape[0]
    half = peers // 2
    ahead = other.shape[2]
    near = (2, CB, ahead)
    far = (peers, CB, own.shape[2] - ahead)
    far, token, *near = call(
        functools.partial(pick_kernel, half),
        "pick_blocks",
        [jax.ShapeDtypeStruct(shape, F32) for shape in [far, (8, LANES)] + [near] * half],
        [whole(pltpu.SMEM)] + [whole()] * 3,
        [whole(pl.ANY), whole()] + [whole(pl.ANY)] * half,
        scratch_shapes=[
            pltpu.VMEM((2, peers, LANES), F32),
            pltpu.VMEM((half,) + near, F32),
            pltpu.VMEM(far, F32),
            pltpu.SemaphoreType.DMA((half,)),
            pltpu.SemaphoreType.DMA((peers,)),
        ],
    )(me, notes, own, other)
    return far, token, near


def iota(shape, dimension):
    return lax.broadcasted_iota(jnp.int32, shape, dimension)


def slot_at(column, half, sides):
    block = column // CB
    return block % sides * half + block // sides


def product(a, b):
    return lax.dot_general(a, b, (((1,), (1,)), ((), ())), preferred_element_type=F32)


def prepare_kernel(
    sides,
    place_ref,
    notes_ref,
    table_ref,
    pools_ref,
    slots_ref,
    pool_mass_ref,
    _,
    listed_ref,
    same_ref,
    spare_ref,
    slot_mass_ref,
    mine_ref,
    own_ref,
    mass_ref,
):
    me, live = place_ref[0], place_ref[1]
    peers, columns = own_ref.shape[0], listed_ref.shape[1]
    half = peers // sides
    targets = own_ref.shape[1]
    pairs = pools_ref.shape[1]

    def hot(rows, values):
        return (rows == values).astype(F32).astype(BF16)

    column_slot = slot_at(iota((columns, 1), 0), half, sides)
    slot = slot_at(iota((1, columns), 1), half, sides)
    mine_ref[...] = (slot == me).astype(F32)
    listing = iota((1, pairs), 1) < live
    pool_hot = hot(iota((listed_ref.shape[0], pairs), 0), pools_ref[...])
    slot_hot = hot(column_slot, jnp.where(listing, slots_ref[...], -1))
    listed_ref[...] = product(pool_hot, slot_hot)

    spread = hot(column_slot, iota((columns, peers), 1))
    tables = notes_ref[:, 0, targets : targets + peers]
    table = table_ref[...].astype(F32)
    wide_tables = product(tables.astype(BF16), spread)
    wide_table = product(table.astype(BF16), spread)
    same_ref[...] = (wide_tables == wide_table).astype(F32)
    spare_ref[...] = (wide_table < 0).astype(F32)

    square = iota((peers, peers), 0), iota((peers, peers), 1)
    asked = jnp.sum(jnp.where(square[1] == me, tables, 0.0), axis=1, keepdims=True)
    block = (iota((peers, targets), 1) // CB).astype(F32)
    own_ref[...] = (asked == block).astype(F32)

    wanted = jnp.sum(jnp.where(square[0] == square[1], table, 0.0), axis=1, keepdims=True)
    masses = jnp.where(wanted == block, notes_ref[:, 0, :targets], 0.0)
    masses = fold(masses)
    slot_mass = [
        jnp.sum(
            jnp.where(
                iota((peers, LANES), 0) == slot_at(iota((peers, LANES), 1) + start, half, sides),
                masses,
                0.0,
            ),
            axis=0,
            keepdims=True,
        )
        for start in range(0, columns, LANES)
    ]
    slot_mass_ref[...] = jnp.concatenate(slot_mass, axis=1)

    diagonal = iota((LANES, LANES), 0) == iota((LANES, LANES), 1)
    for start in range(0, mass_ref.shape[0], LANES):
        row = pool_mass_ref[:, pl.ds(start, LANES)]
        mass_ref[pl.ds(start, LANES), :] = jnp.sum(
            jnp.where(diagonal, row, 0.0), axis=1, keepdims=True
        )


def prepare(place, notes, table, pools, slots, pool_mass, token, pool_count, targets, sides):
    peers = notes.shape[0]
    columns = peers * CB
    shapes = [
        (pool_count, columns),
        (peers, columns),
        (1, columns),
        (1, columns),
        (1, columns),
        (peers, targets),
        (pool_mass.shape[1], 1),
    ]
    return call(
        functools.partial(prepare_kernel, sides),
        "prepare",
        [jax.ShapeDtypeStruct(shape, F32) for shape in shapes],
        [whole(pltpu.SMEM)] + [whole()] * 6,
    )(place, notes, table, pools, slots, pool_mass, token)


def fold(rows):
    folded = rows[:, :LANES]
    for start in range(LANES, rows.shape[1], LANES):
        folded += rows[:, start : start + LANES]
    step = LANES // 2
    while step >= CB:
        folded += pltpu.roll(folded, step, 1)
        step //= 2
    return folded


def send_out(row, out_ref):
    out_ref[...] = jnp.broadcast_to(row[None], out_ref.shape)


def halves(x):
    high = x.astype(BF16)
    return high, (x - high.astype(F32)).astype(BF16)


def assemble_kernel(scale, place_ref, pool_ref, far_ref, listed_ref, mass_ref, *refs):
    near_refs, (kernel_ref, out_ref, near_high, near_low) = refs[:-4], refs[-4:]
    half = len(near_refs)
    me = place_ref[0]
    local = jnp.where(me < half, me, me - half)
    for turn, near_ref in enumerate(near_refs):
        for side in range(2):
            slot = side * half + mate(local, turn, half)
            at = pl.ds(pl.multiple_of(slot * CB, CB), CB)
            near_high[at, :], near_low[at, :] = halves(near_ref[side])
    ahead = near_high.shape[1]
    far_high, far_low = halves(far_ref[...].reshape(kernel_ref.shape[1], -1))
    sums = jnp.zeros((1, kernel_ref.shape[1]), F32)
    rows = kernel_ref.shape[0]

    def scores_of(p, q_high, q_low):
        high, low = halves(p)
        return product(high, q_high) + (product(high, q_low) + product(low, q_high))

    for start in range(0, kernel_ref.shape[0], rows):
        pool = pool_ref[pl.ds(start, rows), :]
        scores = scores_of(pool[:, :ahead], near_high[...], near_low[...])
        scores += scores_of(pool[:, ahead:], far_high, far_low)
        for block in range(rows // RB):
            inner = pl.ds(start + block * RB, RB)
            at = start // RB + block
            listed = listed_ref[at : at + 1, :] > 0
            values = jnp.where(
                listed, jnp.exp(scores[block * RB : (block + 1) * RB] * scale), 0.0
            )
            kernel_ref[inner, :] = values
            scaling = mass_ref[inner, :] / jnp.sum(values, axis=1, keepdims=True)
            sums += jnp.sum(values * scaling, axis=0, keepdims=True)
    send_out(sums, out_ref)


def assemble(place, pool, near, far, listed, mass):
    rows, width = pool.shape
    peers = far.shape[0]
    columns = peers * CB
    ahead = near[0].shape[2]
    return call(
        functools.partial(assemble_kernel, 1.5 / math.sqrt(width)),
        "assemble",
        (
            jax.ShapeDtypeStruct((rows, columns), F32),
            jax.ShapeDtypeStruct((peers, 1, columns), F32),
        ),
        [whole(pltpu.SMEM)] + [whole()] * (4 + len(near)),
        cost=(
            6 * rows * columns * width,
            4 * (rows * width + columns * width + rows * columns),
            rows * columns,
        ),
        scratch_shapes=[pltpu.VMEM((columns, ahead), BF16)] * 2,
    )(place, pool, far, listed, mass, *near)


def iterate_kernel(
    kernel_ref, notes_ref, same_ref, slot_mass_ref, spare_ref, mass_ref, out_ref, *scaling_refs
):
    col_sums = jnp.sum(notes_ref[:, 0, :] * same_ref[...], axis=0, keepdims=True)
    target_scaling = slot_mass_ref[...] / (col_sums + spare_ref[...])
    sums = jnp.zeros_like(target_scaling)
    diagonal = lax.broadcasted_iota(jnp.int32, (LANES, LANES), 0) == lax.broadcasted_iota(
        jnp.int32, (LANES, LANES), 1
    )
    for start in range(0, kernel_ref.shape[0], LANES):
        inner = pl.ds(start, LANES)
        values = kernel_ref[inner, :]
        scaling = mass_ref[inner, :] / jnp.sum(values * target_scaling, axis=1, keepdims=True)
        sums += jnp.sum(values * scaling, axis=0, keepdims=True)
        for scaling_ref in scaling_refs:
            scaling_ref[:, inner] = jnp.sum(
                jnp.where(diagonal, scaling, 0.0), axis=0, keepdims=True
            )
    send_out(sums, out_ref)


def iterate(kernel, notes, same, slot_mass, spare, mass, last):
    rows, columns = kernel.shape
    out_shape = [jax.ShapeDtypeStruct(notes.shape, F32)]
    if last:
        out_shape.append(jax.ShapeDtypeStruct((1, rows), F32))
    return call(
        iterate_kernel,
        "iterate",
        out_shape,
        [whole()] * 6,
        cost=(4 * rows * columns, 4 * rows * columns, 0),
    )(kernel, notes, same, slot_mass, spare, mass)


def finish_kernel(
    notes_ref,
    mine_ref,
    own_ref,
    mass_ref,
    scaling_ref,
    pool_hbm,
    target_hbm,
    pool_ref,
    target_ref,
    sems,
):
    pool_ref[...] = jnp.log(scaling_ref[0])
    pool_copy = pltpu.make_async_copy(pool_ref, pool_hbm, sems.at[0])
    pool_copy.start()
    col_sums = jnp.sum(fold(notes_ref[:, 0, :] * mine_ref[...]) * own_ref[...], axis=0)
    target_ref[...] = jnp.log(mass_ref[...] / col_sums)
    target_copy = pltpu.make_async_copy(target_ref, target_hbm, sems.at[1])
    target_copy.start()
    pool_copy.wait()
    target_copy.wait()


def finish(notes, mine, own, mass, scaling):
    shapes = (scaling.shape[1:], mass.shape)
    return call(
        finish_kernel,
        "finish",
        tuple(jax.ShapeDtypeStruct(shape, F32) for shape in shapes),
        [whole()] * 5,
        (whole(pl.ANY),) * 2,
        scratch_shapes=[pltpu.VMEM(shape, F32) for shape in shapes]
        + [pltpu.SemaphoreType.DMA((2,))],
    )(notes, mine, own, mass, scaling)


def local(
    pool_emb,
    target_emb,
    pool_mass,
    target_mass,
    fetch_table,
    pair_pool,
    listed_pair_slot,
    pair_count,
):
    peers = lax.axis_size("clus")
    me = lax.axis_index("clus").astype(jnp.int32)
    targets, width = target_emb.shape
    pool_count = pool_emb.shape[0] // RB
    columns = peers * CB
    half = peers // 2
    ahead = width // LANES // 3 * LANES

    def trade(x, turn):
        pairs = [
            (side * half + mate(i, turn, half), side * half + i)
            for side in range(2)
            for i in range(half)
        ]
        return lax.ppermute(x, "clus", [pair for pair in pairs if pair[0] != pair[1]])

    blocks = target_emb.reshape(targets // CB, CB, width)
    held, other = cut(blocks, ahead)
    other = lax.ppermute(other, "clus", [(i, (i + half) % peers) for i in range(peers)])
    note = make_note(target_mass[None], fetch_table)
    notes = lax.cond(me < peers, exchange, jnp.zeros_like, note)
    far, token, near = pick_blocks(me[None], notes, held, other)
    far = exchange(far)
    near = [near[0]] + [trade(x, turn) for turn, x in enumerate(near[1:], 1)]
    place = jnp.concatenate([me[None], pair_count])
    listed, same, spare, slot_mass, mine, own, mass = prepare(
        place,
        notes,
        fetch_table,
        pair_pool,
        listed_pair_slot,
        pool_mass[None],
        token,
        pool_count,
        targets,
        1,
    )

    kernel, sums = assemble(place, pool_emb, near, far, listed, mass)
    for step in range(1, ITERS):
        sums, *scalings = iterate(
            kernel, exchange(sums), same, slot_mass, spare, mass, step == ITERS - 1
        )
    return finish(exchange(sums), mine, own, target_mass, scalings[0])


def solution(mesh):
    return jax.shard_map(
        local,
        mesh=mesh,
        in_specs=(
            P(("groups", "clus"), None),
            P(("groups", "clus"), None),
            P(("groups", "clus")),
            P(("groups", "clus")),
            P(("groups", "clus"), None),
            P(("groups", "clus"), None),
            P(("groups", "clus"), None),
            P(("groups", "clus")),
        ),
        out_specs=(P(("groups", "clus")), P(("groups", "clus"))),
        check_vma=False,
    )
```
